32 devices in a mesh: stn: 16 (over z, y, x), tm: 2 (over core).
Axes of the slice: x: 2, y: 2, z: 4, core: 2. Of those that a mesh axis runs over, the one named last changes fastest.
Arguments:
- samples: bfloat16 [64, 8192], P('stn', 'tm'), may hold values from -200 to 200
- array_sizes: int32 [16], replicated, may hold values from 1 to 4, as said below
- partner: int32 [16], replicated, may hold values from 0 to 15, as said below
Outputs:
- correlation: float32 [256, 4096], P(('stn', 'tm'))
- residual: float32 [256, 4096], P(('stn', 'tm'))
The draws below stay inside these ranges and needn't reach their ends.
Inputs may be any that keep to these rules, and one draw needn't show every extreme that they name: partner[i] = i XOR r for one round number r, 1 <= r < 16, the same for every i. Block i's live stations are its first array_sizes[i] slots.
All inputs are finite; a program needn't handle non-finite values.
Results may differ from the reference program's by a relative error of at most 0.0003.
Values may be sent and summed in bfloat16 or wider, within the bound.
No kernel may reach another device: no remote copies, remote signals or barrier semaphores. Data moves between devices by JAX's collectives and lax.ppermute only.
A program may use at most 64 MiB of HBM per device.

```python
import math
import jax
import jax.numpy as jnp
from jax import lax

STN_DEV = 4
LAGS = 4096
SPECTRUM = 8192
BLOCKS = 16
STATIONS = 64
TIME = 8192
WINDOWS = 2
PAIRS = 256


def draw_samples(key, part):
    noise_key = jax.random.fold_in(key, 11)
    scale_key = jax.random.fold_in(key, 12)
    noise = jnp.clip(jax.random.normal(noise_key, (STATIONS, TIME), jnp.float32), -6.0, 6.0)
    growth = math.log(3.0)
    station_scale = jnp.exp(jax.random.uniform(scale_key, (STATIONS, 1), jnp.float32, 0.0, math.log(10.0)))
    envelope = jnp.exp(growth * jnp.arange(TIME, dtype=jnp.float32) / TIME)[None, :]
    return (noise * station_scale * envelope).astype(jnp.bfloat16)


def draw_array_sizes(key, part):
    counts = jax.random.randint(jax.random.fold_in(key, 21), (BLOCKS,), 1, STN_DEV + 1)
    order = jax.random.permutation(jax.random.fold_in(key, 22), BLOCKS)
    counts = counts.at[order[0]].set(STN_DEV)
    counts = counts.at[order[1]].set(1)
    return counts.astype(jnp.int32)


def draw_partner(key, part):
    round_number = jax.random.randint(jax.random.fold_in(key, 31), (), 1, BLOCKS)
    return jnp.bitwise_xor(jnp.arange(BLOCKS, dtype=jnp.int32), round_number).astype(jnp.int32)


def setup_inputs(seed: int = 0) -> dict:
    splits = jax.random.split(jax.random.key(seed), 4)
    return {
        "samples": draw_samples(jax.random.fold_in(splits[3], 71), 0),
        "array_sizes": draw_array_sizes(jax.random.fold_in(splits[3], 71), 0),
        "partner": draw_partner(jax.random.fold_in(splits[3], 71), 0),
    }


small_term = 1e-06

def block_spectra(station_rows):
    count = station_rows.shape[0]
    padded = jnp.concatenate([station_rows, jnp.zeros((count, LAGS), station_rows.dtype)], axis=1)
    pieces = padded.reshape(count, WINDOWS + 1, LAGS)
    windows = jnp.concatenate([pieces[:, :-1], pieces[:, 1:]], axis=2)
    spectra = jnp.fft.fft(windows, axis=-1)
    power = lax.optimization_barrier(jnp.sum(jnp.real(spectra) ** 2 + jnp.imag(spectra) ** 2, axis=1))
    smooth = power
    for shift_by in (-2, -1, 1, 2):
        smooth = smooth + jnp.roll(power, shift_by, axis=1)
    level = smooth / 5.0 / WINDOWS + small_term
    whitened = spectra / jnp.sqrt(level)[:, None, :]
    return (whitened, power / level)

def one_block(block_id, samples, array_sizes, partner):
    other_id = partner[block_id]
    own_rows = lax.dynamic_slice(samples, ((block_id * STN_DEV).astype(jnp.int32), jnp.int32(0)), (STN_DEV, TIME)).astype(jnp.float32)
    far_rows = lax.dynamic_slice(samples, ((other_id * STN_DEV).astype(jnp.int32), jnp.int32(0)), (STN_DEV, TIME)).astype(jnp.float32)
    own_white, own_auto = block_spectra(own_rows)
    far_white, unused_auto = block_spectra(far_rows)
    cross = jnp.einsum('ajf,bjf->abf', jnp.conj(own_white), far_white, precision=lax.Precision.HIGHEST)
    ratio = own_auto / (lax.optimization_barrier(jnp.mean(own_auto, axis=1, keepdims=True)) + small_term)
    refined = cross * (1.0 - ratio)[:, None, :]
    factor = SPECTRUM / jnp.sqrt(jnp.float32(SPECTRUM * WINDOWS))
    plain_lags = jnp.real(jnp.fft.ifft(cross, axis=-1))[..., :LAGS] * factor
    refined_lags = jnp.real(jnp.fft.ifft(refined, axis=-1))[..., :LAGS] * factor
    slots = jnp.arange(STN_DEV, dtype=jnp.int32)
    live = ((slots[:, None] < array_sizes[block_id]) & (slots[None, :] < array_sizes[other_id])).astype(plain_lags.dtype)
    return (plain_lags * live[:, :, None], refined_lags * live[:, :, None])

def reference(samples, array_sizes, partner):

    def step_block(block_id):
        return one_block(block_id, samples, array_sizes, partner)
    plain_all, refined_all = lax.map(step_block, jnp.arange(BLOCKS, dtype=jnp.int32))
    return (plain_all.reshape(PAIRS, LAGS), refined_all.reshape(PAIRS, LAGS))
```

```python
import functools
import math

import jax
import jax.numpy as jnp
import numpy as np
from jax import lax
from jax.experimental import pallas as pl
from jax.experimental.pallas import tpu as pltpu
from jax.sharding import PartitionSpec as P

LAGS = 4096
PERIOD = 2 * LAGS
ROWS = 64
COLS = 128
HALF = ROWS // 2 + 1
RIM = 2
WIDE = HALF + 2 * RIM
SLOTS = 8
SMALL = 1e-06
F32 = jnp.float32
BF16 = jnp.bfloat16


def split_table(table):
    high = table.astype(np.float32).astype(jnp.bfloat16)
    low = (table - high.astype(np.float64)).astype(np.float32).astype(jnp.bfloat16)
    return np.stack([high, low])


@functools.lru_cache(maxsize=None)
def tables(count, windows):
    f1 = np.arange(-RIM, HALF + RIM)
    n1 = np.arange(ROWS)
    angle = 2 * np.pi * ((f1[:, None] * n1[None, :]) % ROWS) / ROWS
    first = np.stack([np.cos(angle), -np.sin(angle)])
    first = np.repeat(np.repeat(first, SLOTS, axis=1), count, axis=2)
    first = first.reshape(2 * WIDE * SLOTS, ROWS * count)
    n2 = np.arange(COLS)
    angle = 2 * np.pi * ((f1[:, None] * n2[None, :]) % PERIOD) / PERIOD
    twist = np.stack([np.cos(angle), np.sin(angle)]).astype(np.float32)
    angle = 2 * np.pi * ((n2[:, None] * n2[None, :]) % COLS) / COLS
    cos, sin = np.cos(angle), np.sin(angle)
    second = np.block([[cos, -sin], [sin, cos]])
    lag = np.arange(LAGS // COLS)
    kept = np.arange(HALF)
    angle = 2 * np.pi * ((lag[:, None] * kept[None, :]) % ROWS) / ROWS
    weight = np.where((kept == 0) | (kept == HALF - 1), 1.0, 2.0) / math.sqrt(PERIOD * windows)
    last = np.concatenate([np.cos(angle) * weight, (np.sin(angle) * weight)[:, 1:-1]], axis=1)
    last = np.kron(last, np.eye(SLOTS))
    return split_table(first), twist, split_table(second), split_table(last)


def dot(left, right):
    return jnp.dot(left, right, preferred_element_type=F32)


def split(value):
    high = value.astype(BF16)
    return high, (value - high.astype(F32)).astype(BF16)


def dot_split(left, right):
    return dot(left[0], right[0]) + (dot(left[1], right[0]) + dot(left[0], right[1]))


def twisted(re, im, twist_ref, start):
    rows = re.shape[0] // SLOTS
    re = re.reshape(rows, SLOTS, COLS)
    im = im.reshape(rows, SLOTS, COLS)
    cos = twist_ref[0, start : start + rows, :][:, None, :]
    sin = twist_ref[1, start : start + rows, :][:, None, :]
    out = jnp.concatenate([re * cos + im * sin, im * cos - re * sin], axis=2)
    return out.reshape(rows * SLOTS, 2 * COLS)


def whitened_rows(rows_ref, mine, picked, first_ref, twist_ref, second_ref):
    windows = rows_ref.shape[0]
    blocks = [rows_ref[jnp.bitwise_xor(mine, j)] for j in range(windows)]
    blocks.append(jnp.zeros_like(blocks[0]))
    stacked = jnp.concatenate(
        [jnp.concatenate(blocks[:-1], axis=1), jnp.concatenate(blocks[1:], axis=1)], axis=0
    )
    size = WIDE * SLOTS
    shape = (2 * size // picked.shape[0],) + picked.shape
    grid = 0.0
    for part in range(2):
        chosen = jnp.where(picked[None], first_ref[part].reshape(shape), jnp.zeros((), BF16))
        grid = grid + dot(chosen.reshape(2 * size, picked.shape[1]), stacked)
    second = (second_ref[0], second_ref[1])
    spectra = []
    power = 0.0
    for j in range(windows):
        here = grid[:, j * COLS : (j + 1) * COLS]
        spec = dot_split(split(twisted(here[:size], here[size:], twist_ref, 0)), second)
        re, im = spec[:, :COLS], spec[:, COLS:]
        power = power + (re * re + im * im)
        spectra.append((re, im))
    inner = HALF * SLOTS
    smooth = 0.0
    for shift in range(2 * RIM + 1):
        smooth = smooth + power[shift * SLOTS : shift * SLOTS + inner]
    level = smooth * (1.0 / (5 * windows)) + SMALL
    root = lax.rsqrt(level)
    kept = slice(RIM * SLOTS, RIM * SLOTS + inner)
    white = [(re[kept] * root, im[kept] * root) for re, im in spectra]
    return white, power[kept], root


def kernel(place_ref, near_ref, far_ref, first_ref, twist_ref, second_ref, last_ref, plain_ref, refined_ref):
    windows, count = near_ref.shape[0], near_ref.shape[1] * COLS // LAGS
    share = plain_ref.shape[0]
    mine, live_near, live_far = place_ref[0], place_ref[1], place_ref[2]
    first_pair = mine * share
    shape = (2 * SLOTS, ROWS * count)
    pair = first_pair + lax.broadcasted_iota(jnp.int32, shape, 0) % SLOTS
    station = lax.broadcasted_iota(jnp.int32, shape, 1) % count
    near, power, root = whitened_rows(
        near_ref, mine, station == pair // count, first_ref, twist_ref, second_ref
    )
    far, _, _ = whitened_rows(far_ref, mine, station == pair % count, first_ref, twist_ref, second_ref)
    auto = power * (root * root)
    inner = HALF * SLOTS
    by_row = auto.reshape(HALF, SLOTS, COLS)
    total = 2.0 * jnp.sum(by_row, axis=0) - by_row[0] - by_row[HALF - 1]
    mean = jnp.sum(total, axis=1, keepdims=True) * (1.0 / PERIOD)
    keep = (1.0 - by_row / (mean + SMALL)[None]).reshape(inner, COLS)
    re = im = 0.0
    for (near_re, near_im), (far_re, far_im) in zip(near, far):
        re = re + (near_re * far_re + near_im * far_im)
        im = im + (near_im * far_re - near_re * far_im)
    second = (second_ref[0], second_ref[1])
    halves = []
    for value_re, value_im in ((re, im), (re * keep, im * keep)):
        half = dot_split(split(jnp.concatenate([value_re, value_im], axis=1)), second)
        half = twisted(half[:, :COLS], half[:, COLS:], twist_ref, RIM)
        halves.append(
            jnp.concatenate([half[:, :COLS], half[SLOTS : inner - SLOTS, COLS:]], axis=0)
        )
    lags = dot_split((last_ref[0], last_ref[1]), split(jnp.concatenate(halves, axis=1)))
    pair = first_pair + lax.broadcasted_iota(jnp.int32, (SLOTS, COLS), 0)
    live = ((pair // count < live_near) & (pair % count < live_far)).astype(F32)
    for j in range(LAGS // COLS):
        here = lags[j * SLOTS : (j + 1) * SLOTS]
        plain_ref[:, j * COLS : (j + 1) * COLS] = (here[:, :COLS] * live)[:share]
        refined_ref[:, j * COLS : (j + 1) * COLS] = (here[:, COLS:] * live)[:share]


def per_device(samples, array_sizes, partner):
    count = samples.shape[0]
    groups = lax.axis_size("tm")
    blocks = lax.axis_size("stn")
    share = count * count // groups
    mine = lax.axis_index("tm")
    block = lax.axis_index("stn")
    round_number = partner[0]
    rows = samples.reshape(count, LAGS // COLS, COLS).transpose(1, 0, 2).reshape(-1, COLS)
    near = jnp.stack(
        [rows]
        + [lax.ppermute(rows, "tm", [(i, i ^ s) for i in range(groups)]) for s in range(1, groups)]
    )

    def sent(number, held):
        return lax.ppermute(held, "stn", [(i, i ^ number) for i in range(blocks)])

    far = lax.switch(
        round_number - 1, [functools.partial(sent, number) for number in range(1, blocks)], near
    )
    place = jnp.stack(
        [mine, array_sizes[block], array_sizes[jnp.bitwise_xor(block, round_number)]]
    )
    vmem = pl.BlockSpec(memory_space=pltpu.VMEM)
    out = jax.ShapeDtypeStruct((share, LAGS), F32)
    return pl.pallas_call(
        kernel,
        out_shape=(out, out),
        in_specs=[pl.BlockSpec(memory_space=pltpu.SMEM)] + [vmem] * 6,
        out_specs=(vmem, vmem),
        compiler_params=pltpu.CompilerParams(vmem_limit_bytes=40 * 1024 * 1024),
    )(place, near, far, *tables(count, groups))


def solution(mesh):
    placed = (P("stn", "tm"), P(), P())
    return jax.shard_map(
        per_device,
        mesh=mesh,
        in_specs=placed,
        out_specs=(P(("stn", "tm"), None), P(("stn", "tm"), None)),
        check_vma=False,
    )
```

```python
import functools
import math

import jax
import jax.numpy as jnp
import numpy as np
from jax import lax
from jax.experimental import pallas as pl
from jax.experimental.pallas import tpu as pltpu
from jax.sharding import PartitionSpec as P

LAGS = 4096
PERIOD = 2 * LAGS
ROWS = 64
COLS = 128
HALF = ROWS // 2 + 1
RIM = 2
WIDE = HALF + 2 * RIM
SLOTS = 8
SMALL = 1e-06
F32 = jnp.float32
BF16 = jnp.bfloat16


def split_table(table):
    high = table.astype(np.float32).astype(jnp.bfloat16)
    low = (table - high.astype(np.float64)).astype(np.float32).astype(jnp.bfloat16)
    return np.stack([high, low])


@functools.lru_cache(maxsize=None)
def tables(count, windows):
    f1 = np.arange(-RIM, HALF + RIM)
    n1 = np.arange(ROWS)
    angle = 2 * np.pi * ((f1[:, None] * n1[None, :]) % ROWS) / ROWS
    first = np.stack([np.cos(angle), -np.sin(angle)])
    first = np.repeat(np.repeat(first, SLOTS, axis=1), count, axis=2)
    first = first.reshape(2 * WIDE * SLOTS, ROWS * count)
    n2 = np.arange(COLS)
    angle = 2 * np.pi * ((f1[:, None] * n2[None, :]) % PERIOD) / PERIOD
    twist = np.stack([np.cos(angle), np.sin(angle)]).astype(np.float32)
    angle = 2 * np.pi * ((n2[:, None] * n2[None, :]) % COLS) / COLS
    cos, sin = np.cos(angle), np.sin(angle)
    second = np.block([[cos, -sin], [sin, cos]])
    lag = np.arange(LAGS // COLS)
    kept = np.arange(HALF)
    angle = 2 * np.pi * ((lag[:, None] * kept[None, :]) % ROWS) / ROWS
    weight = np.where((kept == 0) | (kept == HALF - 1), 1.0, 2.0) / math.sqrt(PERIOD * windows)
    last = np.concatenate([np.cos(angle) * weight, (np.sin(angle) * weight)[:, 1:-1]], axis=1)
    last = np.kron(last, np.eye(SLOTS))
    return split_table(first), twist, split_table(second), split_table(last)


def dot(left, right):
    return jnp.dot(left, right, preferred_element_type=F32)


def split(value):
    high = value.astype(BF16)
    return high, (value - high.astype(F32)).astype(BF16)


def dot_split(left, right):
    return dot(left[0], right[0]) + (dot(left[1], right[0]) + dot(left[0], right[1]))


def twisted(re, im, twist_ref, start):
    rows = re.shape[0] // SLOTS
    re = re.reshape(rows, SLOTS, COLS)
    im = im.reshape(rows, SLOTS, COLS)
    cos = twist_ref[0, start : start + rows, :][:, None, :]
    sin = twist_ref[1, start : start + rows, :][:, None, :]
    out = jnp.concatenate([re * cos + im * sin, im * cos - re * sin], axis=2)
    return out.reshape(rows * SLOTS, 2 * COLS)


def whitened_rows(blocks, picked, first_ref, twist_ref, second_ref):
    windows = len(blocks)
    blocks = blocks + [jnp.zeros_like(blocks[0])]
    stacked = jnp.concatenate(
        [jnp.concatenate(blocks[:-1], axis=1), jnp.concatenate(blocks[1:], axis=1)], axis=0
    )
    size = WIDE * SLOTS
    shape = (2 * size // picked.shape[0],) + picked.shape
    grid = 0.0
    for part in range(2):
        chosen = jnp.where(picked[None], first_ref[part].reshape(shape), jnp.zeros((), BF16))
        grid = grid + dot(chosen.reshape(2 * size, picked.shape[1]), stacked)
    second = (second_ref[0], second_ref[1])
    spectra = []
    power = 0.0
    for j in range(windows):
        here = grid[:, j * COLS : (j + 1) * COLS]
        spec = dot_split(split(twisted(here[:size], here[size:], twist_ref, 0)), second)
        re, im = spec[:, :COLS], spec[:, COLS:]
        power = power + (re * re + im * im)
        spectra.append((re, im))
    inner = HALF * SLOTS
    smooth = 0.0
    for shift in range(2 * RIM + 1):
        smooth = smooth + power[shift * SLOTS : shift * SLOTS + inner]
    level = smooth * (1.0 / (5 * windows)) + SMALL
    root = lax.rsqrt(level)
    kept = slice(RIM * SLOTS, RIM * SLOTS + inner)
    white = [(re[kept] * root, im[kept] * root) for re, im in spectra]
    return white, power[kept], root


def kernel(sizes_ref, partner_ref, rows_ref, first_ref, twist_ref, second_ref, last_ref, plain_ref, refined_ref):
    windows = rows_ref.shape[0] // 2
    count = rows_ref.shape[1] * COLS // LAGS
    share = plain_ref.shape[0]
    mine, block = lax.axis_index("tm"), lax.axis_index("stn")
    other = jnp.bitwise_xor(block, partner_ref[0])
    live_near, live_far = sizes_ref[block], sizes_ref[other]
    near_start = jnp.where(block < other, 0, windows)
    far_start = windows - near_start
    near_blocks = [rows_ref[near_start + j] for j in range(windows)]
    far_blocks = [rows_ref[far_start + j] for j in range(windows)]
    first_pair = mine * share
    shape = (2 * SLOTS, ROWS * count)
    pair = first_pair + lax.broadcasted_iota(jnp.int32, shape, 0) % SLOTS
    station = lax.broadcasted_iota(jnp.int32, shape, 1) % count
    near, power, root = whitened_rows(
        near_blocks, station == pair // count, first_ref, twist_ref, second_ref
    )
    far, _, _ = whitened_rows(far_blocks, station == pair % count, first_ref, twist_ref, second_ref)
    auto = power * (root * root)
    inner = HALF * SLOTS
    by_row = auto.reshape(HALF, SLOTS, COLS)
    total = 2.0 * jnp.sum(by_row, axis=0) - by_row[0] - by_row[HALF - 1]
    mean = jnp.sum(total, axis=1, keepdims=True) * (1.0 / PERIOD)
    keep = (1.0 - by_row / (mean + SMALL)[None]).reshape(inner, COLS)
    re = im = 0.0
    for (near_re, near_im), (far_re, far_im) in zip(near, far):
        re = re + (near_re * far_re + near_im * far_im)
        im = im + (near_im * far_re - near_re * far_im)
    second = (second_ref[0], second_ref[1])
    halves = []
    for value_re, value_im in ((re, im), (re * keep, im * keep)):
        half = dot_split(split(jnp.concatenate([value_re, value_im], axis=1)), second)
        half = twisted(half[:, :COLS], half[:, COLS:], twist_ref, RIM)
        halves.append(
            jnp.concatenate([half[:, :COLS], half[SLOTS : inner - SLOTS, COLS:]], axis=0)
        )
    lags = dot_split((last_ref[0], last_ref[1]), split(jnp.concatenate(halves, axis=1)))
    pair = first_pair + lax.broadcasted_iota(jnp.int32, (SLOTS, COLS), 0)
    live = ((pair // count < live_near) & (pair % count < live_far)).astype(F32)
    for j in range(LAGS // COLS):
        here = lags[j * SLOTS : (j + 1) * SLOTS]
        plain_ref[:, j * COLS : (j + 1) * COLS] = (here[:, :COLS] * live)[:share]
        refined_ref[:, j * COLS : (j + 1) * COLS] = (here[:, COLS:] * live)[:share]


def per_device(samples, array_sizes, partner):
    count = samples.shape[0]
    groups = lax.axis_size("tm")
    blocks = lax.axis_size("stn")
    share = count * count // groups
    rows = samples.reshape(count, LAGS // COLS, COLS).transpose(1, 0, 2).reshape(-1, COLS)

    def gathered(number, held):
        pairs = [(low, low ^ number) for low in range(blocks) if low < low ^ number]
        return lax.all_gather(
            held,
            ("stn", "tm"),
            axis_index_groups=[
                [block * groups + t for block in pair for t in range(groups)] for pair in pairs
            ],
        )

    both = lax.switch(
        partner[0] - 1, [functools.partial(gathered, number) for number in range(1, blocks)], rows
    )
    vmem = pl.BlockSpec(memory_space=pltpu.VMEM)
    smem = pl.BlockSpec(memory_space=pltpu.SMEM)
    out = jax.ShapeDtypeStruct((share, LAGS), F32)
    return pl.pallas_call(
        kernel,
        out_shape=(out, out),
        in_specs=[smem] * 2 + [vmem] * 5,
        out_specs=(vmem, vmem),
        compiler_params=pltpu.CompilerParams(vmem_limit_bytes=40 * 1024 * 1024),
    )(array_sizes, partner, both, *tables(count, groups))


def solution(mesh):
    placed = (P("stn", "tm"), P(), P())
    return jax.shard_map(
        per_device,
        mesh=mesh,
        in_specs=placed,
        out_specs=(P(("stn", "tm"), None), P(("stn", "tm"), None)),
        check_vma=False,
    )
```

```python
import functools
import math

import jax
import jax.numpy as jnp
import numpy as np
from jax import lax
from jax.experimental import pallas as pl
from jax.experimental.pallas import tpu as pltpu
from jax.sharding import PartitionSpec as P

LAGS = 4096
PERIOD = 2 * LAGS
ROWS = 64
COLS = 128
HALF = ROWS // 2 + 1
RIM = 2
WIDE = HALF + 2 * RIM
SLOTS = 8
SMALL = 1e-06
F32 = jnp.float32
BF16 = jnp.bfloat16


def split_table(table):
    high = table.astype(np.float32).astype(jnp.bfloat16)
    low = (table - high.astype(np.float64)).astype(np.float32).astype(jnp.bfloat16)
    return np.stack([high, low])


@functools.lru_cache(maxsize=None)
def tables(count, windows):
    f1 = np.arange(-RIM, HALF + RIM)
    n1 = np.arange(LAGS // COLS)
    angle = 2 * np.pi * ((f1[:, None] * n1[None, :]) % ROWS) / ROWS
    first = np.stack([np.cos(angle), -np.sin(angle)])
    same_block = np.eye(2)[None, None, :, None, :, None, None]
    same_slot = np.eye(count)[None, None, None, :, None, None, :]
    first = first[:, :, None, None, None, :, None] * same_block * same_slot
    first = first.reshape(2 * WIDE * 2 * count, 2 * n1.size * count)
    n2 = np.arange(COLS)
    angle = 2 * np.pi * ((f1[:, None] * n2[None, :]) % PERIOD) / PERIOD
    sign = np.broadcast_to(1.0 - 2.0 * (f1[:, None] % 2), angle.shape)
    twist = np.stack([np.cos(angle), np.sin(angle), sign]).astype(np.float32)
    angle = 2 * np.pi * ((n2[:, None] * n2[None, :]) % COLS) / COLS
    cos, sin = np.cos(angle), np.sin(angle)
    second = np.block([[cos, -sin], [sin, cos]])
    lag = np.arange(LAGS // COLS)
    kept = np.arange(HALF)
    angle = 2 * np.pi * ((lag[:, None] * kept[None, :]) % ROWS) / ROWS
    weight = np.where((kept == 0) | (kept == HALF - 1), 1.0, 2.0) / math.sqrt(PERIOD * windows)
    last = np.concatenate([np.cos(angle) * weight, (np.sin(angle) * weight)[:, 1:-1]], axis=1)
    last = np.kron(last, np.eye(SLOTS))
    return split_table(first), twist, split_table(second), split_table(last)


def dot(left, right):
    return jnp.dot(left, right, preferred_element_type=F32)


def split(value):
    high = value.astype(BF16)
    return high, (value - high.astype(F32)).astype(BF16)


def dot_split(left, right):
    return dot(left[0], right[0]) + (dot(left[1], right[0]) + dot(left[0], right[1]))


def twisted(re, im, twist_ref, start):
    rows = re.shape[0] // SLOTS
    re = re.reshape(rows, SLOTS, COLS)
    im = im.reshape(rows, SLOTS, COLS)
    cos = twist_ref[0, start : start + rows, :][:, None, :]
    sin = twist_ref[1, start : start + rows, :][:, None, :]
    out = jnp.concatenate([re * cos + im * sin, im * cos - re * sin], axis=2)
    return out.reshape(rows * SLOTS, 2 * COLS)


def placed(value, index):
    rows = value.shape[0] // SLOTS
    value = value.reshape(rows, SLOTS, COLS)
    index = jnp.broadcast_to(index[None], value.shape)
    return jnp.take_along_axis(value, index, axis=1).reshape(rows * SLOTS, COLS)


def kernel(
    sizes_ref, partner_ref, rows_ref, first_ref, twist_ref, second_ref, last_ref,
    plain_ref, refined_ref,
):
    windows = rows_ref.shape[0] // 2
    count = SLOTS // 2
    share = plain_ref.shape[0]
    mine, block = lax.axis_index("tm"), lax.axis_index("stn")
    other = jnp.bitwise_xor(block, partner_ref[:, 0:1])
    pair = mine * share + lax.broadcasted_iota(jnp.int32, (SLOTS, COLS), 0)
    near_slot = jnp.minimum(pair // count, count - 1)
    far_slot = pair % count
    near_index = near_slot + jnp.where(block < other, 0, count)
    far_index = far_slot + jnp.where(block < other, count, 0)

    size = WIDE * SLOTS
    inner = HALF * SLOTS
    stacked = jnp.concatenate(
        [
            jnp.concatenate([rows_ref[j], rows_ref[windows + j]], axis=0)
            for j in range(windows)
        ],
        axis=1,
    )
    grid = dot(first_ref[0], stacked) + dot(first_ref[1], stacked)
    second = (second_ref[0], second_ref[1])
    sign = twist_ref[2][:, None, :]
    spectra = []
    power = 0.0
    for j in reversed(range(windows)):
        here = grid[:, j * COLS : (j + 1) * COLS]
        here = twisted(here[:size], here[size:], twist_ref, 0)
        value = here
        if spectra:
            turned = later.reshape(WIDE, SLOTS, 2 * COLS) * jnp.concatenate([sign, sign], axis=2)
            value = here + turned.reshape(size, 2 * COLS)
        later = here
        spec = dot_split(split(value), second)
        re, im = spec[:, :COLS], spec[:, COLS:]
        power = power + (re * re + im * im)
        spectra.append((re, im))
    smooth = 0.0
    for shift in range(2 * RIM + 1):
        smooth = smooth + power[shift * SLOTS : shift * SLOTS + inner]
    level = smooth * (1.0 / (5 * windows)) + SMALL
    root = lax.rsqrt(level)
    kept = slice(RIM * SLOTS, RIM * SLOTS + inner)
    by_row = (power[kept] * (root * root)).reshape(HALF, SLOTS, COLS)
    total = 2.0 * jnp.sum(by_row, axis=0) - by_row[0] - by_row[HALF - 1]
    mean = jnp.sum(total, axis=1, keepdims=True) * (1.0 / PERIOD)
    keep = (1.0 - by_row / (mean + SMALL)[None]).reshape(inner, COLS)
    keep = placed(keep, near_index)
    re = im = 0.0
    for spec_re, spec_im in spectra:
        spec_re, spec_im = spec_re[kept] * root, spec_im[kept] * root
        near_re, near_im = placed(spec_re, near_index), placed(spec_im, near_index)
        far_re, far_im = placed(spec_re, far_index), placed(spec_im, far_index)
        re = re + (near_re * far_re + near_im * far_im)
        im = im + (near_im * far_re - near_re * far_im)
    halves = []
    for value_re, value_im in ((re, im), (re * keep, im * keep)):
        half = dot_split(split(jnp.concatenate([value_re, value_im], axis=1)), second)
        half = twisted(half[:, :COLS], half[:, COLS:], twist_ref, RIM)
        halves.append(
            jnp.concatenate([half[:, :COLS], half[SLOTS : inner - SLOTS, COLS:]], axis=0)
        )
    lags = dot_split((last_ref[0], last_ref[1]), split(jnp.concatenate(halves, axis=1)))

    places = lax.broadcasted_iota(jnp.int32, sizes_ref.shape, 1)
    held = sizes_ref[...]
    live_near = jnp.sum(jnp.where(places == block, held, 0), axis=1, keepdims=True)
    live_far = jnp.sum(jnp.where(places == other, held, 0), axis=1, keepdims=True)
    live = ((near_slot < live_near) & (far_slot < live_far)).astype(F32)
    for j in range(LAGS // COLS):
        here = lags[j * SLOTS : (j + 1) * SLOTS]
        plain_ref[:, j * COLS : (j + 1) * COLS] = (here[:, :COLS] * live)[:share]
        refined_ref[:, j * COLS : (j + 1) * COLS] = (here[:, COLS:] * live)[:share]


def per_device(samples, array_sizes, partner):
    count = samples.shape[0]
    groups = lax.axis_size("tm")
    blocks = lax.axis_size("stn")
    share = count * count // groups
    rows = samples.reshape(count, LAGS // COLS, COLS).transpose(1, 0, 2).reshape(-1, COLS)

    def gathered(number, held):
        pairs = [(low, low ^ number) for low in range(blocks) if low < low ^ number]
        return lax.all_gather(
            held,
            ("stn", "tm"),
            axis_index_groups=[
                [block * groups + t for block in pair for t in range(groups)] for pair in pairs
            ],
        )

    number = jnp.minimum(partner[0], jnp.maximum(partner[0], array_sizes[0]))
    both = lax.switch(
        number - 1, [functools.partial(gathered, number) for number in range(1, blocks)], rows
    )
    vmem = pl.BlockSpec(memory_space=pltpu.VMEM)
    out = jax.ShapeDtypeStruct((share, LAGS), F32)
    return pl.pallas_call(
        kernel,
        out_shape=(out, out),
        in_specs=[vmem] * 7,
        out_specs=(vmem, vmem),
        compiler_params=pltpu.CompilerParams(vmem_limit_bytes=40 * 1024 * 1024),
    )(array_sizes[None], partner[None], both, *tables(count, groups))


def solution(mesh):
    placed = (P("stn", "tm"), P(), P())
    return jax.shard_map(
        per_device,
        mesh=mesh,
        in_specs=placed,
        out_specs=(P(("stn", "tm"), None), P(("stn", "tm"), None)),
        check_vma=False,
    )
```

```python
import functools
import math

import jax
import jax.numpy as jnp
import numpy as np
from jax import lax
from jax.experimental import pallas as pl
from jax.experimental.pallas import tpu as pltpu
from jax.sharding import PartitionSpec as P

LAGS = 4096
PERIOD = 2 * LAGS
ROWS = 64
COLS = 128
EVEN = ROWS // 4 + 1
ODD = ROWS // 4
HALF = EVEN + ODD
FOLD = COLS // 2
SLOTS = 8
SMALL = 1e-06
F32 = jnp.float32
BF16 = jnp.bfloat16


def split_table(table):
    high = table.astype(np.float32).astype(jnp.bfloat16)
    low = (table - high.astype(np.float64)).astype(np.float32).astype(jnp.bfloat16)
    return np.stack([high, low])


@functools.lru_cache(maxsize=None)
def tables(count, windows):
    f1 = np.concatenate([np.arange(0, ROWS // 2 + 1, 2), np.arange(1, ROWS // 2, 2)])
    lag = np.arange(LAGS // COLS)
    angle = 2 * np.pi * ((f1[:, None] * lag[None, :]) % ROWS) / ROWS
    half = ODD // 2
    base = np.concatenate([np.arange(half + 1), np.arange(EVEN, EVEN + half)])
    first = []
    for parity in range(2):
        kept = angle[base, parity::2]
        part = np.concatenate([np.cos(kept), -np.sin(kept[1:])])
        part = part[:, None, :, None] * np.eye(SLOTS)[None, :, None, :]
        first.append(np.concatenate(list(split_table(part.reshape(-1, COLS))), axis=1))
    first = np.stack(first)
    n2 = np.arange(COLS)
    twist = 2 * np.pi * ((f1[:, None] * n2[None, :]) % PERIOD) / PERIOD
    twist = np.stack([np.cos(twist), np.sin(twist)]).astype(np.float32)
    folded = np.where(n2 > FOLD, n2 - FOLD, n2)
    turn = 2 * np.pi * ((n2[:, None] * folded[None, :]) % COLS) / COLS
    turn = np.where(n2 > FOLD, np.sin(turn), np.cos(turn))
    second = []
    for table in (turn, turn.T):
        high, low = split_table(table)
        second.append(np.block([[high, low], [high, np.zeros_like(low)]]))
    second = np.stack(second)
    weight = np.where(f1 % (ROWS // 2) == 0, 1.0, 2.0)[:, None] / math.sqrt(PERIOD * windows)
    cos, sin = (np.cos(angle) * weight)[:, :EVEN].T, (np.sin(angle) * weight)[:, :EVEN].T
    same = np.concatenate([cos[:, : EVEN - 1], sin[:, EVEN:]], axis=1)
    turned = np.concatenate([cos[:, EVEN:], sin[:, : EVEN - 1]], axis=1)
    last = np.stack([np.kron(same, np.eye(SLOTS)), np.kron(turned, np.eye(SLOTS))])
    return first, twist, second, split_table(last)


def dot(left, right):
    return jnp.dot(left, right, preferred_element_type=F32)


def split(value):
    high = value.astype(BF16)
    return high, (value - high.astype(F32)).astype(BF16)


def dot_split(left, right):
    rows = left[0].shape[0]
    both = dot(jnp.concatenate(left, axis=0), right[0])
    return both[:rows] + (both[rows:] + dot(left[0], right[1]))


def dot_packed(value, table):
    out = dot(jnp.concatenate(split(value), axis=1), table)
    return out[:, :COLS] + out[:, COLS:]


def lanes(rows):
    lane = lax.broadcasted_iota(jnp.int32, (rows, COLS), 1)
    return (lane > 0) & (lane < FOLD), lane > FOLD


def turned_half(value):
    return pltpu.roll(value, FOLD, axis=1)


def transformed(re, im, table):
    rows = re.shape[0]
    out = dot_packed(jnp.concatenate([re, im], axis=0), table)
    re, im = out[:rows], out[rows:]
    lower, upper = lanes(rows)
    far_re, far_im = turned_half(re), turned_half(im)
    out_re = jnp.where(upper, far_re - im, re + jnp.where(lower, far_im, 0.0))
    out_im = jnp.where(upper, far_im + re, im - jnp.where(lower, far_re, 0.0))
    return out_re, out_im


def transformed_back(re, im, table):
    rows = re.shape[0]
    lower, upper = lanes(rows)
    far_re, far_im = turned_half(re), turned_half(im)
    even_re = jnp.where(upper, far_im - im, re + jnp.where(lower, far_re, 0.0))
    even_im = jnp.where(upper, re - far_re, im + jnp.where(lower, far_im, 0.0))
    out = dot_packed(jnp.concatenate([even_re, even_im], axis=0), table)
    return out[:rows], out[rows:]


def first_stage(lower, upper, first_ref):
    def joined(a, b):
        a = a.astype(F32).reshape(ODD, SLOTS, COLS)
        b = b.astype(F32).reshape(ODD, SLOTS, COLS)
        front = lax.broadcasted_iota(jnp.int32, a.shape, 1) < SLOTS // 2
        even = jnp.where(front, a, pltpu.roll(b, SLOTS // 2, axis=1))
        odd = jnp.where(front, pltpu.roll(a, SLOTS // 2, axis=1), b)
        return [part.reshape(ODD * SLOTS, COLS).astype(BF16) for part in (even, odd)]

    parts = [joined(a, b) for a, b in zip(lower, upper)]
    sums = []
    for parity in range(2):
        held = jnp.concatenate([part[parity] for part in parts], axis=1)
        sums.append(dot(first_ref[parity], jnp.concatenate([held, held], axis=0)))
    plus, minus = sums[0] + sums[1], sums[0] - sums[1]
    half = ODD // 2

    def group(value, i):
        return value[i * SLOTS : (i + 1) * SLOTS]

    none = jnp.zeros_like(group(plus, 0))
    back = list(range(half - 1, -1, -1))
    re = [group(plus, i) for i in range(half + 1)] + [group(minus, i) for i in back]
    re += [group(plus, half + 1 + i) for i in range(half)]
    re += [group(minus, half + 1 + i) for i in back]
    at = 2 * half + 1
    im = [none] + [group(plus, at + i) for i in range(half)]
    im += [-group(minus, at + i) for i in back[1:]] + [none]
    im += [group(plus, at + half + i) for i in range(half)]
    im += [-group(minus, at + half + i) for i in back]
    return jnp.concatenate(re, axis=0), jnp.concatenate(im, axis=0)


def twisted(re, im, twist_ref):
    re = re.reshape(HALF, SLOTS, COLS)
    im = im.reshape(HALF, SLOTS, COLS)
    cos = twist_ref[0][:, None, :]
    sin = twist_ref[1][:, None, :]
    out_re = (re * cos + im * sin).reshape(HALF * SLOTS, COLS)
    out_im = (im * cos - re * sin).reshape(HALF * SLOTS, COLS)
    return out_re, out_im


def smoothed(power):
    power = power.reshape(HALF, SLOTS, COLS)
    lane = lax.broadcasted_iota(jnp.int32, (SLOTS, COLS), 1)
    below = jnp.where(lane % FOLD == 0, lane, (lane + FOLD) % COLS)
    above = jnp.where(lane < FOLD, lane + FOLD + 1, lane - FOLD - 1)
    above = jnp.where(lane == FOLD - 1, FOLD, jnp.where(lane == FOLD, FOLD - 1, above))

    def mirrored(row, index):
        return jnp.take_along_axis(power[row], index, axis=1)[None]

    even = jnp.concatenate(
        [mirrored(1, below), power[:EVEN], mirrored(EVEN - 2, above)], axis=0
    )
    odd = jnp.concatenate(
        [mirrored(EVEN, below), power[EVEN:], mirrored(HALF - 1, above)], axis=0
    )
    pairs_even = even[:-1] + even[1:]
    pairs_odd = odd[:-1] + odd[1:]
    smooth_even = (pairs_even[:-1] + even[2:]) + pairs_odd
    smooth_odd = (pairs_odd[:-1] + odd[2:]) + pairs_even[1:-1]
    return jnp.concatenate([smooth_even, smooth_odd], axis=0).reshape(HALF * SLOTS, COLS)


def placed(value, index):
    rows = value.shape[0] // SLOTS
    value = value.reshape(rows, SLOTS, COLS)
    index = jnp.broadcast_to(index[None], value.shape)
    return jnp.take_along_axis(value, index, axis=1).reshape(rows * SLOTS, COLS)


def kernel(
    sizes_ref, partner_ref, rows_ref, first_ref, twist_ref, second_ref, last_ref,
    plain_ref, refined_ref,
):
    windows = rows_ref.shape[0] // 2
    count = SLOTS // 2
    share = plain_ref.shape[0]
    mine, block = lax.axis_index("tm"), lax.axis_index("stn")
    other = jnp.bitwise_xor(block, partner_ref[:, 0:1])
    pair = mine * share + lax.broadcasted_iota(jnp.int32, (SLOTS, COLS), 0)
    near_slot = jnp.minimum(pair // count, count - 1)
    far_slot = pair % count
    near_index = near_slot + jnp.where(block < other, 0, count)
    far_index = far_slot + jnp.where(block < other, count, 0)

    grid_re, grid_im = first_stage(
        [rows_ref[j] for j in range(windows)],
        [rows_ref[windows + j] for j in range(windows)],
        first_ref,
    )
    size, evens = HALF * SLOTS, EVEN * SLOTS
    spectra = []
    power = 0.0
    later = None
    for j in reversed(range(windows)):
        cols = slice(j * COLS, (j + 1) * COLS)
        here = twisted(grid_re[:, cols], grid_im[:, cols], twist_ref)
        value = here
        if later is not None:
            value = [
                jnp.concatenate([a[:evens] + b[:evens], a[evens:] - b[evens:]], axis=0)
                for a, b in zip(here, later)
            ]
        later = here
        re, im = transformed(*value, second_ref[0])
        power = power + (re * re + im * im)
        spectra.append((re, im))
    level = smoothed(power) * (1.0 / (5 * windows)) + SMALL
    root = lax.rsqrt(level)
    by_row = (power * (root * root)).reshape(HALF, SLOTS, COLS)
    total = 2.0 * jnp.sum(by_row, axis=0) - by_row[0] - by_row[EVEN - 1]
    mean = jnp.sum(total, axis=1, keepdims=True) * (1.0 / PERIOD)
    keep = (1.0 - by_row / (mean + SMALL)[None]).reshape(size, COLS)
    keep = placed(keep, near_index)
    re = im = 0.0
    for spec_re, spec_im in spectra:
        spec_re, spec_im = spec_re * root, spec_im * root
        near_re, near_im = placed(spec_re, near_index), placed(spec_im, near_index)
        far_re, far_im = placed(spec_re, far_index), placed(spec_im, far_index)
        re = re + (near_re * far_re + near_im * far_im)
        im = im + (near_im * far_re - near_re * far_im)
    halves = []
    for value_re, value_im in ((re, im), (re * keep, im * keep)):
        half = transformed_back(value_re, value_im, second_ref[1])
        halves.append(twisted(*half, twist_ref))
    half_re = jnp.concatenate([halves[0][0], halves[1][0]], axis=1)
    half_im = jnp.concatenate([halves[0][1], halves[1][1]], axis=1)
    edge = evens - SLOTS
    middle = half_re[edge:evens] * (1.0 / math.sqrt(PERIOD * windows))
    same = jnp.concatenate([half_re[:edge], half_im[evens:]], axis=0)
    turned = jnp.concatenate([half_re[evens:], half_im[:edge]], axis=0)
    same = dot_split((last_ref[0, 0], last_ref[1, 0]), split(same))
    turned = dot_split((last_ref[0, 1], last_ref[1, 1]), split(turned))

    places = lax.broadcasted_iota(jnp.int32, sizes_ref.shape, 1)
    held = sizes_ref[...]
    live_near = jnp.sum(jnp.where(places == block, held, 0), axis=1, keepdims=True)
    live_far = jnp.sum(jnp.where(places == other, held, 0), axis=1, keepdims=True)
    live = ((near_slot < live_near) & (far_slot < live_far)).astype(F32)
    for j in range(EVEN):
        rows = slice(j * SLOTS, (j + 1) * SLOTS)
        steady = same[rows] + (middle if j % 2 == 0 else -middle)
        mirrored = [(2 * ODD - j, steady - turned[rows])] if 0 < j < ODD else []
        for lag, here in [(j, steady + turned[rows])] + mirrored:
            cols = slice(lag * COLS, (lag + 1) * COLS)
            plain_ref[:, cols] = (here[:, :COLS] * live)[:share]
            refined_ref[:, cols] = (here[:, COLS:] * live)[:share]


def per_device(samples, array_sizes, partner):
    count = samples.shape[0]
    groups = lax.axis_size("tm")
    blocks = lax.axis_size("stn")
    share = count * count // groups
    rows = samples.reshape(count, LAGS // COLS, COLS).transpose(1, 0, 2).reshape(-1, COLS)

    def gathered(number, held):
        pairs = [(low, low ^ number) for low in range(blocks) if low < low ^ number]
        return lax.all_gather(
            held,
            ("stn", "tm"),
            axis_index_groups=[
                [block * groups + t for block in pair for t in range(groups)] for pair in pairs
            ],
        )

    number = jnp.minimum(partner[0], jnp.maximum(partner[0], array_sizes[0]))
    both = lax.switch(
        number - 1, [functools.partial(gathered, number) for number in range(1, blocks)], rows
    )
    vmem = pl.BlockSpec(memory_space=pltpu.VMEM)
    out = jax.ShapeDtypeStruct((share, LAGS), F32)
    return pl.pallas_call(
        kernel,
        out_shape=(out, out),
        in_specs=[vmem] * 7,
        out_specs=(vmem, vmem),
        compiler_params=pltpu.CompilerParams(vmem_limit_bytes=40 * 1024 * 1024),
    )(array_sizes[None], partner[None], both, *tables(count, groups))


def solution(mesh):
    placed = (P("stn", "tm"), P(), P())
    return jax.shard_map(
        per_device,
        mesh=mesh,
        in_specs=placed,
        out_specs=(P(("stn", "tm"), None), P(("stn", "tm"), None)),
        check_vma=False,
    )
```

```python
import functools
import math

import jax
import jax.numpy as jnp
import numpy as np
from jax import lax
from jax.experimental import pallas as pl
from jax.experimental.pallas import tpu as pltpu
from jax.sharding import PartitionSpec as P

LAGS = 4096
PERIOD = 2 * LAGS
ROWS = 64
COLS = 128
EVEN = ROWS // 4 + 1
ODD = ROWS // 4
HALF = EVEN + ODD
FOLD = COLS // 2
SLOTS = 8
SMALL = 1e-06
F32 = jnp.float32
BF16 = jnp.bfloat16


def split_table(table):
    high = table.astype(np.float32).astype(jnp.bfloat16)
    low = (table - high.astype(np.float64)).astype(np.float32).astype(jnp.bfloat16)
    return np.stack([high, low])


@functools.lru_cache(maxsize=None)
def tables(count, windows):
    f1 = np.concatenate([np.arange(0, ROWS // 2 + 1, 2), np.arange(1, ROWS // 2, 2)])
    lag = np.arange(LAGS // COLS)
    angle = 2 * np.pi * ((f1[:, None] * lag[None, :]) % ROWS) / ROWS
    half = ODD // 2
    base = np.concatenate([np.arange(half + 1), np.arange(EVEN, EVEN + half)])
    first = []
    for parity in range(2):
        kept = angle[base, parity::2]
        part = np.concatenate([np.cos(kept), -np.sin(kept[1:])])
        part = part[:, None, :, None] * np.eye(SLOTS)[None, :, None, :]
        first.append(np.concatenate(list(split_table(part.reshape(-1, COLS))), axis=1))
    first = np.stack(first)
    n2 = np.arange(COLS)
    twist = 2 * np.pi * ((f1[:, None] * n2[None, :]) % PERIOD) / PERIOD
    twist = np.stack([np.cos(twist), np.sin(twist)]).astype(np.float32)
    folded = np.where(n2 > FOLD, n2 - FOLD, n2)
    turn = 2 * np.pi * ((n2[:, None] * folded[None, :]) % COLS) / COLS
    turn = np.where(n2 > FOLD, np.sin(turn), np.cos(turn))
    second = []
    for table in (turn, turn.T):
        high, low = split_table(table)
        second.append(np.block([[high, low], [high, np.zeros_like(low)]]))
    second = np.stack(second)
    weight = np.where(f1 % (ROWS // 2) == 0, 1.0, 2.0)[:, None] / math.sqrt(PERIOD * windows)
    cos, sin = (np.cos(angle) * weight)[:, :EVEN].T, (np.sin(angle) * weight)[:, :EVEN].T
    same = np.concatenate([cos[:, : EVEN - 1], sin[:, EVEN:]], axis=1)
    turned = np.concatenate([cos[:, EVEN:], sin[:, : EVEN - 1]], axis=1)
    last = np.stack([np.kron(same, np.eye(SLOTS)), np.kron(turned, np.eye(SLOTS))])
    last = split_table(last).reshape(4, EVEN * SLOTS, 2 * COLS)

    def padded(table):
        extra = -table.shape[1] % 16
        return np.pad(table, ((0, 0), (0, extra), (0, 0))).reshape(-1, 2 * COLS)

    near = np.concatenate([padded(first), second[0]])
    far = np.concatenate([padded(first), second[0], second[1], padded(last)])
    far_twist = np.pad(twist, ((0, 0), (0, -HALF % SLOTS), (0, 0)))
    return near, twist, far, far_twist


def table_slice(ref, which):
    rows = -(-HALF * SLOTS // 16) * 16
    if which < 2:
        return ref[which * rows : which * rows + HALF * SLOTS]
    start = 2 * rows + (which - 2) * 2 * COLS
    if which < 4:
        return ref[start : start + 2 * COLS]
    rows = -(-EVEN * SLOTS // 16) * 16
    start = 2 * -(-HALF * SLOTS // 16) * 16 + 4 * COLS + (which - 4) * rows
    return ref[start : start + EVEN * SLOTS]


def dot(left, right):
    return jnp.dot(left, right, preferred_element_type=F32)


def split(value):
    high = value.astype(BF16)
    return high, (value - high.astype(F32)).astype(BF16)


def dot_split(left, right):
    rows = left[0].shape[0]
    both = dot(jnp.concatenate(left, axis=0), right[0])
    return both[:rows] + (both[rows:] + dot(left[0], right[1]))


def dot_packed(value, table):
    out = dot(jnp.concatenate(split(value), axis=1), table)
    return out[:, :COLS] + out[:, COLS:]


def lanes(rows):
    lane = lax.broadcasted_iota(jnp.int32, (rows, COLS), 1)
    return (lane > 0) & (lane < FOLD), lane > FOLD


def turned_half(value):
    return pltpu.roll(value, FOLD, axis=1)


def transformed(re, im, table):
    rows = re.shape[0]
    out = dot_packed(jnp.concatenate([re, im], axis=0), table)
    re, im = out[:rows], out[rows:]
    lower, upper = lanes(rows)
    far_re, far_im = turned_half(re), turned_half(im)
    out_re = jnp.where(upper, far_re - im, re + jnp.where(lower, far_im, 0.0))
    out_im = jnp.where(upper, far_im + re, im - jnp.where(lower, far_re, 0.0))
    return out_re, out_im


def transformed_back(re, im, table):
    rows = re.shape[0]
    lower, upper = lanes(rows)
    far_re, far_im = turned_half(re), turned_half(im)
    even_re = jnp.where(upper, far_im - im, re + jnp.where(lower, far_re, 0.0))
    even_im = jnp.where(upper, re - far_re, im + jnp.where(lower, far_im, 0.0))
    out = dot_packed(jnp.concatenate([even_re, even_im], axis=0), table)
    return out[:rows], out[rows:]


def first_stage(lower, upper, tables_ref):
    def joined(a, b):
        a = a.astype(F32).reshape(ODD, SLOTS, COLS)
        b = b.astype(F32).reshape(ODD, SLOTS, COLS)
        front = lax.broadcasted_iota(jnp.int32, a.shape, 1) < SLOTS // 2
        even = jnp.where(front, a, pltpu.roll(b, SLOTS // 2, axis=1))
        odd = jnp.where(front, pltpu.roll(a, SLOTS // 2, axis=1), b)
        return [part.reshape(ODD * SLOTS, COLS).astype(BF16) for part in (even, odd)]

    parts = [joined(a, b) for a, b in zip(lower, upper)]
    sums = []
    for parity in range(2):
        held = jnp.concatenate([part[parity] for part in parts], axis=1)
        sums.append(dot(table_slice(tables_ref, parity), jnp.concatenate([held, held], axis=0)))
    plus, minus = sums[0] + sums[1], sums[0] - sums[1]
    half = ODD // 2

    def group(value, i):
        return value[i * SLOTS : (i + 1) * SLOTS]

    none = jnp.zeros_like(group(plus, 0))
    back = list(range(half - 1, -1, -1))
    re = [group(plus, i) for i in range(half + 1)] + [group(minus, i) for i in back]
    re += [group(plus, half + 1 + i) for i in range(half)]
    re += [group(minus, half + 1 + i) for i in back]
    at = 2 * half + 1
    im = [none] + [group(plus, at + i) for i in range(half)]
    im += [-group(minus, at + i) for i in back[1:]] + [none]
    im += [group(plus, at + half + i) for i in range(half)]
    im += [-group(minus, at + half + i) for i in back]
    return jnp.concatenate(re, axis=0), jnp.concatenate(im, axis=0)


def twisted(re, im, twist_ref):
    re = re.reshape(HALF, SLOTS, COLS)
    im = im.reshape(HALF, SLOTS, COLS)
    cos = twist_ref[0, :HALF][:, None, :]
    sin = twist_ref[1, :HALF][:, None, :]
    out_re = (re * cos + im * sin).reshape(HALF * SLOTS, COLS)
    out_im = (im * cos - re * sin).reshape(HALF * SLOTS, COLS)
    return out_re, out_im


def smoothed(power):
    power = power.reshape(HALF, SLOTS, COLS)
    lane = lax.broadcasted_iota(jnp.int32, (SLOTS, COLS), 1)
    below = jnp.where(lane % FOLD == 0, lane, (lane + FOLD) % COLS)
    above = jnp.where(lane < FOLD, lane + FOLD + 1, lane - FOLD - 1)
    above = jnp.where(lane == FOLD - 1, FOLD, jnp.where(lane == FOLD, FOLD - 1, above))

    def mirrored(row, index):
        return jnp.take_along_axis(power[row], index, axis=1)[None]

    even = jnp.concatenate(
        [mirrored(1, below), power[:EVEN], mirrored(EVEN - 2, above)], axis=0
    )
    odd = jnp.concatenate(
        [mirrored(EVEN, below), power[EVEN:], mirrored(HALF - 1, above)], axis=0
    )
    pairs_even = even[:-1] + even[1:]
    pairs_odd = odd[:-1] + odd[1:]
    smooth_even = (pairs_even[:-1] + even[2:]) + pairs_odd
    smooth_odd = (pairs_odd[:-1] + odd[2:]) + pairs_even[1:-1]
    return jnp.concatenate([smooth_even, smooth_odd], axis=0).reshape(HALF * SLOTS, COLS)


def placed(value, index):
    rows = value.shape[0] // SLOTS
    value = value.reshape(rows, SLOTS, COLS)
    index = jnp.broadcast_to(index[None], value.shape)
    return jnp.take_along_axis(value, index, axis=1).reshape(rows * SLOTS, COLS)


def in_order(rows_ref, start):
    mine = lax.axis_index("tm")
    windows = lax.axis_size("tm")
    return [rows_ref[start + jnp.bitwise_xor(mine, j)] for j in range(windows)]


def whitened(halves, tables_ref, twist_ref):
    windows = len(halves)
    size, evens = HALF * SLOTS, EVEN * SLOTS
    grid_re, grid_im = first_stage(halves[0::2], halves[1::2], tables_ref)
    front = lax.broadcasted_iota(jnp.int32, (HALF, SLOTS, COLS), 1) < SLOTS // 2

    def rolled(value):
        return pltpu.roll(value.reshape(HALF, SLOTS, COLS), SLOTS // 2, axis=1)

    table = table_slice(tables_ref, 2)
    packs = []
    power = 0.0
    later = None
    for g in reversed(range(windows // 2)):
        cols = slice(g * COLS, (g + 1) * COLS)
        here = twisted(grid_re[:, cols], grid_im[:, cols], twist_ref)
        turned = [rolled(part) for part in here]
        value = []
        for i in range(2):
            follow = 0.0 if later is None else later[i]
            follow = jnp.where(front, turned[i], follow).reshape(size, COLS)
            value.append(
                jnp.concatenate(
                    [here[i][:evens] + follow[:evens], here[i][evens:] - follow[evens:]], axis=0
                )
            )
        later = turned
        re, im = transformed(*value, table)
        power = power + (re * re + im * im)
        packs.insert(0, (re, im))
    power = power + rolled(power).reshape(size, COLS)
    root = lax.rsqrt(smoothed(power) * (1.0 / (5 * windows)) + SMALL)
    return [(re * root, im * root) for re, im in packs], power, root


def pair_slots(share):
    pair = lax.axis_index("tm") * share + lax.broadcasted_iota(jnp.int32, (SLOTS, COLS), 0)
    count = SLOTS // 2
    return jnp.minimum(pair // count, count - 1), pair % count


def near_kernel(
    share, rows_ref, partner_ref, sizes_hbm, tables_hbm, twist_hbm, near_ref, keep_ref,
    sizes_ref, tables_ref, twist_ref, sems,
):
    fetches = [
        pltpu.make_async_copy(tables_hbm, tables_ref, sems.at[0]),
        pltpu.make_async_copy(twist_hbm, twist_ref, sems.at[1]),
        pltpu.make_async_copy(sizes_hbm, sizes_ref, sems.at[2]),
    ]
    for fetch in fetches:
        fetch.start()
    for fetch in fetches:
        fetch.wait()
    windows = rows_ref.shape[0]
    slot, far_slot = pair_slots(share)
    packs, power, root = whitened(in_order(rows_ref, 0), tables_ref, twist_ref)
    for g, pack in enumerate(packs):
        for h in range(2):
            for i in range(2):
                near_ref[2 * g + h, i] = placed(pack[i], slot + h * (SLOTS // 2))
    by_row = (power * (root * root)).reshape(HALF, SLOTS, COLS)
    total = 2.0 * jnp.sum(by_row, axis=0) - by_row[0] - by_row[EVEN - 1]
    mean = jnp.sum(total, axis=1, keepdims=True) * (1.0 / PERIOD)
    keep = (1.0 - by_row / (mean + SMALL)[None]).reshape(HALF * SLOTS, COLS)
    keep_ref[: HALF * SLOTS] = placed(keep, slot)
    block = lax.axis_index("stn")
    other = jnp.bitwise_xor(block, partner_ref[:, 0:1])
    places = lax.broadcasted_iota(jnp.int32, sizes_ref.shape, 1)
    sizes = sizes_ref[...]
    live_near = jnp.sum(jnp.where(places == block, sizes, 0), axis=1, keepdims=True)
    live_far = jnp.sum(jnp.where(places == other, sizes, 0), axis=1, keepdims=True)
    keep_ref[HALF * SLOTS :] = ((slot < live_near) & (far_slot < live_far)).astype(F32)


def far_kernel(rows_ref, near_ref, keep_ref, tables_ref, twist_ref, plain_ref, refined_ref):
    windows = near_ref.shape[0]
    share = plain_ref.shape[0]
    _, far_slot = pair_slots(share)
    evens = EVEN * SLOTS
    packs, _, _ = whitened(in_order(rows_ref, windows), tables_ref, twist_ref)
    re = im = 0.0
    for g, pack in enumerate(packs):
        for h in range(2):
            index = far_slot + h * (SLOTS // 2)
            far_re, far_im = placed(pack[0], index), placed(pack[1], index)
            near_re, near_im = near_ref[2 * g + h, 0], near_ref[2 * g + h, 1]
            re = re + (near_re * far_re + near_im * far_im)
            im = im + (near_im * far_re - near_re * far_im)
    keep, live = keep_ref[: HALF * SLOTS], keep_ref[HALF * SLOTS :]
    back = table_slice(tables_ref, 3)
    halves = []
    for value_re, value_im in ((re, im), (re * keep, im * keep)):
        half = transformed_back(value_re, value_im, back)
        halves.append(twisted(*half, twist_ref))
    half_re = jnp.concatenate([halves[0][0], halves[1][0]], axis=1)
    half_im = jnp.concatenate([halves[0][1], halves[1][1]], axis=1)
    edge = evens - SLOTS
    middle = half_re[edge:evens] * (1.0 / math.sqrt(PERIOD * windows))
    same = jnp.concatenate([half_re[:edge], half_im[evens:]], axis=0)
    turned = jnp.concatenate([half_re[evens:], half_im[:edge]], axis=0)
    same = dot_split((table_slice(tables_ref, 4), table_slice(tables_ref, 6)), split(same))
    turned = dot_split((table_slice(tables_ref, 5), table_slice(tables_ref, 7)), split(turned))

    for j in range(EVEN):
        rows = slice(j * SLOTS, (j + 1) * SLOTS)
        steady = same[rows] + (middle if j % 2 == 0 else -middle)
        mirrored = [(2 * ODD - j, steady - turned[rows])] if 0 < j < ODD else []
        for lag, here in [(j, steady + turned[rows])] + mirrored:
            cols = slice(lag * COLS, (lag + 1) * COLS)
            plain_ref[:, cols] = (here[:, :COLS] * live)[:share]
            refined_ref[:, cols] = (here[:, COLS:] * live)[:share]


def per_device(samples, array_sizes, partner):
    count = samples.shape[0]
    groups = lax.axis_size("tm")
    blocks = lax.axis_size("stn")
    share = count * count // groups
    size = HALF * SLOTS
    vmem = pl.BlockSpec(memory_space=pltpu.VMEM)
    hbm = pl.BlockSpec(memory_space=pltpu.HBM)
    params = pltpu.CompilerParams(vmem_limit_bytes=32 * 1024 * 1024)
    near_tables, near_twist, far_tables, far_twist = tables(count, groups)

    rows = samples.reshape(count, LAGS // COLS, COLS).transpose(1, 0, 2).reshape(-1, COLS)
    held = jnp.stack(
        [
            lax.ppermute(rows, "tm", [(i, i ^ step) for i in range(groups)])
            for step in range(groups)
        ]
    )

    def in_hbm(value):
        return pltpu.with_memory_space_constraint(value, pltpu.HBM)

    def exchanged(number, held, partner, sizes, tables, twist):
        far = lax.ppermute(held, "stn", [(i, i ^ number) for i in range(blocks)])
        near, keep = pl.pallas_call(
            functools.partial(near_kernel, share),
            out_shape=(
                jax.ShapeDtypeStruct((groups, 2, size, COLS), F32),
                jax.ShapeDtypeStruct((size + SLOTS, COLS), F32),
            ),
            in_specs=[vmem, vmem, hbm, hbm, hbm],
            out_specs=(vmem, vmem),
            scratch_shapes=[
                pltpu.VMEM(sizes.shape, sizes.dtype),
                pltpu.VMEM(tables.shape, tables.dtype),
                pltpu.VMEM(twist.shape, twist.dtype),
                pltpu.SemaphoreType.DMA((3,)),
            ],
            compiler_params=params,
        )(held, partner, in_hbm(sizes), in_hbm(tables), in_hbm(twist))
        return jnp.concatenate([held, far], axis=0), near, keep

    both, near, keep = lax.switch(
        partner[0] - 1,
        [functools.partial(exchanged, number) for number in range(1, blocks)],
        held, partner[None], array_sizes[None], jnp.asarray(near_tables), jnp.asarray(near_twist),
    )
    out = jax.ShapeDtypeStruct((share, LAGS), F32)
    return pl.pallas_call(
        far_kernel,
        out_shape=(out, out),
        in_specs=[vmem] * 5,
        out_specs=(vmem, vmem),
        compiler_params=params,
    )(both, near, keep, far_tables, far_twist)


def solution(mesh):
    placed = (P("stn", "tm"), P(), P())
    return jax.shard_map(
        per_device,
        mesh=mesh,
        in_specs=placed,
        out_specs=(P(("stn", "tm"), None), P(("stn", "tm"), None)),
        check_vma=False,
    )
```

```python
import functools
import math

import jax
import jax.numpy as jnp
import numpy as np
from jax import lax
from jax.experimental import pallas as pl
from jax.experimental.pallas import tpu as pltpu
from jax.sharding import PartitionSpec as P

LAGS = 4096
PERIOD = 2 * LAGS
ROWS = 64
COLS = 128
EVEN = ROWS // 4 + 1
ODD = ROWS // 4
HALF = EVEN + ODD
FOLD = COLS // 2
SLOTS = 8
SMALL = 1e-06
F32 = jnp.float32
BF16 = jnp.bfloat16


def split_table(table):
    high = table.astype(np.float32).astype(jnp.bfloat16)
    low = (table - high.astype(np.float64)).astype(np.float32).astype(jnp.bfloat16)
    return np.stack([high, low])


@functools.lru_cache(maxsize=None)
def tables(count, windows):
    f1 = np.concatenate([np.arange(0, ROWS // 2 + 1, 2), np.arange(1, ROWS // 2, 2)])
    lag = np.arange(LAGS // COLS)
    angle = 2 * np.pi * ((f1[:, None] * lag[None, :]) % ROWS) / ROWS
    half = ODD // 2
    base = np.concatenate([np.arange(half + 1), np.arange(EVEN, EVEN + half)])
    first = []
    for parity in range(2):
        kept = angle[base, parity::2]
        part = np.concatenate([np.cos(kept), -np.sin(kept[1:])])
        part = part[:, None, :, None] * np.eye(SLOTS)[None, :, None, :]
        first.append(np.concatenate(list(split_table(part.reshape(-1, COLS))), axis=1))
    first = np.stack(first)
    n2 = np.arange(COLS)
    twist = 2 * np.pi * ((f1[:, None] * n2[None, :]) % PERIOD) / PERIOD
    twist = np.stack([np.cos(twist), np.sin(twist)]).astype(np.float32)
    folded = np.where(n2 > FOLD, n2 - FOLD, n2)
    turn = 2 * np.pi * ((n2[:, None] * folded[None, :]) % COLS) / COLS
    turn = np.where(n2 > FOLD, np.sin(turn), np.cos(turn))
    second = []
    for table in (turn, turn.T):
        high, low = split_table(table)
        second.append(np.block([[high, low], [high, np.zeros_like(low)]]))
    second = np.stack(second)
    weight = np.where(f1 % (ROWS // 2) == 0, 1.0, 2.0)[:, None] / math.sqrt(PERIOD * windows)
    cos, sin = (np.cos(angle) * weight)[:, :EVEN].T, (np.sin(angle) * weight)[:, :EVEN].T
    same = np.concatenate([cos[:, : EVEN - 1], sin[:, EVEN:]], axis=1)
    turned = np.concatenate([cos[:, EVEN:], sin[:, : EVEN - 1]], axis=1)
    last = np.stack([np.kron(same, np.eye(SLOTS)), np.kron(turned, np.eye(SLOTS))])
    last = split_table(last).reshape(4, EVEN * SLOTS, 2 * COLS)

    def padded(table):
        extra = -table.shape[1] % 16
        return np.pad(table, ((0, 0), (0, extra), (0, 0))).reshape(-1, 2 * COLS)

    return np.concatenate([padded(first), second[0], second[1], padded(last)]), twist


def table_slice(ref, which):
    rows = -(-HALF * SLOTS // 16) * 16
    if which < 2:
        return ref[which * rows : which * rows + HALF * SLOTS]
    start = 2 * rows + (which - 2) * 2 * COLS
    if which < 4:
        return ref[start : start + 2 * COLS]
    rows = -(-EVEN * SLOTS // 16) * 16
    start = 2 * -(-HALF * SLOTS // 16) * 16 + 4 * COLS + (which - 4) * rows
    return ref[start : start + EVEN * SLOTS]


def dot(left, right):
    return jnp.dot(left, right, preferred_element_type=F32)


def split(value):
    high = value.astype(BF16)
    return high, (value - high.astype(F32)).astype(BF16)


def dot_split(left, right):
    rows = left[0].shape[0]
    both = dot(jnp.concatenate(left, axis=0), right[0])
    return both[:rows] + (both[rows:] + dot(left[0], right[1]))


def dot_packed(value, table):
    out = dot(jnp.concatenate(split(value), axis=1), table)
    return out[:, :COLS] + out[:, COLS:]


def lanes(rows):
    lane = lax.broadcasted_iota(jnp.int32, (rows, COLS), 1)
    return (lane > 0) & (lane < FOLD), lane > FOLD


def turned_half(value):
    return pltpu.roll(value, FOLD, axis=1)


def transformed(re, im, table):
    rows = re.shape[0]
    out = dot_packed(jnp.concatenate([re, im], axis=0), table)
    re, im = out[:rows], out[rows:]
    lower, upper = lanes(rows)
    far_re, far_im = turned_half(re), turned_half(im)
    out_re = jnp.where(upper, far_re - im, re + jnp.where(lower, far_im, 0.0))
    out_im = jnp.where(upper, far_im + re, im - jnp.where(lower, far_re, 0.0))
    return out_re, out_im


def transformed_back(re, im, table):
    rows = re.shape[0]
    lower, upper = lanes(rows)
    far_re, far_im = turned_half(re), turned_half(im)
    even_re = jnp.where(upper, far_im - im, re + jnp.where(lower, far_re, 0.0))
    even_im = jnp.where(upper, re - far_re, im + jnp.where(lower, far_im, 0.0))
    out = dot_packed(jnp.concatenate([even_re, even_im], axis=0), table)
    return out[:rows], out[rows:]


def first_stage(lower, upper, tables_ref):
    def joined(a, b):
        a = a.astype(F32).reshape(ODD, SLOTS, COLS)
        b = b.astype(F32).reshape(ODD, SLOTS, COLS)
        front = lax.broadcasted_iota(jnp.int32, a.shape, 1) < SLOTS // 2
        even = jnp.where(front, a, pltpu.roll(b, SLOTS // 2, axis=1))
        odd = jnp.where(front, pltpu.roll(a, SLOTS // 2, axis=1), b)
        return [part.reshape(ODD * SLOTS, COLS).astype(BF16) for part in (even, odd)]

    parts = [joined(a, b) for a, b in zip(lower, upper)]
    sums = []
    for parity in range(2):
        held = jnp.concatenate([part[parity] for part in parts], axis=1)
        sums.append(dot(table_slice(tables_ref, parity), jnp.concatenate([held, held], axis=0)))
    plus, minus = sums[0] + sums[1], sums[0] - sums[1]
    half = ODD // 2

    def group(value, i):
        return value[i * SLOTS : (i + 1) * SLOTS]

    none = jnp.zeros_like(group(plus, 0))
    back = list(range(half - 1, -1, -1))
    re = [group(plus, i) for i in range(half + 1)] + [group(minus, i) for i in back]
    re += [group(plus, half + 1 + i) for i in range(half)]
    re += [group(minus, half + 1 + i) for i in back]
    at = 2 * half + 1
    im = [none] + [group(plus, at + i) for i in range(half)]
    im += [-group(minus, at + i) for i in back[1:]] + [none]
    im += [group(plus, at + half + i) for i in range(half)]
    im += [-group(minus, at + half + i) for i in back]
    return jnp.concatenate(re, axis=0), jnp.concatenate(im, axis=0)


def twisted(re, im, twist_ref):
    re = re.reshape(HALF, SLOTS, COLS)
    im = im.reshape(HALF, SLOTS, COLS)
    cos = twist_ref[0][:, None, :]
    sin = twist_ref[1][:, None, :]
    out_re = (re * cos + im * sin).reshape(HALF * SLOTS, COLS)
    out_im = (im * cos - re * sin).reshape(HALF * SLOTS, COLS)
    return out_re, out_im


def smoothed(power):
    power = power.reshape(HALF, SLOTS, COLS)
    lane = lax.broadcasted_iota(jnp.int32, (SLOTS, COLS), 1)
    below = jnp.where(lane % FOLD == 0, lane, (lane + FOLD) % COLS)
    above = jnp.where(lane < FOLD, lane + FOLD + 1, lane - FOLD - 1)
    above = jnp.where(lane == FOLD - 1, FOLD, jnp.where(lane == FOLD, FOLD - 1, above))

    def mirrored(row, index):
        return jnp.take_along_axis(power[row], index, axis=1)[None]

    even = jnp.concatenate(
        [mirrored(1, below), power[:EVEN], mirrored(EVEN - 2, above)], axis=0
    )
    odd = jnp.concatenate(
        [mirrored(EVEN, below), power[EVEN:], mirrored(HALF - 1, above)], axis=0
    )
    pairs_even = even[:-1] + even[1:]
    pairs_odd = odd[:-1] + odd[1:]
    smooth_even = (pairs_even[:-1] + even[2:]) + pairs_odd
    smooth_odd = (pairs_odd[:-1] + odd[2:]) + pairs_even[1:-1]
    return jnp.concatenate([smooth_even, smooth_odd], axis=0).reshape(HALF * SLOTS, COLS)


def placed(value, index):
    rows = value.shape[0] // SLOTS
    value = value.reshape(rows, SLOTS, COLS)
    index = jnp.broadcast_to(index[None], value.shape)
    return jnp.take_along_axis(value, index, axis=1).reshape(rows * SLOTS, COLS)


def pair_slots(share):
    pair = lax.axis_index("tm") * share + lax.broadcasted_iota(jnp.int32, (SLOTS, COLS), 0)
    count = SLOTS // 2
    return jnp.minimum(pair // count, count - 1), pair % count


def live_kernel(share, number, sizes_hbm, live_ref, sizes_ref, sem):
    fetch = pltpu.make_async_copy(sizes_hbm, sizes_ref, sem)
    fetch.start()
    fetch.wait()
    block = lax.axis_index("stn")
    other = jnp.bitwise_xor(block, number)
    near_slot, far_slot = pair_slots(share)
    places = lax.broadcasted_iota(jnp.int32, sizes_ref.shape, 1)
    held = sizes_ref[...]
    live_near = jnp.sum(jnp.where(places == block, held, 0), axis=1, keepdims=True)
    live_far = jnp.sum(jnp.where(places == other, held, 0), axis=1, keepdims=True)
    live_ref[...] = ((near_slot < live_near) & (far_slot < live_far)).astype(F32)


def kernel(rows_ref, live_ref, tables_ref, twist_ref, plain_ref, refined_ref):
    windows = rows_ref.shape[0] // 2
    count = SLOTS // 2
    share = plain_ref.shape[0]
    mine = lax.axis_index("tm")
    near_slot, far_slot = pair_slots(share)
    near_index, far_index = near_slot, count + far_slot

    grid_re, grid_im = first_stage(
        [rows_ref[jnp.bitwise_xor(mine, j)] for j in range(windows)],
        [rows_ref[windows + jnp.bitwise_xor(mine, j)] for j in range(windows)],
        tables_ref,
    )
    forth, back = table_slice(tables_ref, 2), table_slice(tables_ref, 3)
    size, evens = HALF * SLOTS, EVEN * SLOTS
    spectra = []
    power = 0.0
    later = None
    for j in reversed(range(windows)):
        cols = slice(j * COLS, (j + 1) * COLS)
        here = twisted(grid_re[:, cols], grid_im[:, cols], twist_ref)
        value = here
        if later is not None:
            value = [
                jnp.concatenate([a[:evens] + b[:evens], a[evens:] - b[evens:]], axis=0)
                for a, b in zip(here, later)
            ]
        later = here
        re, im = transformed(*value, forth)
        power = power + (re * re + im * im)
        spectra.append((re, im))
    level = smoothed(power) * (1.0 / (5 * windows)) + SMALL
    root = lax.rsqrt(level)
    by_row = (power * (root * root)).reshape(HALF, SLOTS, COLS)
    total = 2.0 * jnp.sum(by_row, axis=0) - by_row[0] - by_row[EVEN - 1]
    mean = jnp.sum(total, axis=1, keepdims=True) * (1.0 / PERIOD)
    keep = (1.0 - by_row / (mean + SMALL)[None]).reshape(size, COLS)
    keep = placed(keep, near_index)
    re = im = 0.0
    for spec_re, spec_im in spectra:
        spec_re, spec_im = spec_re * root, spec_im * root
        near_re, near_im = placed(spec_re, near_index), placed(spec_im, near_index)
        far_re, far_im = placed(spec_re, far_index), placed(spec_im, far_index)
        re = re + (near_re * far_re + near_im * far_im)
        im = im + (near_im * far_re - near_re * far_im)
    halves = []
    for value_re, value_im in ((re, im), (re * keep, im * keep)):
        half = transformed_back(value_re, value_im, back)
        halves.append(twisted(*half, twist_ref))
    half_re = jnp.concatenate([halves[0][0], halves[1][0]], axis=1)
    half_im = jnp.concatenate([halves[0][1], halves[1][1]], axis=1)
    edge = evens - SLOTS
    middle = half_re[edge:evens] * (1.0 / math.sqrt(PERIOD * windows))
    same = jnp.concatenate([half_re[:edge], half_im[evens:]], axis=0)
    turned = jnp.concatenate([half_re[evens:], half_im[:edge]], axis=0)
    same = dot_split((table_slice(tables_ref, 4), table_slice(tables_ref, 6)), split(same))
    turned = dot_split((table_slice(tables_ref, 5), table_slice(tables_ref, 7)), split(turned))

    live = live_ref[...]
    for j in range(EVEN):
        rows = slice(j * SLOTS, (j + 1) * SLOTS)
        steady = same[rows] + (middle if j % 2 == 0 else -middle)
        mirrored = [(2 * ODD - j, steady - turned[rows])] if 0 < j < ODD else []
        for lag, here in [(j, steady + turned[rows])] + mirrored:
            cols = slice(lag * COLS, (lag + 1) * COLS)
            plain_ref[:, cols] = (here[:, :COLS] * live)[:share]
            refined_ref[:, cols] = (here[:, COLS:] * live)[:share]


def per_device(samples, array_sizes, partner):
    count = samples.shape[0]
    groups = lax.axis_size("tm")
    blocks = lax.axis_size("stn")
    share = count * count // groups
    vmem = pl.BlockSpec(memory_space=pltpu.VMEM)
    params = pltpu.CompilerParams(vmem_limit_bytes=32 * 1024 * 1024)
    rows = samples.reshape(count, LAGS // COLS, COLS).transpose(1, 0, 2).reshape(-1, COLS)

    def to_fast_memory(value):
        return lax.ppermute(value, "tm", [(i, i) for i in range(groups)])

    own = to_fast_memory(rows)

    def with_others(value):
        return [value] + [
            lax.ppermute(value, "tm", [(i, i ^ step) for i in range(groups)])
            for step in range(1, groups)
        ]

    def exchanged(number, own, sizes):
        far = lax.ppermute(own, "stn", [(i, i ^ number) for i in range(blocks)])
        live = pl.pallas_call(
            functools.partial(live_kernel, share, number),
            out_shape=jax.ShapeDtypeStruct((SLOTS, COLS), F32),
            in_specs=[pl.BlockSpec(memory_space=pltpu.HBM)],
            out_specs=vmem,
            scratch_shapes=[pltpu.VMEM(sizes.shape, sizes.dtype), pltpu.SemaphoreType.DMA],
            compiler_params=params,
        )(pltpu.with_memory_space_constraint(sizes, pltpu.HBM))
        return jnp.stack(with_others(own) + with_others(far)), live

    both, live = lax.switch(
        partner[0] - 1,
        [functools.partial(exchanged, number) for number in range(1, blocks)],
        own, array_sizes[None],
    )
    out = jax.ShapeDtypeStruct((share, LAGS), F32)
    return pl.pallas_call(
        kernel,
        out_shape=(out, out),
        in_specs=[vmem] * 4,
        out_specs=(vmem, vmem),
        compiler_params=params,
    )(both, live, *tables(count, groups))


def solution(mesh):
    placed = (P("stn", "tm"), P(), P())
    return jax.shard_map(
        per_device,
        mesh=mesh,
        in_specs=placed,
        out_specs=(P(("stn", "tm"), None), P(("stn", "tm"), None)),
        check_vma=False,
    )
```

```python
import functools
import math

import jax
import jax.numpy as jnp
import numpy as np
from jax import lax
from jax.experimental import pallas as pl
from jax.experimental.pallas import tpu as pltpu
from jax.sharding import PartitionSpec as P

LAGS = 4096
PERIOD = 2 * LAGS
ROWS = 64
COLS = 128
EVEN = ROWS // 4 + 1
ODD = ROWS // 4
HALF = EVEN + ODD
SLOTS = 8
SMALL = 1e-06
F32 = jnp.float32
BF16 = jnp.bfloat16


def split_table(table):
    high = table.astype(np.float32).astype(jnp.bfloat16)
    low = (table - high.astype(np.float64)).astype(np.float32).astype(jnp.bfloat16)
    return np.stack([high, low])


@functools.lru_cache(maxsize=None)
def tables(count, windows):
    f1 = np.concatenate([np.arange(0, ROWS // 2 + 1, 2), np.arange(1, ROWS // 2, 2)])
    lag = np.arange(LAGS // COLS)
    angle = 2 * np.pi * ((f1[:, None] * lag[None, :]) % ROWS) / ROWS
    half = ODD // 2
    base = np.concatenate([np.arange(half + 1), np.arange(EVEN, EVEN + half)])
    first = []
    for parity in range(2):
        kept = angle[base, parity::2]
        part = np.concatenate([np.cos(kept), -np.sin(kept[1:])])
        part = part[:, None, :, None] * np.eye(SLOTS)[None, :, None, :]
        first.append(np.concatenate(list(split_table(part.reshape(-1, COLS))), axis=1))
    first = np.stack(first)
    n2 = np.arange(COLS)
    twist = 2 * np.pi * ((f1[:, None] * n2[None, :]) % PERIOD) / PERIOD
    twist = np.stack([np.cos(twist), np.sin(twist)]).astype(np.float32)
    turn = 2 * np.pi * ((n2[:, None] * n2[None, :]) % COLS) / COLS
    cos, sin = np.cos(turn), np.sin(turn)
    second = split_table(np.block([[cos, -sin], [sin, cos]]))
    weight = np.where(f1 % (ROWS // 2) == 0, 1.0, 2.0)[:, None] / math.sqrt(PERIOD * windows)
    cos, sin = (np.cos(angle) * weight)[:, :EVEN].T, (np.sin(angle) * weight)[:, :EVEN].T
    same = np.concatenate([cos[:, : EVEN - 1], sin[:, EVEN:]], axis=1)
    turned = np.concatenate([cos[:, EVEN:], sin[:, : EVEN - 1]], axis=1)
    last = np.stack([np.kron(same, np.eye(SLOTS)), np.kron(turned, np.eye(SLOTS))])
    last = split_table(last).reshape(4, EVEN * SLOTS, 2 * COLS)

    def padded(table):
        extra = -table.shape[1] % 16
        return np.pad(table, ((0, 0), (0, extra), (0, 0))).reshape(-1, 2 * COLS)

    return np.concatenate([padded(first), second[0], second[1], padded(last)]), twist


def table_slice(ref, which):
    rows = -(-HALF * SLOTS // 16) * 16
    if which < 2:
        return ref[which * rows : which * rows + HALF * SLOTS]
    start = 2 * rows + (which - 2) * 2 * COLS
    if which < 4:
        return ref[start : start + 2 * COLS]
    rows = -(-EVEN * SLOTS // 16) * 16
    start = 2 * -(-HALF * SLOTS // 16) * 16 + 4 * COLS + (which - 4) * rows
    return ref[start : start + EVEN * SLOTS]


def dot(left, right):
    return jnp.dot(left, right, preferred_element_type=F32)


def split(value):
    high = value.astype(BF16)
    return high, (value - high.astype(F32)).astype(BF16)


def dot_split(left, right):
    rows = left[0].shape[0]
    both = dot(jnp.concatenate(left, axis=0), right[0])
    return both[:rows] + (both[rows:] + dot(left[0], right[1]))


def transformed(re, im, table):
    out = dot_split(split(jnp.concatenate([re, im], axis=1)), table)
    return out[:, :COLS], out[:, COLS:]


def first_stage(lower, upper, tables_ref):
    def joined(a, b):
        a = a.astype(F32).reshape(ODD, SLOTS, COLS)
        b = b.astype(F32).reshape(ODD, SLOTS, COLS)
        front = lax.broadcasted_iota(jnp.int32, a.shape, 1) < SLOTS // 2
        even = jnp.where(front, a, pltpu.roll(b, SLOTS // 2, axis=1))
        odd = jnp.where(front, pltpu.roll(a, SLOTS // 2, axis=1), b)
        return [part.reshape(ODD * SLOTS, COLS).astype(BF16) for part in (even, odd)]

    parts = [joined(a, b) for a, b in zip(lower, upper)]
    sums = []
    for parity in range(2):
        held = jnp.concatenate([part[parity] for part in parts], axis=1)
        sums.append(dot(table_slice(tables_ref, parity), jnp.concatenate([held, held], axis=0)))
    plus, minus = sums[0] + sums[1], sums[0] - sums[1]
    half = ODD // 2

    def group(value, i):
        return value[i * SLOTS : (i + 1) * SLOTS]

    none = jnp.zeros_like(group(plus, 0))
    back = list(range(half - 1, -1, -1))
    re = [group(plus, i) for i in range(half + 1)] + [group(minus, i) for i in back]
    re += [group(plus, half + 1 + i) for i in range(half)]
    re += [group(minus, half + 1 + i) for i in back]
    at = 2 * half + 1
    im = [none] + [group(plus, at + i) for i in range(half)]
    im += [-group(minus, at + i) for i in back[1:]] + [none]
    im += [group(plus, at + half + i) for i in range(half)]
    im += [-group(minus, at + half + i) for i in back]
    return jnp.concatenate(re, axis=0), jnp.concatenate(im, axis=0)


def twisted(re, im, twist_ref):
    re = re.reshape(HALF, SLOTS, COLS)
    im = im.reshape(HALF, SLOTS, COLS)
    cos = twist_ref[0][:, None, :]
    sin = twist_ref[1][:, None, :]
    out_re = (re * cos + im * sin).reshape(HALF * SLOTS, COLS)
    out_im = (im * cos - re * sin).reshape(HALF * SLOTS, COLS)
    return out_re, out_im


def smoothed(power):
    power = power.reshape(HALF, SLOTS, COLS)
    lane = lax.broadcasted_iota(jnp.int32, (SLOTS, COLS), 1)
    below, above = (COLS - lane) % COLS, COLS - 1 - lane

    def mirrored(row, index):
        return jnp.take_along_axis(power[row], index, axis=1)[None]

    even = jnp.concatenate(
        [mirrored(1, below), power[:EVEN], mirrored(EVEN - 2, above)], axis=0
    )
    odd = jnp.concatenate(
        [mirrored(EVEN, below), power[EVEN:], mirrored(HALF - 1, above)], axis=0
    )
    pairs_even = even[:-1] + even[1:]
    pairs_odd = odd[:-1] + odd[1:]
    smooth_even = (pairs_even[:-1] + even[2:]) + pairs_odd
    smooth_odd = (pairs_odd[:-1] + odd[2:]) + pairs_even[1:-1]
    return jnp.concatenate([smooth_even, smooth_odd], axis=0).reshape(HALF * SLOTS, COLS)


def placed(value, index):
    rows = value.shape[0] // SLOTS
    value = value.reshape(rows, SLOTS, COLS)
    index = jnp.broadcast_to(index[None], value.shape)
    return jnp.take_along_axis(value, index, axis=1).reshape(rows * SLOTS, COLS)


def pair_slots(share):
    pair = lax.axis_index("tm") * share + lax.broadcasted_iota(jnp.int32, (SLOTS, COLS), 0)
    count = SLOTS // 2
    return jnp.minimum(pair // count, count - 1), pair % count


def live_kernel(share, number, sizes_hbm, live_ref, sizes_ref, sem):
    fetch = pltpu.make_async_copy(sizes_hbm, sizes_ref, sem)
    fetch.start()
    fetch.wait()
    block = lax.axis_index("stn")
    other = jnp.bitwise_xor(block, number)
    near_slot, far_slot = pair_slots(share)
    places = lax.broadcasted_iota(jnp.int32, sizes_ref.shape, 1)
    held = sizes_ref[...]
    live_near = jnp.sum(jnp.where(places == block, held, 0), axis=1, keepdims=True)
    live_far = jnp.sum(jnp.where(places == other, held, 0), axis=1, keepdims=True)
    live_ref[...] = ((near_slot < live_near) & (far_slot < live_far)).astype(F32)


def kernel(rows_ref, live_ref, tables_ref, twist_ref, plain_ref, refined_ref):
    windows = rows_ref.shape[0] // 2
    count = SLOTS // 2
    share = plain_ref.shape[0]
    mine = lax.axis_index("tm")
    near_slot, far_slot = pair_slots(share)
    near_index, far_index = near_slot, count + far_slot

    grid_re, grid_im = first_stage(
        [rows_ref[jnp.bitwise_xor(mine, j)] for j in range(windows)],
        [rows_ref[windows + jnp.bitwise_xor(mine, j)] for j in range(windows)],
        tables_ref,
    )
    turn = (table_slice(tables_ref, 2), table_slice(tables_ref, 3))
    size, evens = HALF * SLOTS, EVEN * SLOTS
    spectra = []
    power = 0.0
    later = None
    for j in reversed(range(windows)):
        cols = slice(j * COLS, (j + 1) * COLS)
        here = twisted(grid_re[:, cols], grid_im[:, cols], twist_ref)
        value = here
        if later is not None:
            value = [
                jnp.concatenate([a[:evens] + b[:evens], a[evens:] - b[evens:]], axis=0)
                for a, b in zip(here, later)
            ]
        later = here
        re, im = transformed(*value, turn)
        power = power + (re * re + im * im)
        spectra.append((re, im))
    level = smoothed(power) * (1.0 / (5 * windows)) + SMALL
    root = lax.rsqrt(level)
    by_row = (power * (root * root)).reshape(HALF, SLOTS, COLS)
    total = 2.0 * jnp.sum(by_row, axis=0) - by_row[0] - by_row[EVEN - 1]
    mean = jnp.sum(total, axis=1, keepdims=True) * (1.0 / PERIOD)
    scale = 1.0 / (mean + SMALL)
    keep = (1.0 - by_row * scale[None]).reshape(size, COLS)
    keep = placed(keep, near_index)
    re = im = 0.0
    for spec_re, spec_im in spectra:
        spec_re, spec_im = spec_re * root, spec_im * root
        near_re, near_im = placed(spec_re, near_index), placed(spec_im, near_index)
        far_re, far_im = placed(spec_re, far_index), placed(spec_im, far_index)
        re = re + (near_re * far_re + near_im * far_im)
        im = im + (near_im * far_re - near_re * far_im)
    halves = []
    for value_re, value_im in ((re, im), (re * keep, im * keep)):
        half = transformed(value_re, value_im, turn)
        halves.append(twisted(*half, twist_ref))
    half_re = jnp.concatenate([halves[0][0], halves[1][0]], axis=1)
    half_im = jnp.concatenate([halves[0][1], halves[1][1]], axis=1)
    edge = evens - SLOTS
    middle = half_re[edge:evens] * (1.0 / math.sqrt(PERIOD * windows))
    same = jnp.concatenate([half_re[:edge], half_im[evens:]], axis=0)
    turned = jnp.concatenate([half_re[evens:], half_im[:edge]], axis=0)
    same = dot_split((table_slice(tables_ref, 4), table_slice(tables_ref, 6)), split(same))
    turned = dot_split((table_slice(tables_ref, 5), table_slice(tables_ref, 7)), split(turned))

    live = live_ref[...]
    for j in range(EVEN):
        rows = slice(j * SLOTS, (j + 1) * SLOTS)
        steady = same[rows] + (middle if j % 2 == 0 else -middle)
        mirrored = [(2 * ODD - j, steady - turned[rows])] if 0 < j < ODD else []
        for lag, here in [(j, steady + turned[rows])] + mirrored:
            cols = slice(lag * COLS, (lag + 1) * COLS)
            plain_ref[:, cols] = (here[:, :COLS] * live)[:share]
            refined_ref[:, cols] = (here[:, COLS:] * live)[:share]


def per_device(samples, array_sizes, partner):
    count = samples.shape[0]
    groups = lax.axis_size("tm")
    blocks = lax.axis_size("stn")
    share = count * count // groups
    vmem = pl.BlockSpec(memory_space=pltpu.VMEM)
    params = pltpu.CompilerParams(vmem_limit_bytes=32 * 1024 * 1024)
    rows = samples.reshape(count, LAGS // COLS, COLS).transpose(1, 0, 2).reshape(-1, COLS)

    def to_fast_memory(value):
        return lax.ppermute(value, "tm", [(i, i) for i in range(groups)])

    own = to_fast_memory(rows)

    def with_others(value):
        return [value] + [
            lax.ppermute(value, "tm", [(i, i ^ step) for i in range(groups)])
            for step in range(1, groups)
        ]

    def exchanged(number, own, sizes):
        far = lax.ppermute(own, "stn", [(i, i ^ number) for i in range(blocks)])
        live = pl.pallas_call(
            functools.partial(live_kernel, share, number),
            out_shape=jax.ShapeDtypeStruct((SLOTS, COLS), F32),
            in_specs=[pl.BlockSpec(memory_space=pltpu.HBM)],
            out_specs=vmem,
            scratch_shapes=[pltpu.VMEM(sizes.shape, sizes.dtype), pltpu.SemaphoreType.DMA],
            compiler_params=params,
        )(pltpu.with_memory_space_constraint(sizes, pltpu.HBM))
        return jnp.stack(with_others(own) + with_others(far)), live

    both, live = lax.switch(
        partner[0] - 1,
        [functools.partial(exchanged, number) for number in range(1, blocks)],
        own, array_sizes[None],
    )
    out = jax.ShapeDtypeStruct((share, LAGS), F32)
    return pl.pallas_call(
        kernel,
        out_shape=(out, out),
        in_specs=[vmem] * 4,
        out_specs=(vmem, vmem),
        compiler_params=params,
    )(both, live, *tables(count, groups))


def solution(mesh):
    placed = (P("stn", "tm"), P(), P())
    return jax.shard_map(
        per_device,
        mesh=mesh,
        in_specs=placed,
        out_specs=(P(("stn", "tm"), None), P(("stn", "tm"), None)),
        check_vma=False,
    )
```

```python
import functools
import math

import jax
import jax.numpy as jnp
import numpy as np
from jax import lax
from jax.experimental import pallas as pl
from jax.experimental.pallas import tpu as pltpu
from jax.sharding import PartitionSpec as P

LAGS = 4096
PERIOD = 2 * LAGS
ROWS = 64
COLS = 128
EVEN = ROWS // 4 + 1
ODD = ROWS // 4
HALF = EVEN + ODD
SLOTS = 8
SMALL = 1e-06
F32 = jnp.float32
BF16 = jnp.bfloat16


def split_table(table):
    high = table.astype(np.float32).astype(jnp.bfloat16)
    low = (table - high.astype(np.float64)).astype(np.float32).astype(jnp.bfloat16)
    return np.stack([high, low])


@functools.lru_cache(maxsize=None)
def tables(count, windows):
    f1 = np.concatenate([np.arange(0, ROWS // 2 + 1, 2), np.arange(1, ROWS // 2, 2)])
    lag = np.arange(LAGS // COLS)
    angle = 2 * np.pi * ((f1[:, None] * lag[None, :]) % ROWS) / ROWS
    half = ODD // 2
    base = np.concatenate([np.arange(half + 1), np.arange(EVEN, EVEN + half)])
    first = []
    for parity in range(2):
        kept = angle[base, parity::2]
        part = np.concatenate([np.cos(kept), -np.sin(kept[1:])])
        part = part[:, None, :, None] * np.eye(SLOTS)[None, :, None, :]
        first.append(np.concatenate(list(split_table(part.reshape(-1, COLS))), axis=1))
    first = np.stack(first)
    n2 = np.arange(COLS)
    twist = 2 * np.pi * ((f1[:, None] * n2[None, :]) % PERIOD) / PERIOD
    twist = np.stack([np.cos(twist), np.sin(twist)]).astype(np.float32)
    turn = 2 * np.pi * ((n2[:, None] * n2[None, :]) % COLS) / COLS
    cos, sin = np.cos(turn), np.sin(turn)
    second = split_table(np.block([[cos, -sin], [sin, cos]]))
    weight = np.where(f1 % (ROWS // 2) == 0, 1.0, 2.0)[:, None] / math.sqrt(PERIOD * windows)
    cos, sin = (np.cos(angle) * weight)[:, :EVEN].T, (np.sin(angle) * weight)[:, :EVEN].T
    same = np.concatenate([cos[:, : EVEN - 1], sin[:, EVEN:]], axis=1)
    turned = np.concatenate([cos[:, EVEN:], sin[:, : EVEN - 1]], axis=1)
    last = np.stack([np.kron(same, np.eye(SLOTS)), np.kron(turned, np.eye(SLOTS))])
    last = split_table(last).reshape(4, EVEN * SLOTS, 2 * COLS)

    def padded(table):
        extra = -table.shape[1] % 16
        return np.pad(table, ((0, 0), (0, extra), (0, 0))).reshape(-1, 2 * COLS)

    near = np.concatenate([padded(first), second[0], second[1]])
    far_twist = np.pad(twist, ((0, 0), (0, -HALF % SLOTS), (0, 0)))
    return near, twist, np.concatenate([near, padded(last)]), far_twist


def table_slice(ref, which):
    rows = -(-HALF * SLOTS // 16) * 16
    if which < 2:
        return ref[which * rows : which * rows + HALF * SLOTS]
    start = 2 * rows + (which - 2) * 2 * COLS
    if which < 4:
        return ref[start : start + 2 * COLS]
    rows = -(-EVEN * SLOTS // 16) * 16
    start = 2 * -(-HALF * SLOTS // 16) * 16 + 4 * COLS + (which - 4) * rows
    return ref[start : start + EVEN * SLOTS]


def dot(left, right):
    return jnp.dot(left, right, preferred_element_type=F32)


def split(value):
    high = value.astype(BF16)
    return high, (value - high.astype(F32)).astype(BF16)


def dot_split(left, right):
    rows = left[0].shape[0]
    both = dot(jnp.concatenate(left, axis=0), right[0])
    return both[:rows] + (both[rows:] + dot(left[0], right[1]))


def transformed(re, im, table):
    out = dot_split(split(jnp.concatenate([re, im], axis=1)), table)
    return out[:, :COLS], out[:, COLS:]


def first_stage(lower, upper, tables_ref):
    def joined(a, b):
        a = a.astype(F32).reshape(ODD, SLOTS, COLS)
        b = b.astype(F32).reshape(ODD, SLOTS, COLS)
        front = lax.broadcasted_iota(jnp.int32, a.shape, 1) < SLOTS // 2
        even = jnp.where(front, a, pltpu.roll(b, SLOTS // 2, axis=1))
        odd = jnp.where(front, pltpu.roll(a, SLOTS // 2, axis=1), b)
        return [part.reshape(ODD * SLOTS, COLS).astype(BF16) for part in (even, odd)]

    parts = [joined(a, b) for a, b in zip(lower, upper)]
    sums = []
    for parity in range(2):
        held = jnp.concatenate([part[parity] for part in parts], axis=1)
        sums.append(dot(table_slice(tables_ref, parity), jnp.concatenate([held, held], axis=0)))
    plus, minus = sums[0] + sums[1], sums[0] - sums[1]
    half = ODD // 2

    def group(value, i):
        return value[i * SLOTS : (i + 1) * SLOTS]

    none = jnp.zeros_like(group(plus, 0))
    back = list(range(half - 1, -1, -1))
    re = [group(plus, i) for i in range(half + 1)] + [group(minus, i) for i in back]
    re += [group(plus, half + 1 + i) for i in range(half)]
    re += [group(minus, half + 1 + i) for i in back]
    at = 2 * half + 1
    im = [none] + [group(plus, at + i) for i in range(half)]
    im += [-group(minus, at + i) for i in back[1:]] + [none]
    im += [group(plus, at + half + i) for i in range(half)]
    im += [-group(minus, at + half + i) for i in back]
    return jnp.concatenate(re, axis=0), jnp.concatenate(im, axis=0)


def twisted(re, im, twist_ref):
    re = re.reshape(HALF, SLOTS, COLS)
    im = im.reshape(HALF, SLOTS, COLS)
    cos = twist_ref[0, :HALF][:, None, :]
    sin = twist_ref[1, :HALF][:, None, :]
    out_re = (re * cos + im * sin).reshape(HALF * SLOTS, COLS)
    out_im = (im * cos - re * sin).reshape(HALF * SLOTS, COLS)
    return out_re, out_im


def smoothed(power):
    power = power.reshape(HALF, SLOTS, COLS)
    lane = lax.broadcasted_iota(jnp.int32, (SLOTS, COLS), 1)
    below, above = (COLS - lane) % COLS, COLS - 1 - lane

    def mirrored(row, index):
        return jnp.take_along_axis(power[row], index, axis=1)[None]

    even = jnp.concatenate(
        [mirrored(1, below), power[:EVEN], mirrored(EVEN - 2, above)], axis=0
    )
    odd = jnp.concatenate(
        [mirrored(EVEN, below), power[EVEN:], mirrored(HALF - 1, above)], axis=0
    )
    pairs_even = even[:-1] + even[1:]
    pairs_odd = odd[:-1] + odd[1:]
    smooth_even = (pairs_even[:-1] + even[2:]) + pairs_odd
    smooth_odd = (pairs_odd[:-1] + odd[2:]) + pairs_even[1:-1]
    return jnp.concatenate([smooth_even, smooth_odd], axis=0).reshape(HALF * SLOTS, COLS)


def placed(value, index):
    rows = value.shape[0] // SLOTS
    value = value.reshape(rows, SLOTS, COLS)
    index = jnp.broadcast_to(index[None], value.shape)
    return jnp.take_along_axis(value, index, axis=1).reshape(rows * SLOTS, COLS)


def in_order(rows_ref):
    mine = lax.axis_index("tm")
    windows = lax.axis_size("tm")
    return [rows_ref[jnp.bitwise_xor(mine, j)] for j in range(windows)]


def whitened(halves, tables_ref, twist_ref):
    windows = len(halves)
    size, evens = HALF * SLOTS, EVEN * SLOTS
    grid_re, grid_im = first_stage(halves[0::2], halves[1::2], tables_ref)
    front = lax.broadcasted_iota(jnp.int32, (HALF, SLOTS, COLS), 1) < SLOTS // 2

    def rolled(value):
        return pltpu.roll(value.reshape(HALF, SLOTS, COLS), SLOTS // 2, axis=1)

    turn = (table_slice(tables_ref, 2), table_slice(tables_ref, 3))
    packs = []
    power = 0.0
    later = None
    for g in reversed(range(windows // 2)):
        cols = slice(g * COLS, (g + 1) * COLS)
        here = twisted(grid_re[:, cols], grid_im[:, cols], twist_ref)
        turned = [rolled(part) for part in here]
        value = []
        for i in range(2):
            follow = 0.0 if later is None else later[i]
            follow = jnp.where(front, turned[i], follow).reshape(size, COLS)
            value.append(
                jnp.concatenate(
                    [here[i][:evens] + follow[:evens], here[i][evens:] - follow[evens:]], axis=0
                )
            )
        later = turned
        re, im = transformed(*value, turn)
        power = power + (re * re + im * im)
        packs.insert(0, (re, im))
    power = power + rolled(power).reshape(size, COLS)
    root = lax.rsqrt(smoothed(power) * (1.0 / (5 * windows)) + SMALL)
    return [(re * root, im * root) for re, im in packs], power, root


def pair_slots(share):
    pair = lax.axis_index("tm") * share + lax.broadcasted_iota(jnp.int32, (SLOTS, COLS), 0)
    count = SLOTS // 2
    return jnp.minimum(pair // count, count - 1), pair % count


def fetch_kernel(share, number, sizes_hbm, tables_hbm, twist_hbm, tables_ref, twist_ref, live_ref, sizes_ref, sems):
    fetches = [
        pltpu.make_async_copy(tables_hbm, tables_ref, sems.at[0]),
        pltpu.make_async_copy(twist_hbm, twist_ref, sems.at[1]),
        pltpu.make_async_copy(sizes_hbm, sizes_ref, sems.at[2]),
    ]
    for fetch in fetches:
        fetch.start()
    for fetch in fetches:
        fetch.wait()
    slot, far_slot = pair_slots(share)
    block = lax.axis_index("stn")
    other = jnp.bitwise_xor(block, number)
    places = lax.broadcasted_iota(jnp.int32, sizes_ref.shape, 1)
    sizes = sizes_ref[...]
    live_near = jnp.sum(jnp.where(places == block, sizes, 0), axis=1, keepdims=True)
    live_far = jnp.sum(jnp.where(places == other, sizes, 0), axis=1, keepdims=True)
    live_ref[...] = ((slot < live_near) & (far_slot < live_far)).astype(F32)


def near_kernel(share, rows_ref, tables_ref, twist_ref, near_ref, keep_ref):
    windows = rows_ref.shape[0]
    slot, _ = pair_slots(share)
    packs, power, root = whitened(in_order(rows_ref), tables_ref, twist_ref)
    for g, pack in enumerate(packs):
        for h in range(2):
            for i in range(2):
                near_ref[2 * g + h, i] = placed(pack[i], slot + h * (SLOTS // 2))
    by_row = (power * (root * root)).reshape(HALF, SLOTS, COLS)
    total = 2.0 * jnp.sum(by_row, axis=0) - by_row[0] - by_row[EVEN - 1]
    mean = jnp.sum(total, axis=1, keepdims=True) * (1.0 / PERIOD)
    scale = 1.0 / (mean + SMALL)
    keep = (1.0 - by_row * scale[None]).reshape(HALF * SLOTS, COLS)
    keep_ref[...] = placed(keep, slot)


def far_kernel(
    rows_ref, near_ref, keep_ref, live_ref, tables_ref, twist_ref, plain_ref, refined_ref
):
    windows = near_ref.shape[0]
    share = plain_ref.shape[0]
    _, far_slot = pair_slots(share)
    evens = EVEN * SLOTS
    packs, _, _ = whitened(in_order(rows_ref), tables_ref, twist_ref)
    re = im = 0.0
    for g, pack in enumerate(packs):
        for h in range(2):
            index = far_slot + h * (SLOTS // 2)
            far_re, far_im = placed(pack[0], index), placed(pack[1], index)
            near_re, near_im = near_ref[2 * g + h, 0], near_ref[2 * g + h, 1]
            re = re + (near_re * far_re + near_im * far_im)
            im = im + (near_im * far_re - near_re * far_im)
    keep, live = keep_ref[...], live_ref[...]
    turn = (table_slice(tables_ref, 2), table_slice(tables_ref, 3))
    halves = []
    for value_re, value_im in ((re, im), (re * keep, im * keep)):
        half = transformed(value_re, value_im, turn)
        halves.append(twisted(*half, twist_ref))
    half_re = jnp.concatenate([halves[0][0], halves[1][0]], axis=1)
    half_im = jnp.concatenate([halves[0][1], halves[1][1]], axis=1)
    edge = evens - SLOTS
    middle = half_re[edge:evens] * (1.0 / math.sqrt(PERIOD * windows))
    same = jnp.concatenate([half_re[:edge], half_im[evens:]], axis=0)
    turned = jnp.concatenate([half_re[evens:], half_im[:edge]], axis=0)
    same = dot_split((table_slice(tables_ref, 4), table_slice(tables_ref, 6)), split(same))
    turned = dot_split((table_slice(tables_ref, 5), table_slice(tables_ref, 7)), split(turned))

    for j in range(EVEN):
        rows = slice(j * SLOTS, (j + 1) * SLOTS)
        steady = same[rows] + (middle if j % 2 == 0 else -middle)
        mirrored = [(2 * ODD - j, steady - turned[rows])] if 0 < j < ODD else []
        for lag, here in [(j, steady + turned[rows])] + mirrored:
            cols = slice(lag * COLS, (lag + 1) * COLS)
            plain_ref[:, cols] = (here[:, :COLS] * live)[:share]
            refined_ref[:, cols] = (here[:, COLS:] * live)[:share]


def per_device(samples, array_sizes, partner):
    count = samples.shape[0]
    groups = lax.axis_size("tm")
    blocks = lax.axis_size("stn")
    share = count * count // groups
    vmem = pl.BlockSpec(memory_space=pltpu.VMEM)
    params = pltpu.CompilerParams(vmem_limit_bytes=32 * 1024 * 1024)
    rows = samples.reshape(count, LAGS // COLS, COLS).transpose(1, 0, 2).reshape(-1, COLS)

    def to_fast_memory(value):
        return lax.ppermute(value, "tm", [(i, i) for i in range(groups)])

    own = to_fast_memory(rows)

    def with_others(value):
        return [value] + [
            lax.ppermute(value, "tm", [(i, i ^ step) for i in range(groups)])
            for step in range(1, groups)
        ]

    def fast(shape, kind=F32):
        return jax.ShapeDtypeStruct(shape, kind)

    early = groups == 2

    def own_stations(own, tables, twist):
        return pl.pallas_call(
            functools.partial(near_kernel, share),
            out_shape=(
                fast((groups, 2, HALF * SLOTS, COLS)), fast((HALF * SLOTS, COLS))
            ),
            in_specs=[vmem] * 3,
            out_specs=(vmem,) * 2,
            compiler_params=params,
        )(jnp.stack(with_others(own)), tables, twist)

    def exchanged(number, own, sizes, tables, twist):
        far = lax.ppermute(own, "stn", [(i, i ^ number) for i in range(blocks)])
        fetched = pl.pallas_call(
            functools.partial(fetch_kernel, share, number),
            out_shape=(fast(tables.shape, BF16), fast(twist.shape), fast((SLOTS, COLS))),
            in_specs=[pl.BlockSpec(memory_space=pltpu.HBM)] * 3,
            out_specs=(vmem,) * 3,
            scratch_shapes=[
                pltpu.VMEM(sizes.shape, sizes.dtype), pltpu.SemaphoreType.DMA((3,))
            ],
            compiler_params=params,
        )(*(pltpu.with_memory_space_constraint(v, pltpu.HBM) for v in (sizes, tables, twist)))
        far, (tables, twist, live) = lax.optimization_barrier((far, fetched))
        mine = own_stations(own, tables, twist) if early else (tables, twist)
        return jnp.stack(with_others(far)), live, *mine

    near_tables, near_twist, far_tables, far_twist = tables(count, groups)
    both, live, *mine = lax.switch(
        partner[0] - 1,
        [functools.partial(exchanged, number) for number in range(1, blocks)],
        own, array_sizes[None], jnp.asarray(near_tables), jnp.asarray(near_twist),
    )
    near, keep = mine if early else own_stations(own, *mine)
    out = fast((share, LAGS))
    return pl.pallas_call(
        far_kernel,
        out_shape=(out, out),
        in_specs=[vmem] * 6,
        out_specs=(vmem, vmem),
        compiler_params=params,
    )(both, near, keep, live, far_tables, far_twist)


def solution(mesh):
    placed = (P("stn", "tm"), P(), P())
    return jax.shard_map(
        per_device,
        mesh=mesh,
        in_specs=placed,
        out_specs=(P(("stn", "tm"), None), P(("stn", "tm"), None)),
        check_vma=False,
    )
```

```python
import functools
import math

import jax
import jax.numpy as jnp
import numpy as np
from jax import lax
from jax.experimental import pallas as pl
from jax.experimental.pallas import tpu as pltpu
from jax.sharding import PartitionSpec as P

LAGS = 4096
PERIOD = 2 * LAGS
ROWS = 64
COLS = 128
EVEN = ROWS // 4 + 1
ODD = ROWS // 4
HALF = EVEN + ODD
SLOTS = 8
SMALL = 1e-06
F32 = jnp.float32
BF16 = jnp.bfloat16


def split_table(table):
    high = table.astype(np.float32).astype(jnp.bfloat16)
    low = (table - high.astype(np.float64)).astype(np.float32).astype(jnp.bfloat16)
    return np.stack([high, low])


@functools.lru_cache(maxsize=None)
def tables(count, windows):
    f1 = np.concatenate([np.arange(0, ROWS // 2 + 1, 2), np.arange(1, ROWS // 2, 2)])
    lag = np.arange(LAGS // COLS)
    angle = 2 * np.pi * ((f1[:, None] * lag[None, :]) % ROWS) / ROWS
    half = ODD // 2
    base = np.concatenate([np.arange(half + 1), np.arange(EVEN, EVEN + half)])
    first = []
    for parity in range(2):
        kept = angle[base, parity::2]
        part = np.concatenate([np.cos(kept), -np.sin(kept[1:])])
        part = part[:, None, :, None] * np.eye(SLOTS)[None, :, None, :]
        first.append(np.concatenate(list(split_table(part.reshape(-1, COLS))), axis=1))
    first = np.stack(first)
    n2 = np.arange(COLS)
    twist = 2 * np.pi * ((f1[:, None] * n2[None, :]) % PERIOD) / PERIOD
    twist = np.stack([np.cos(twist), np.sin(twist)]).astype(np.float32)
    turn = 2 * np.pi * ((n2[:, None] * n2[None, :]) % COLS) / COLS
    cos, sin = np.cos(turn), np.sin(turn)
    second = split_table(np.block([[cos, -sin], [sin, cos]]))
    weight = np.where(f1 % (ROWS // 2) == 0, 1.0, 2.0)[:, None] / math.sqrt(PERIOD * windows)
    cos, sin = (np.cos(angle) * weight)[:, :EVEN].T, (np.sin(angle) * weight)[:, :EVEN].T
    same = np.concatenate([cos[:, : EVEN - 1], sin[:, EVEN:]], axis=1)
    turned = np.concatenate([cos[:, EVEN:], sin[:, : EVEN - 1]], axis=1)
    last = np.stack([np.kron(same, np.eye(SLOTS)), np.kron(turned, np.eye(SLOTS))])
    last = split_table(last).reshape(4, EVEN * SLOTS, 2 * COLS)

    def padded(table):
        extra = -table.shape[1] % 16
        return np.pad(table, ((0, 0), (0, extra), (0, 0))).reshape(-1, 2 * COLS)

    near = np.concatenate([padded(first), second[0], second[1]])
    far_twist = np.pad(twist, ((0, 0), (0, -HALF % SLOTS), (0, 0)))
    return near, twist, np.concatenate([near, padded(last)]), far_twist


def table_slice(ref, which):
    rows = -(-HALF * SLOTS // 16) * 16
    if which < 2:
        return ref[which * rows : which * rows + HALF * SLOTS]
    start = 2 * rows + (which - 2) * 2 * COLS
    if which < 4:
        return ref[start : start + 2 * COLS]
    rows = -(-EVEN * SLOTS // 16) * 16
    start = 2 * -(-HALF * SLOTS // 16) * 16 + 4 * COLS + (which - 4) * rows
    return ref[start : start + EVEN * SLOTS]


def dot(left, right):
    return jnp.dot(left, right, preferred_element_type=F32)


def split(value):
    high = value.astype(BF16)
    return high, (value - high.astype(F32)).astype(BF16)


def dot_split(left, right):
    rows = left[0].shape[0]
    both = dot(jnp.concatenate(left, axis=0), right[0])
    return both[:rows] + (both[rows:] + dot(left[0], right[1]))


def transformed(re, im, table):
    out = dot_split(split(jnp.concatenate([re, im], axis=1)), table)
    return out[:, :COLS], out[:, COLS:]


def first_stage(lower, upper, tables_ref):
    def joined(a, b):
        a = a.astype(F32).reshape(ODD, SLOTS, COLS)
        b = b.astype(F32).reshape(ODD, SLOTS, COLS)
        front = lax.broadcasted_iota(jnp.int32, a.shape, 1) < SLOTS // 2
        even = jnp.where(front, a, pltpu.roll(b, SLOTS // 2, axis=1))
        odd = jnp.where(front, pltpu.roll(a, SLOTS // 2, axis=1), b)
        return [part.reshape(ODD * SLOTS, COLS).astype(BF16) for part in (even, odd)]

    parts = [joined(a, b) for a, b in zip(lower, upper)]
    sums = []
    for parity in range(2):
        held = jnp.concatenate([part[parity] for part in parts], axis=1)
        sums.append(dot(table_slice(tables_ref, parity), jnp.concatenate([held, held], axis=0)))
    plus, minus = sums[0] + sums[1], sums[0] - sums[1]
    half = ODD // 2

    def group(value, i):
        return value[i * SLOTS : (i + 1) * SLOTS]

    none = jnp.zeros_like(group(plus, 0))
    back = list(range(half - 1, -1, -1))
    re = [group(plus, i) for i in range(half + 1)] + [group(minus, i) for i in back]
    re += [group(plus, half + 1 + i) for i in range(half)]
    re += [group(minus, half + 1 + i) for i in back]
    at = 2 * half + 1
    im = [none] + [group(plus, at + i) for i in range(half)]
    im += [-group(minus, at + i) for i in back[1:]] + [none]
    im += [group(plus, at + half + i) for i in range(half)]
    im += [-group(minus, at + half + i) for i in back]
    return jnp.concatenate(re, axis=0), jnp.concatenate(im, axis=0)


def twisted(re, im, twist_ref):
    re = re.reshape(HALF, SLOTS, COLS)
    im = im.reshape(HALF, SLOTS, COLS)
    cos = twist_ref[0, :HALF][:, None, :]
    sin = twist_ref[1, :HALF][:, None, :]
    out_re = (re * cos + im * sin).reshape(HALF * SLOTS, COLS)
    out_im = (im * cos - re * sin).reshape(HALF * SLOTS, COLS)
    return out_re, out_im


def smoothed(power):
    power = power.reshape(HALF, SLOTS, COLS)
    lane = lax.broadcasted_iota(jnp.int32, (SLOTS, COLS), 1)
    below, above = (COLS - lane) % COLS, COLS - 1 - lane

    def mirrored(row, index):
        return jnp.take_along_axis(power[row], index, axis=1)[None]

    even = jnp.concatenate(
        [mirrored(1, below), power[:EVEN], mirrored(EVEN - 2, above)], axis=0
    )
    odd = jnp.concatenate(
        [mirrored(EVEN, below), power[EVEN:], mirrored(HALF - 1, above)], axis=0
    )
    pairs_even = even[:-1] + even[1:]
    pairs_odd = odd[:-1] + odd[1:]
    smooth_even = (pairs_even[:-1] + even[2:]) + pairs_odd
    smooth_odd = (pairs_odd[:-1] + odd[2:]) + pairs_even[1:-1]
    return jnp.concatenate([smooth_even, smooth_odd], axis=0).reshape(HALF * SLOTS, COLS)


def placed(value, index):
    rows = value.shape[0] // SLOTS
    value = value.reshape(rows, SLOTS, COLS)
    index = jnp.broadcast_to(index[None], value.shape)
    return jnp.take_along_axis(value, index, axis=1).reshape(rows * SLOTS, COLS)


def in_order(rows_ref):
    mine = lax.axis_index("tm")
    windows = lax.axis_size("tm")
    return [rows_ref[jnp.bitwise_xor(mine, j)] for j in range(windows)]


def whitened(halves, tables_ref, twist_ref):
    windows = len(halves)
    size, evens = HALF * SLOTS, EVEN * SLOTS
    grid_re, grid_im = first_stage(halves[0::2], halves[1::2], tables_ref)
    front = lax.broadcasted_iota(jnp.int32, (HALF, SLOTS, COLS), 1) < SLOTS // 2

    def rolled(value):
        return pltpu.roll(value.reshape(HALF, SLOTS, COLS), SLOTS // 2, axis=1)

    turn = (table_slice(tables_ref, 2), table_slice(tables_ref, 3))
    packs = []
    power = 0.0
    later = None
    for g in reversed(range(windows // 2)):
        cols = slice(g * COLS, (g + 1) * COLS)
        here = twisted(grid_re[:, cols], grid_im[:, cols], twist_ref)
        turned = [rolled(part) for part in here]
        value = []
        for i in range(2):
            follow = 0.0 if later is None else later[i]
            follow = jnp.where(front, turned[i], follow).reshape(size, COLS)
            value.append(
                jnp.concatenate(
                    [here[i][:evens] + follow[:evens], here[i][evens:] - follow[evens:]], axis=0
                )
            )
        later = turned
        re, im = transformed(*value, turn)
        power = power + (re * re + im * im)
        packs.insert(0, (re, im))
    power = power + rolled(power).reshape(size, COLS)
    root = lax.rsqrt(smoothed(power) * (1.0 / (5 * windows)) + SMALL)
    return [(re * root, im * root) for re, im in packs], power, root


def pair_slots(share):
    pair = lax.axis_index("tm") * share + lax.broadcasted_iota(jnp.int32, (SLOTS, COLS), 0)
    count = SLOTS // 2
    return jnp.minimum(pair // count, count - 1), pair % count


def fetch_kernel(share, number, sizes_hbm, tables_hbm, twist_hbm, tables_ref, twist_ref, live_ref, sizes_ref, sems):
    fetches = [
        pltpu.make_async_copy(tables_hbm, tables_ref, sems.at[0]),
        pltpu.make_async_copy(twist_hbm, twist_ref, sems.at[1]),
        pltpu.make_async_copy(sizes_hbm, sizes_ref, sems.at[2]),
    ]
    for fetch in fetches:
        fetch.start()
    for fetch in fetches:
        fetch.wait()
    slot, far_slot = pair_slots(share)
    block = lax.axis_index("stn")
    other = jnp.bitwise_xor(block, number)
    places = lax.broadcasted_iota(jnp.int32, sizes_ref.shape, 1)
    sizes = sizes_ref[...]
    live_near = jnp.sum(jnp.where(places == block, sizes, 0), axis=1, keepdims=True)
    live_far = jnp.sum(jnp.where(places == other, sizes, 0), axis=1, keepdims=True)
    live_ref[...] = ((slot < live_near) & (far_slot < live_far)).astype(F32)


def near_kernel(share, rows_ref, tables_ref, twist_ref, live_ref, near_ref, keep_ref):
    windows = rows_ref.shape[0]
    slot, _ = pair_slots(share)
    packs, power, root = whitened(in_order(rows_ref), tables_ref, twist_ref)
    live = live_ref[...][None]
    for g, pack in enumerate(packs):
        for h in range(2):
            for i in range(2):
                value = placed(pack[i], slot + h * (SLOTS // 2))
                value = value.reshape(HALF, SLOTS, COLS) * live
                near_ref[2 * g + h, i] = value.reshape(HALF * SLOTS, COLS)
    by_row = (power * (root * root)).reshape(HALF, SLOTS, COLS)
    total = 2.0 * jnp.sum(by_row, axis=0) - by_row[0] - by_row[EVEN - 1]
    mean = jnp.sum(total, axis=1, keepdims=True) * (1.0 / PERIOD)
    scale = 1.0 / (mean + SMALL)
    keep = (1.0 - by_row * scale[None]).reshape(HALF * SLOTS, COLS)
    keep_ref[...] = placed(keep, slot)


def far_kernel(rows_ref, near_ref, keep_ref, tables_ref, twist_ref, plain_ref, refined_ref):
    windows = near_ref.shape[0]
    share = plain_ref.shape[0]
    _, far_slot = pair_slots(share)
    evens = EVEN * SLOTS
    packs, _, _ = whitened(in_order(rows_ref), tables_ref, twist_ref)
    re = im = 0.0
    for g, pack in enumerate(packs):
        for h in range(2):
            index = far_slot + h * (SLOTS // 2)
            far_re, far_im = placed(pack[0], index), placed(pack[1], index)
            near_re, near_im = near_ref[2 * g + h, 0], near_ref[2 * g + h, 1]
            re = re + (near_re * far_re + near_im * far_im)
            im = im + (near_im * far_re - near_re * far_im)
    keep = keep_ref[...]
    turn = (table_slice(tables_ref, 2), table_slice(tables_ref, 3))
    halves = []
    for value_re, value_im in ((re, im), (re * keep, im * keep)):
        half = transformed(value_re, value_im, turn)
        halves.append(twisted(*half, twist_ref))
    half_re = jnp.concatenate([halves[0][0], halves[1][0]], axis=1)
    half_im = jnp.concatenate([halves[0][1], halves[1][1]], axis=1)
    edge = evens - SLOTS
    middle = half_re[edge:evens] * (1.0 / math.sqrt(PERIOD * windows))
    same = jnp.concatenate([half_re[:edge], half_im[evens:]], axis=0)
    turned = jnp.concatenate([half_re[evens:], half_im[:edge]], axis=0)
    same = dot_split((table_slice(tables_ref, 4), table_slice(tables_ref, 6)), split(same))
    turned = dot_split((table_slice(tables_ref, 5), table_slice(tables_ref, 7)), split(turned))

    for j in range(EVEN):
        rows = slice(j * SLOTS, (j + 1) * SLOTS)
        steady = same[rows] + (middle if j % 2 == 0 else -middle)
        mirrored = [(2 * ODD - j, steady - turned[rows])] if 0 < j < ODD else []
        for lag, here in [(j, steady + turned[rows])] + mirrored:
            cols = slice(lag * COLS, (lag + 1) * COLS)
            plain_ref[:, cols] = here[:share, :COLS]
            refined_ref[:, cols] = here[:share, COLS:]


def per_device(samples, array_sizes, partner):
    count = samples.shape[0]
    groups = lax.axis_size("tm")
    blocks = lax.axis_size("stn")
    share = count * count // groups
    vmem = pl.BlockSpec(memory_space=pltpu.VMEM)
    params = pltpu.CompilerParams(vmem_limit_bytes=32 * 1024 * 1024)
    rows = samples.reshape(count, LAGS // COLS, COLS).transpose(1, 0, 2).reshape(-1, COLS)

    def to_fast_memory(value):
        return lax.ppermute(value, "tm", [(i, i) for i in range(groups)])

    own = to_fast_memory(rows)

    def with_others(value):
        return [value] + [
            lax.ppermute(value, "tm", [(i, i ^ step) for i in range(groups)])
            for step in range(1, groups)
        ]

    def fast(shape, kind=F32):
        return jax.ShapeDtypeStruct(shape, kind)

    early = groups == 2

    def own_stations(own, tables, twist, live):
        return pl.pallas_call(
            functools.partial(near_kernel, share),
            out_shape=(
                fast((groups, 2, HALF * SLOTS, COLS)), fast((HALF * SLOTS, COLS))
            ),
            in_specs=[vmem] * 4,
            out_specs=(vmem,) * 2,
            compiler_params=params,
        )(jnp.stack(with_others(own)), tables, twist, live)

    def exchanged(number, own, sizes, tables, twist):
        far = lax.ppermute(own, "stn", [(i, i ^ number) for i in range(blocks)])
        fetched = pl.pallas_call(
            functools.partial(fetch_kernel, share, number),
            out_shape=(fast(tables.shape, BF16), fast(twist.shape), fast((SLOTS, COLS))),
            in_specs=[pl.BlockSpec(memory_space=pltpu.HBM)] * 3,
            out_specs=(vmem,) * 3,
            scratch_shapes=[
                pltpu.VMEM(sizes.shape, sizes.dtype), pltpu.SemaphoreType.DMA((3,))
            ],
            compiler_params=params,
        )(*(pltpu.with_memory_space_constraint(v, pltpu.HBM) for v in (sizes, tables, twist)))
        far, fetched = lax.optimization_barrier((far, fetched))
        mine = own_stations(own, *fetched) if early else fetched
        return jnp.stack(with_others(far)), *mine

    near_tables, near_twist, far_tables, far_twist = tables(count, groups)
    both, *mine = lax.switch(
        partner[0] - 1,
        [functools.partial(exchanged, number) for number in range(1, blocks)],
        own, array_sizes[None], jnp.asarray(near_tables), jnp.asarray(near_twist),
    )
    near, keep = mine if early else own_stations(own, *mine)
    out = fast((share, LAGS))
    return pl.pallas_call(
        far_kernel,
        out_shape=(out, out),
        in_specs=[vmem] * 5,
        out_specs=(vmem, vmem),
        compiler_params=params,
    )(both, near, keep, far_tables, far_twist)


def solution(mesh):
    placed = (P("stn", "tm"), P(), P())
    return jax.shard_map(
        per_device,
        mesh=mesh,
        in_specs=placed,
        out_specs=(P(("stn", "tm"), None), P(("stn", "tm"), None)),
        check_vma=False,
    )
```

```python
import functools
import math

import jax
import jax.numpy as jnp
import numpy as np
from jax import lax
from jax.experimental import pallas as pl
from jax.experimental.pallas import tpu as pltpu
from jax.sharding import PartitionSpec as P

LAGS = 4096
PERIOD = 2 * LAGS
ROWS = 64
COLS = 128
EVEN = ROWS // 4 + 1
ODD = ROWS // 4
HALF = EVEN + ODD
FOLD = COLS // 2
SLOTS = 8
SMALL = 1e-06
F32 = jnp.float32
BF16 = jnp.bfloat16


def split_table(table):
    high = table.astype(np.float32).astype(jnp.bfloat16)
    low = (table - high.astype(np.float64)).astype(np.float32).astype(jnp.bfloat16)
    return np.stack([high, low])


@functools.lru_cache(maxsize=None)
def tables(count, windows):
    f1 = np.concatenate([np.arange(0, ROWS // 2 + 1, 2), np.arange(1, ROWS // 2, 2)])
    lag = np.arange(LAGS // COLS)
    angle = 2 * np.pi * ((f1[:, None] * lag[None, :]) % ROWS) / ROWS
    half = ODD // 2
    base = np.concatenate([np.arange(half + 1), np.arange(EVEN, EVEN + half)])
    first = []
    for parity in range(2):
        kept = angle[base, parity::2]
        part = np.concatenate([np.cos(kept), -np.sin(kept[1:])])
        part = part[:, None, :, None] * np.eye(SLOTS)[None, :, None, :]
        first.append(np.concatenate(list(split_table(part.reshape(-1, COLS))), axis=1))
    first = np.stack(first)
    n2 = np.arange(COLS)
    twist = 2 * np.pi * ((f1[:, None] * n2[None, :]) % PERIOD) / PERIOD
    twist = np.stack([np.cos(twist), np.sin(twist)]).astype(np.float32)
    turn = 2 * np.pi * ((n2[:, None] * n2[None, :]) % COLS) / COLS
    cos, sin = np.cos(turn), np.sin(turn)
    order = np.where(n2 > FOLD, COLS + FOLD - n2, n2)
    pairs = np.concatenate([order, COLS + order])
    inverse = split_table(np.block([[cos, -sin], [sin, cos]])[pairs])
    folded = np.where(n2 > FOLD, n2 - FOLD, n2)
    table = np.where(n2[None, :] > FOLD, sin[:, folded], cos[:, folded])
    high, low = split_table(table)
    rest = (table - high.astype(np.float64) - low.astype(np.float64)).astype(np.float32)
    rest = np.pad(rest.astype(jnp.bfloat16), ((0, 0), (0, COLS)))
    second = np.concatenate([high, low], axis=1), rest
    weight = np.where(f1 % (ROWS // 2) == 0, 1.0, 2.0)[:, None] / math.sqrt(PERIOD * windows)
    cos, sin = (np.cos(angle) * weight)[:, :EVEN].T, (np.sin(angle) * weight)[:, :EVEN].T
    same = np.concatenate([cos[:, : EVEN - 1], sin[:, EVEN:]], axis=1)
    turned = np.concatenate([cos[:, EVEN:], sin[:, : EVEN - 1]], axis=1)
    last = np.stack([np.kron(same, np.eye(SLOTS)), np.kron(turned, np.eye(SLOTS))])
    last = split_table(last).reshape(4, EVEN * SLOTS, 2 * COLS)

    def padded(table):
        extra = -table.shape[1] % 16
        return np.pad(table, ((0, 0), (0, extra), (0, 0))).reshape(-1, 2 * COLS)

    near = np.concatenate([padded(first), second[0], second[1]])
    far_twist = np.pad(twist, ((0, 0), (0, -HALF % SLOTS), (0, 0)))
    far = np.concatenate([near, inverse[0], inverse[1], padded(last)])
    return near, twist, far, far_twist


def table_slice(ref, which):
    rows = -(-HALF * SLOTS // 16) * 16
    if which < 2:
        return ref[which * rows : which * rows + HALF * SLOTS]
    start = 2 * rows + (which - 2) * 2 * COLS
    if which < 5:
        return ref[start : start + 2 * COLS]
    start = 2 * rows + 6 * COLS
    rows = -(-EVEN * SLOTS // 16) * 16
    start += (which - 5) * rows
    return ref[start : start + EVEN * SLOTS]


def dot(left, right):
    return jnp.dot(left, right, preferred_element_type=F32)


def split(value):
    high = value.astype(BF16)
    return high, (value - high.astype(F32)).astype(BF16)


def dot_split(left, right):
    rows = left[0].shape[0]
    both = dot(jnp.concatenate(left, axis=0), right[0])
    return both[:rows] + (both[rows:] + dot(left[0], right[1]))


def transformed(re, im, table):
    rows = re.shape[0]
    value = jnp.concatenate([re, im], axis=0)
    high = value.astype(BF16)
    value = value - high.astype(F32)
    middle = value.astype(BF16)
    low = (value - middle.astype(F32)).astype(BF16)
    main, rest = table[:COLS], table[COLS:, :COLS]
    out = dot(jnp.concatenate([high, middle], axis=1), jnp.concatenate([main, main], axis=0))
    rest = jnp.concatenate([main[:, :COLS], rest], axis=0)
    small = dot(jnp.concatenate([low, high], axis=1), rest)
    out = out[:, :COLS] + (out[:, COLS:] + small)
    re, im = out[:rows], out[rows:]
    lane = lax.broadcasted_iota(jnp.int32, (rows, COLS), 1)
    lower, upper = (lane > 0) & (lane < FOLD), lane > FOLD
    far_re, far_im = pltpu.roll(re, FOLD, axis=1), pltpu.roll(im, FOLD, axis=1)
    out_re = jnp.where(upper, far_re - im, re + jnp.where(lower, far_im, 0.0))
    out_im = jnp.where(upper, far_im + re, im - jnp.where(lower, far_re, 0.0))
    return out_re, out_im


def transformed_back(re, im, table):
    out = dot_split(split(jnp.concatenate([re, im], axis=1)), table)
    return out[:, :COLS], out[:, COLS:]


def first_stage(lower, upper, tables_ref):
    def joined(a, b):
        a = a.astype(F32).reshape(ODD, SLOTS, COLS)
        b = b.astype(F32).reshape(ODD, SLOTS, COLS)
        front = lax.broadcasted_iota(jnp.int32, a.shape, 1) < SLOTS // 2
        even = jnp.where(front, a, pltpu.roll(b, SLOTS // 2, axis=1))
        odd = jnp.where(front, pltpu.roll(a, SLOTS // 2, axis=1), b)
        return [part.reshape(ODD * SLOTS, COLS).astype(BF16) for part in (even, odd)]

    parts = [joined(a, b) for a, b in zip(lower, upper)]
    sums = []
    for parity in range(2):
        held = jnp.concatenate([part[parity] for part in parts], axis=1)
        sums.append(dot(table_slice(tables_ref, parity), jnp.concatenate([held, held], axis=0)))
    plus, minus = sums[0] + sums[1], sums[0] - sums[1]
    half = ODD // 2

    def group(value, i):
        return value[i * SLOTS : (i + 1) * SLOTS]

    none = jnp.zeros_like(group(plus, 0))
    back = list(range(half - 1, -1, -1))
    re = [group(plus, i) for i in range(half + 1)] + [group(minus, i) for i in back]
    re += [group(plus, half + 1 + i) for i in range(half)]
    re += [group(minus, half + 1 + i) for i in back]
    at = 2 * half + 1
    im = [none] + [group(plus, at + i) for i in range(half)]
    im += [-group(minus, at + i) for i in back[1:]] + [none]
    im += [group(plus, at + half + i) for i in range(half)]
    im += [-group(minus, at + half + i) for i in back]
    return jnp.concatenate(re, axis=0), jnp.concatenate(im, axis=0)


def twisted(re, im, twist_ref):
    re = re.reshape(HALF, SLOTS, COLS)
    im = im.reshape(HALF, SLOTS, COLS)
    cos = twist_ref[0, :HALF][:, None, :]
    sin = twist_ref[1, :HALF][:, None, :]
    out_re = (re * cos + im * sin).reshape(HALF * SLOTS, COLS)
    out_im = (im * cos - re * sin).reshape(HALF * SLOTS, COLS)
    return out_re, out_im


def smoothed(power):
    power = power.reshape(HALF, SLOTS, COLS)
    lane = lax.broadcasted_iota(jnp.int32, (SLOTS, COLS), 1)
    below = jnp.where(lane % FOLD == 0, lane, (lane + FOLD) % COLS)
    above = jnp.where(lane < FOLD, lane + FOLD + 1, lane - FOLD - 1)
    above = jnp.where(lane == FOLD - 1, FOLD, jnp.where(lane == FOLD, FOLD - 1, above))

    def mirrored(row, index):
        return jnp.take_along_axis(power[row], index, axis=1)[None]

    even = jnp.concatenate(
        [mirrored(1, below), power[:EVEN], mirrored(EVEN - 2, above)], axis=0
    )
    odd = jnp.concatenate(
        [mirrored(EVEN, below), power[EVEN:], mirrored(HALF - 1, above)], axis=0
    )
    pairs_even = even[:-1] + even[1:]
    pairs_odd = odd[:-1] + odd[1:]
    smooth_even = (pairs_even[:-1] + even[2:]) + pairs_odd
    smooth_odd = (pairs_odd[:-1] + odd[2:]) + pairs_even[1:-1]
    return jnp.concatenate([smooth_even, smooth_odd], axis=0).reshape(HALF * SLOTS, COLS)


def placed(value, index):
    rows = value.shape[0] // SLOTS
    value = value.reshape(rows, SLOTS, COLS)
    index = jnp.broadcast_to(index[None], value.shape)
    return jnp.take_along_axis(value, index, axis=1).reshape(rows * SLOTS, COLS)


def in_order(rows_ref):
    mine = lax.axis_index("tm")
    windows = lax.axis_size("tm")
    return [rows_ref[jnp.bitwise_xor(mine, j)] for j in range(windows)]


def whitened(halves, tables_ref, twist_ref):
    windows = len(halves)
    size, evens = HALF * SLOTS, EVEN * SLOTS
    grid_re, grid_im = first_stage(halves[0::2], halves[1::2], tables_ref)
    front = lax.broadcasted_iota(jnp.int32, (HALF, SLOTS, COLS), 1) < SLOTS // 2

    def rolled(value):
        return pltpu.roll(value.reshape(HALF, SLOTS, COLS), SLOTS // 2, axis=1)

    forth = table_slice(tables_ref, 2)
    packs = []
    power = 0.0
    later = None
    for g in reversed(range(windows // 2)):
        cols = slice(g * COLS, (g + 1) * COLS)
        here = twisted(grid_re[:, cols], grid_im[:, cols], twist_ref)
        turned = [rolled(part) for part in here]
        value = []
        for i in range(2):
            follow = 0.0 if later is None else later[i]
            follow = jnp.where(front, turned[i], follow).reshape(size, COLS)
            value.append(
                jnp.concatenate(
                    [here[i][:evens] + follow[:evens], here[i][evens:] - follow[evens:]], axis=0
                )
            )
        later = turned
        re, im = transformed(*value, forth)
        power = power + (re * re + im * im)
        packs.insert(0, (re, im))
    power = power + rolled(power).reshape(size, COLS)
    root = lax.rsqrt(smoothed(power) * (1.0 / (5 * windows)) + SMALL)
    return [(re * root, im * root) for re, im in packs], power, root


def pair_slots(share):
    pair = lax.axis_index("tm") * share + lax.broadcasted_iota(jnp.int32, (SLOTS, COLS), 0)
    count = SLOTS // 2
    return jnp.minimum(pair // count, count - 1), pair % count


def fetch_kernel(share, number, sizes_hbm, tables_hbm, twist_hbm, tables_ref, twist_ref, live_ref, sizes_ref, sems):
    fetches = [
        pltpu.make_async_copy(tables_hbm, tables_ref, sems.at[0]),
        pltpu.make_async_copy(twist_hbm, twist_ref, sems.at[1]),
        pltpu.make_async_copy(sizes_hbm, sizes_ref, sems.at[2]),
    ]
    for fetch in fetches:
        fetch.start()
    for fetch in fetches:
        fetch.wait()
    slot, far_slot = pair_slots(share)
    block = lax.axis_index("stn")
    other = jnp.bitwise_xor(block, number)
    places = lax.broadcasted_iota(jnp.int32, sizes_ref.shape, 1)
    sizes = sizes_ref[...]
    live_near = jnp.sum(jnp.where(places == block, sizes, 0), axis=1, keepdims=True)
    live_far = jnp.sum(jnp.where(places == other, sizes, 0), axis=1, keepdims=True)
    live_ref[...] = ((slot < live_near) & (far_slot < live_far)).astype(F32)


def near_kernel(share, rows_ref, tables_ref, twist_ref, live_ref, near_ref, keep_ref):
    windows = rows_ref.shape[0]
    slot, _ = pair_slots(share)
    packs, power, root = whitened(in_order(rows_ref), tables_ref, twist_ref)
    live = live_ref[...][None]
    for g, pack in enumerate(packs):
        for h in range(2):
            for i in range(2):
                value = placed(pack[i], slot + h * (SLOTS // 2))
                value = value.reshape(HALF, SLOTS, COLS) * live
                near_ref[2 * g + h, i] = value.reshape(HALF * SLOTS, COLS)
    by_row = (power * (root * root)).reshape(HALF, SLOTS, COLS)
    total = 2.0 * jnp.sum(by_row, axis=0) - by_row[0] - by_row[EVEN - 1]
    mean = jnp.sum(total, axis=1, keepdims=True) * (1.0 / PERIOD)
    scale = 1.0 / (mean + SMALL)
    keep = (1.0 - by_row * scale[None]).reshape(HALF * SLOTS, COLS)
    keep_ref[...] = placed(keep, slot)


def far_kernel(rows_ref, near_ref, keep_ref, tables_ref, twist_ref, plain_ref, refined_ref):
    windows = near_ref.shape[0]
    share = plain_ref.shape[0]
    _, far_slot = pair_slots(share)
    evens = EVEN * SLOTS
    packs, _, _ = whitened(in_order(rows_ref), tables_ref, twist_ref)
    re = im = 0.0
    for g, pack in enumerate(packs):
        for h in range(2):
            index = far_slot + h * (SLOTS // 2)
            far_re, far_im = placed(pack[0], index), placed(pack[1], index)
            near_re, near_im = near_ref[2 * g + h, 0], near_ref[2 * g + h, 1]
            re = re + (near_re * far_re + near_im * far_im)
            im = im + (near_im * far_re - near_re * far_im)
    keep = keep_ref[...]
    back = (table_slice(tables_ref, 3), table_slice(tables_ref, 4))
    halves = []
    for value_re, value_im in ((re, im), (re * keep, im * keep)):
        half = transformed_back(value_re, value_im, back)
        halves.append(twisted(*half, twist_ref))
    half_re = jnp.concatenate([halves[0][0], halves[1][0]], axis=1)
    half_im = jnp.concatenate([halves[0][1], halves[1][1]], axis=1)
    edge = evens - SLOTS
    middle = half_re[edge:evens] * (1.0 / math.sqrt(PERIOD * windows))
    same = jnp.concatenate([half_re[:edge], half_im[evens:]], axis=0)
    turned = jnp.concatenate([half_re[evens:], half_im[:edge]], axis=0)
    same = dot_split((table_slice(tables_ref, 5), table_slice(tables_ref, 7)), split(same))
    turned = dot_split((table_slice(tables_ref, 6), table_slice(tables_ref, 8)), split(turned))

    for j in range(EVEN):
        rows = slice(j * SLOTS, (j + 1) * SLOTS)
        steady = same[rows] + (middle if j % 2 == 0 else -middle)
        mirrored = [(2 * ODD - j, steady - turned[rows])] if 0 < j < ODD else []
        for lag, here in [(j, steady + turned[rows])] + mirrored:
            cols = slice(lag * COLS, (lag + 1) * COLS)
            plain_ref[:, cols] = here[:share, :COLS]
            refined_ref[:, cols] = here[:share, COLS:]


def per_device(samples, array_sizes, partner):
    count = samples.shape[0]
    groups = lax.axis_size("tm")
    blocks = lax.axis_size("stn")
    share = count * count // groups
    vmem = pl.BlockSpec(memory_space=pltpu.VMEM)
    params = pltpu.CompilerParams(vmem_limit_bytes=32 * 1024 * 1024)
    rows = samples.reshape(count, LAGS // COLS, COLS).transpose(1, 0, 2).reshape(-1, COLS)

    def to_fast_memory(value):
        return lax.ppermute(value, "tm", [(i, i) for i in range(groups)])

    own = to_fast_memory(rows)

    def with_others(value):
        return [value] + [
            lax.ppermute(value, "tm", [(i, i ^ step) for i in range(groups)])
            for step in range(1, groups)
        ]

    def fast(shape, kind=F32):
        return jax.ShapeDtypeStruct(shape, kind)

    early = groups == 2

    def own_stations(own, tables, twist, live):
        return pl.pallas_call(
            functools.partial(near_kernel, share),
            out_shape=(
                fast((groups, 2, HALF * SLOTS, COLS)), fast((HALF * SLOTS, COLS))
            ),
            in_specs=[vmem] * 4,
            out_specs=(vmem,) * 2,
            compiler_params=params,
        )(jnp.stack(with_others(own)), tables, twist, live)

    def exchanged(number, own, sizes, tables, twist):
        far = lax.ppermute(own, "stn", [(i, i ^ number) for i in range(blocks)])
        fetched = pl.pallas_call(
            functools.partial(fetch_kernel, share, number),
            out_shape=(fast(tables.shape, BF16), fast(twist.shape), fast((SLOTS, COLS))),
            in_specs=[pl.BlockSpec(memory_space=pltpu.HBM)] * 3,
            out_specs=(vmem,) * 3,
            scratch_shapes=[
                pltpu.VMEM(sizes.shape, sizes.dtype), pltpu.SemaphoreType.DMA((3,))
            ],
            compiler_params=params,
        )(*(pltpu.with_memory_space_constraint(v, pltpu.HBM) for v in (sizes, tables, twist)))
        far, fetched = lax.optimization_barrier((far, fetched))
        mine = own_stations(own, *fetched) if early else fetched
        return jnp.stack(with_others(far)), *mine

    near_tables, near_twist, far_tables, far_twist = tables(count, groups)
    both, *mine = lax.switch(
        partner[0] - 1,
        [functools.partial(exchanged, number) for number in range(1, blocks)],
        own, array_sizes[None], jnp.asarray(near_tables), jnp.asarray(near_twist),
    )
    near, keep = mine if early else own_stations(own, *mine)
    out = fast((share, LAGS))
    return pl.pallas_call(
        far_kernel,
        out_shape=(out, out),
        in_specs=[vmem] * 5,
        out_specs=(vmem, vmem),
        compiler_params=params,
    )(both, near, keep, far_tables, far_twist)


def solution(mesh):
    placed = (P("stn", "tm"), P(), P())
    return jax.shard_map(
        per_device,
        mesh=mesh,
        in_specs=placed,
        out_specs=(P(("stn", "tm"), None), P(("stn", "tm"), None)),
        check_vma=False,
    )
```

```python
import functools
import math

import jax
import jax.numpy as jnp
import numpy as np
from jax import lax
from jax.experimental import pallas as pl
from jax.experimental.pallas import tpu as pltpu
from jax.sharding import PartitionSpec as P

LAGS = 4096
PERIOD = 2 * LAGS
ROWS = 64
COLS = 128
EVEN = ROWS // 4 + 1
ODD = ROWS // 4
HALF = EVEN + ODD
FOLD = COLS // 2
SLOTS = 8
SMALL = 1e-06
F32 = jnp.float32
BF16 = jnp.bfloat16


def split_table(table):
    high = table.astype(np.float32).astype(jnp.bfloat16)
    low = (table - high.astype(np.float64)).astype(np.float32).astype(jnp.bfloat16)
    return np.stack([high, low])


@functools.lru_cache(maxsize=None)
def tables(count, windows):
    f1 = np.concatenate([np.arange(0, ROWS // 2 + 1, 2), np.arange(1, ROWS // 2, 2)])
    lag = np.arange(LAGS // COLS)
    angle = 2 * np.pi * ((f1[:, None] * lag[None, :]) % ROWS) / ROWS
    half = ODD // 2
    base = np.concatenate([np.arange(half + 1), np.arange(EVEN, EVEN + half)])
    first = []
    for parity in range(2):
        kept = angle[base, parity::2]
        part = np.concatenate([np.cos(kept), -np.sin(kept[1:])])
        part = part[:, None, :, None] * np.eye(SLOTS)[None, :, None, :]
        first.append(np.concatenate(list(split_table(part.reshape(-1, COLS))), axis=1))
    first = np.stack(first)
    n2 = np.arange(COLS)
    twist = 2 * np.pi * ((f1[:, None] * n2[None, :]) % PERIOD) / PERIOD
    twist = np.stack([np.cos(twist), np.sin(twist)]).astype(np.float32)
    turn = 2 * np.pi * ((n2[:, None] * n2[None, :]) % COLS) / COLS
    cos, sin = np.cos(turn), np.sin(turn)
    order = np.where(n2 > FOLD, COLS + FOLD - n2, n2)
    pairs = np.concatenate([order, COLS + order])
    inverse = split_table(np.block([[cos, -sin], [sin, cos]])[pairs])
    folded = np.where(n2 > FOLD, n2 - FOLD, n2)
    table = np.where(n2[None, :] > FOLD, sin[:, folded], cos[:, folded])
    high, low = split_table(table)
    rest = (table - high.astype(np.float64) - low.astype(np.float64)).astype(np.float32)
    rest = np.pad(rest.astype(jnp.bfloat16), ((0, 0), (0, COLS)))
    second = np.concatenate([high, low], axis=1), rest
    weight = np.where(f1 % (ROWS // 2) == 0, 1.0, 2.0)[:, None] / math.sqrt(PERIOD * windows)
    cos, sin = (np.cos(angle) * weight)[:, :EVEN].T, (np.sin(angle) * weight)[:, :EVEN].T
    same = np.concatenate([cos[:, : EVEN - 1], sin[:, EVEN:]], axis=1)
    turned = np.concatenate([cos[:, EVEN:], sin[:, : EVEN - 1]], axis=1)
    last = np.stack([np.kron(same, np.eye(SLOTS)), np.kron(turned, np.eye(SLOTS))])
    last = split_table(last).reshape(4, EVEN * SLOTS, 2 * COLS)

    def padded(table):
        extra = -table.shape[1] % 16
        return np.pad(table, ((0, 0), (0, extra), (0, 0))).reshape(-1, 2 * COLS)

    near = np.concatenate([padded(first), second[0], second[1]])
    wide = np.concatenate([twist[0], twist[1]], axis=1).astype(np.float64)
    parts = []
    for _ in range(3):
        parts.append(wide.astype(np.float32).astype(jnp.bfloat16))
        wide = wide - parts[-1].astype(np.float64)
    far_twist = padded(np.stack(parts))
    return near, twist, np.concatenate([near, inverse[0], inverse[1], padded(last), far_twist])


def table_slice(ref, which):
    rows = -(-HALF * SLOTS // 16) * 16
    if which < 2:
        return ref[which * rows : which * rows + HALF * SLOTS]
    start = 2 * rows + (which - 2) * 2 * COLS
    if which < 5:
        return ref[start : start + 2 * COLS]
    start = 2 * rows + 6 * COLS
    rows = -(-EVEN * SLOTS // 16) * 16
    start += (which - 5) * rows
    return ref[start : start + EVEN * SLOTS]


def dot(left, right):
    return jnp.dot(left, right, preferred_element_type=F32)


def split(value):
    high = value.astype(BF16)
    return high, (value - high.astype(F32)).astype(BF16)


def dot_split(left, right):
    rows = left[0].shape[0]
    both = dot(jnp.concatenate(left, axis=0), right[0])
    return both[:rows] + (both[rows:] + dot(left[0], right[1]))


def transformed(re, im, table):
    rows = re.shape[0]
    value = jnp.concatenate([re, im], axis=0)
    high = value.astype(BF16)
    value = value - high.astype(F32)
    middle = value.astype(BF16)
    low = (value - middle.astype(F32)).astype(BF16)
    main, rest = table[:COLS], table[COLS:, :COLS]
    out = dot(jnp.concatenate([high, middle], axis=1), jnp.concatenate([main, main], axis=0))
    rest = jnp.concatenate([main[:, :COLS], rest], axis=0)
    small = dot(jnp.concatenate([low, high], axis=1), rest)
    out = out[:, :COLS] + (out[:, COLS:] + small)
    re, im = out[:rows], out[rows:]
    lane = lax.broadcasted_iota(jnp.int32, (rows, COLS), 1)
    lower, upper = (lane > 0) & (lane < FOLD), lane > FOLD
    far_re, far_im = pltpu.roll(re, FOLD, axis=1), pltpu.roll(im, FOLD, axis=1)
    out_re = jnp.where(upper, far_re - im, re + jnp.where(lower, far_im, 0.0))
    out_im = jnp.where(upper, far_im + re, im - jnp.where(lower, far_re, 0.0))
    return out_re, out_im


def transformed_back(re, im, table):
    out = dot_split(split(jnp.concatenate([re, im], axis=1)), table)
    return out[:, :COLS], out[:, COLS:]


def twist_of(ref):
    rows = -(-HALF // 16) * 16
    start = ref.shape[0] - 3 * rows
    parts = [ref[start + i * rows : start + i * rows + HALF].astype(F32) for i in range(3)]
    whole = (parts[2] + parts[1]) + parts[0]
    return whole[:, :COLS], whole[:, COLS:]


def first_stage(lower, upper, tables_ref):
    def joined(a, b):
        a = a.astype(F32).reshape(ODD, SLOTS, COLS)
        b = b.astype(F32).reshape(ODD, SLOTS, COLS)
        front = lax.broadcasted_iota(jnp.int32, a.shape, 1) < SLOTS // 2
        even = jnp.where(front, a, pltpu.roll(b, SLOTS // 2, axis=1))
        odd = jnp.where(front, pltpu.roll(a, SLOTS // 2, axis=1), b)
        return [part.reshape(ODD * SLOTS, COLS).astype(BF16) for part in (even, odd)]

    parts = [joined(a, b) for a, b in zip(lower, upper)]
    sums = []
    for parity in range(2):
        held = jnp.concatenate([part[parity] for part in parts], axis=1)
        sums.append(dot(table_slice(tables_ref, parity), jnp.concatenate([held, held], axis=0)))
    plus, minus = sums[0] + sums[1], sums[0] - sums[1]
    half = ODD // 2

    def group(value, i):
        return value[i * SLOTS : (i + 1) * SLOTS]

    none = jnp.zeros_like(group(plus, 0))
    back = list(range(half - 1, -1, -1))
    re = [group(plus, i) for i in range(half + 1)] + [group(minus, i) for i in back]
    re += [group(plus, half + 1 + i) for i in range(half)]
    re += [group(minus, half + 1 + i) for i in back]
    at = 2 * half + 1
    im = [none] + [group(plus, at + i) for i in range(half)]
    im += [-group(minus, at + i) for i in back[1:]] + [none]
    im += [group(plus, at + half + i) for i in range(half)]
    im += [-group(minus, at + half + i) for i in back]
    return jnp.concatenate(re, axis=0), jnp.concatenate(im, axis=0)


def twisted(re, im, twist_ref):
    re = re.reshape(HALF, SLOTS, COLS)
    im = im.reshape(HALF, SLOTS, COLS)
    cos = twist_ref[0][:, None, :]
    sin = twist_ref[1][:, None, :]
    out_re = (re * cos + im * sin).reshape(HALF * SLOTS, COLS)
    out_im = (im * cos - re * sin).reshape(HALF * SLOTS, COLS)
    return out_re, out_im


def smoothed(power):
    power = power.reshape(HALF, SLOTS, COLS)
    lane = lax.broadcasted_iota(jnp.int32, (SLOTS, COLS), 1)
    below = jnp.where(lane % FOLD == 0, lane, (lane + FOLD) % COLS)
    above = jnp.where(lane < FOLD, lane + FOLD + 1, lane - FOLD - 1)
    above = jnp.where(lane == FOLD - 1, FOLD, jnp.where(lane == FOLD, FOLD - 1, above))

    def mirrored(row, index):
        return jnp.take_along_axis(power[row], index, axis=1)[None]

    even = jnp.concatenate(
        [mirrored(1, below), power[:EVEN], mirrored(EVEN - 2, above)], axis=0
    )
    odd = jnp.concatenate(
        [mirrored(EVEN, below), power[EVEN:], mirrored(HALF - 1, above)], axis=0
    )
    pairs_even = even[:-1] + even[1:]
    pairs_odd = odd[:-1] + odd[1:]
    smooth_even = (pairs_even[:-1] + even[2:]) + pairs_odd
    smooth_odd = (pairs_odd[:-1] + odd[2:]) + pairs_even[1:-1]
    return jnp.concatenate([smooth_even, smooth_odd], axis=0).reshape(HALF * SLOTS, COLS)


def placed(value, index):
    rows = value.shape[0] // SLOTS
    value = value.reshape(rows, SLOTS, COLS)
    index = jnp.broadcast_to(index[None], value.shape)
    return jnp.take_along_axis(value, index, axis=1).reshape(rows * SLOTS, COLS)


def in_order(rows_ref):
    mine = lax.axis_index("tm")
    windows = lax.axis_size("tm")
    return [rows_ref[jnp.bitwise_xor(mine, j)] for j in range(windows)]


def whitened(halves, tables_ref, twist_ref):
    windows = len(halves)
    size, evens = HALF * SLOTS, EVEN * SLOTS
    grid_re, grid_im = first_stage(halves[0::2], halves[1::2], tables_ref)
    front = lax.broadcasted_iota(jnp.int32, (HALF, SLOTS, COLS), 1) < SLOTS // 2

    def rolled(value):
        return pltpu.roll(value.reshape(HALF, SLOTS, COLS), SLOTS // 2, axis=1)

    forth = table_slice(tables_ref, 2)
    packs = []
    power = 0.0
    later = None
    for g in reversed(range(windows // 2)):
        cols = slice(g * COLS, (g + 1) * COLS)
        here = twisted(grid_re[:, cols], grid_im[:, cols], twist_ref)
        turned = [rolled(part) for part in here]
        value = []
        for i in range(2):
            follow = 0.0 if later is None else later[i]
            follow = jnp.where(front, turned[i], follow).reshape(size, COLS)
            value.append(
                jnp.concatenate(
                    [here[i][:evens] + follow[:evens], here[i][evens:] - follow[evens:]], axis=0
                )
            )
        later = turned
        re, im = transformed(*value, forth)
        power = power + (re * re + im * im)
        packs.insert(0, (re, im))
    power = power + rolled(power).reshape(size, COLS)
    root = lax.rsqrt(smoothed(power) * (1.0 / (5 * windows)) + SMALL)
    return [(re * root, im * root) for re, im in packs], power, root


def pair_slots(share):
    pair = lax.axis_index("tm") * share + lax.broadcasted_iota(jnp.int32, (SLOTS, COLS), 0)
    count = SLOTS // 2
    return jnp.minimum(pair // count, count - 1), pair % count


def fetch_kernel(share, number, sizes_hbm, tables_hbm, twist_hbm, tables_ref, twist_ref, live_ref, sizes_ref, sems):
    fetches = [
        pltpu.make_async_copy(tables_hbm, tables_ref, sems.at[0]),
        pltpu.make_async_copy(twist_hbm, twist_ref, sems.at[1]),
        pltpu.make_async_copy(sizes_hbm, sizes_ref, sems.at[2]),
    ]
    for fetch in fetches:
        fetch.start()
    for fetch in fetches:
        fetch.wait()
    slot, far_slot = pair_slots(share)
    block = lax.axis_index("stn")
    other = jnp.bitwise_xor(block, number)
    places = lax.broadcasted_iota(jnp.int32, sizes_ref.shape, 1)
    sizes = sizes_ref[...]
    live_near = jnp.sum(jnp.where(places == block, sizes, 0), axis=1, keepdims=True)
    live_far = jnp.sum(jnp.where(places == other, sizes, 0), axis=1, keepdims=True)
    live_ref[...] = ((slot < live_near) & (far_slot < live_far)).astype(F32)


def near_kernel(share, rows_ref, tables_ref, twist_ref, live_ref, near_ref, keep_ref):
    windows = rows_ref.shape[0]
    slot, _ = pair_slots(share)
    packs, power, root = whitened(in_order(rows_ref), tables_ref, twist_ref)
    live = live_ref[...][None]
    for g, pack in enumerate(packs):
        for h in range(2):
            for i in range(2):
                value = placed(pack[i], slot + h * (SLOTS // 2))
                value = value.reshape(HALF, SLOTS, COLS) * live
                near_ref[2 * g + h, i] = value.reshape(HALF * SLOTS, COLS)
    by_row = (power * (root * root)).reshape(HALF, SLOTS, COLS)
    total = 2.0 * jnp.sum(by_row, axis=0) - by_row[0] - by_row[EVEN - 1]
    mean = jnp.sum(total, axis=1, keepdims=True) * (1.0 / PERIOD)
    scale = 1.0 / (mean + SMALL)
    keep = (1.0 - by_row * scale[None]).reshape(HALF * SLOTS, COLS)
    keep_ref[...] = placed(keep, slot)


def far_kernel(rows_ref, near_ref, keep_ref, tables_ref, plain_ref, refined_ref):
    twist_ref = twist_of(tables_ref)
    windows = near_ref.shape[0]
    share = plain_ref.shape[0]
    _, far_slot = pair_slots(share)
    evens = EVEN * SLOTS
    packs, _, _ = whitened(in_order(rows_ref), tables_ref, twist_ref)
    re = im = 0.0
    for g, pack in enumerate(packs):
        for h in range(2):
            index = far_slot + h * (SLOTS // 2)
            far_re, far_im = placed(pack[0], index), placed(pack[1], index)
            near_re, near_im = near_ref[2 * g + h, 0], near_ref[2 * g + h, 1]
            re = re + (near_re * far_re + near_im * far_im)
            im = im + (near_im * far_re - near_re * far_im)
    keep = keep_ref[...]
    back = (table_slice(tables_ref, 3), table_slice(tables_ref, 4))
    halves = []
    for value_re, value_im in ((re, im), (re * keep, im * keep)):
        half = transformed_back(value_re, value_im, back)
        halves.append(twisted(*half, twist_ref))
    half_re = jnp.concatenate([halves[0][0], halves[1][0]], axis=1)
    half_im = jnp.concatenate([halves[0][1], halves[1][1]], axis=1)
    edge = evens - SLOTS
    middle = half_re[edge:evens] * (1.0 / math.sqrt(PERIOD * windows))
    same = jnp.concatenate([half_re[:edge], half_im[evens:]], axis=0)
    turned = jnp.concatenate([half_re[evens:], half_im[:edge]], axis=0)
    same = dot_split((table_slice(tables_ref, 5), table_slice(tables_ref, 7)), split(same))
    turned = dot_split((table_slice(tables_ref, 6), table_slice(tables_ref, 8)), split(turned))

    for j in range(EVEN):
        rows = slice(j * SLOTS, (j + 1) * SLOTS)
        steady = same[rows] + (middle if j % 2 == 0 else -middle)
        mirrored = [(2 * ODD - j, steady - turned[rows])] if 0 < j < ODD else []
        for lag, here in [(j, steady + turned[rows])] + mirrored:
            cols = slice(lag * COLS, (lag + 1) * COLS)
            plain_ref[:, cols] = here[:share, :COLS]
            refined_ref[:, cols] = here[:share, COLS:]


def per_device(samples, array_sizes, partner):
    count = samples.shape[0]
    groups = lax.axis_size("tm")
    blocks = lax.axis_size("stn")
    share = count * count // groups
    vmem = pl.BlockSpec(memory_space=pltpu.VMEM)
    params = pltpu.CompilerParams(vmem_limit_bytes=32 * 1024 * 1024)
    rows = samples.reshape(count, LAGS // COLS, COLS).transpose(1, 0, 2).reshape(-1, COLS)

    def to_fast_memory(value):
        return lax.ppermute(value, "tm", [(i, i) for i in range(groups)])

    own = to_fast_memory(rows)

    def with_others(value):
        return [value] + [
            lax.ppermute(value, "tm", [(i, i ^ step) for i in range(groups)])
            for step in range(1, groups)
        ]

    def fast(shape, kind=F32):
        return jax.ShapeDtypeStruct(shape, kind)

    early = groups == 2

    def own_stations(own, tables, twist, live):
        return pl.pallas_call(
            functools.partial(near_kernel, share),
            out_shape=(
                fast((groups, 2, HALF * SLOTS, COLS)), fast((HALF * SLOTS, COLS))
            ),
            in_specs=[vmem] * 4,
            out_specs=(vmem,) * 2,
            compiler_params=params,
        )(jnp.stack(with_others(own)), tables, twist, live)

    def exchanged(number, own, sizes, tables, twist):
        far = lax.ppermute(own, "stn", [(i, i ^ number) for i in range(blocks)])
        fetched = pl.pallas_call(
            functools.partial(fetch_kernel, share, number),
            out_shape=(fast(tables.shape, BF16), fast(twist.shape), fast((SLOTS, COLS))),
            in_specs=[pl.BlockSpec(memory_space=pltpu.HBM)] * 3,
            out_specs=(vmem,) * 3,
            scratch_shapes=[
                pltpu.VMEM(sizes.shape, sizes.dtype), pltpu.SemaphoreType.DMA((3,))
            ],
            compiler_params=params,
        )(*(pltpu.with_memory_space_constraint(v, pltpu.HBM) for v in (sizes, tables, twist)))
        far, fetched = lax.optimization_barrier((far, fetched))
        mine = own_stations(own, *fetched) if early else fetched
        return jnp.stack(with_others(far)), *mine

    near_tables, near_twist, far_tables = tables(count, groups)
    both, *mine = lax.switch(
        partner[0] - 1,
        [functools.partial(exchanged, number) for number in range(1, blocks)],
        own, array_sizes[None], jnp.asarray(near_tables), jnp.asarray(near_twist),
    )
    near, keep = mine if early else own_stations(own, *mine)
    out = fast((share, LAGS))
    return pl.pallas_call(
        far_kernel,
        out_shape=(out, out),
        in_specs=[vmem] * 4,
        out_specs=(vmem, vmem),
        compiler_params=params,
    )(both, near, keep, far_tables)


def solution(mesh):
    placed = (P("stn", "tm"), P(), P())
    return jax.shard_map(
        per_device,
        mesh=mesh,
        in_specs=placed,
        out_specs=(P(("stn", "tm"), None), P(("stn", "tm"), None)),
        check_vma=False,
    )
```

```python
import functools
import math

import jax
import jax.numpy as jnp
import numpy as np
from jax import lax
from jax.experimental import pallas as pl
from jax.experimental.pallas import tpu as pltpu
from jax.sharding import PartitionSpec as P

LAGS = 4096
PERIOD = 2 * LAGS
ROWS = 64
COLS = 128
EVEN = ROWS // 4 + 1
ODD = ROWS // 4
HALF = EVEN + ODD
FOLD = COLS // 2
SLOTS = 8
SMALL = 1e-06
F32 = jnp.float32
BF16 = jnp.bfloat16


def split_table(table):
    high = table.astype(np.float32).astype(jnp.bfloat16)
    low = (table - high.astype(np.float64)).astype(np.float32).astype(jnp.bfloat16)
    return np.stack([high, low])


@functools.lru_cache(maxsize=None)
def tables(count, windows):
    f1 = np.concatenate([np.arange(0, ROWS // 2 + 1, 2), np.arange(1, ROWS // 2, 2)])
    lag = np.arange(LAGS // COLS)
    angle = 2 * np.pi * ((f1[:, None] * lag[None, :]) % ROWS) / ROWS
    half = ODD // 2
    base = np.concatenate([np.arange(half + 1), np.arange(EVEN, EVEN + half)])
    first = []
    for parity in range(2):
        kept = angle[base, parity::2]
        part = np.concatenate([np.cos(kept), -np.sin(kept[1:])])
        part = part[:, None, :, None] * np.eye(SLOTS)[None, :, None, :]
        first.append(np.concatenate(list(split_table(part.reshape(-1, COLS))), axis=1))
    first = np.stack(first)
    n2 = np.arange(COLS)
    twist = 2 * np.pi * ((f1[:, None] * n2[None, :]) % PERIOD) / PERIOD
    twist = np.stack([np.cos(twist), np.sin(twist)]).astype(np.float32)
    turn = 2 * np.pi * ((n2[:, None] * n2[None, :]) % COLS) / COLS
    cos, sin = np.cos(turn), np.sin(turn)
    order = np.where(n2 > FOLD, COLS + FOLD - n2, n2)
    pairs = np.concatenate([order, COLS + order])
    inverse = split_table(np.block([[cos, -sin], [sin, cos]])[pairs])
    folded = np.where(n2 > FOLD, n2 - FOLD, n2)
    table = np.where(n2[None, :] > FOLD, sin[:, folded], cos[:, folded])
    high, low = split_table(table)
    rest = (table - high.astype(np.float64) - low.astype(np.float64)).astype(np.float32)
    rest = np.pad(rest.astype(jnp.bfloat16), ((0, 0), (0, COLS)))
    second = np.concatenate([high, low], axis=1), rest
    weight = np.where(f1 % (ROWS // 2) == 0, 1.0, 2.0)[:, None] / math.sqrt(PERIOD * windows)
    cos, sin = (np.cos(angle) * weight)[:, :EVEN].T, (np.sin(angle) * weight)[:, :EVEN].T
    same = np.concatenate([cos[:, : EVEN - 1], sin[:, EVEN:]], axis=1)
    turned = np.concatenate([cos[:, EVEN:], sin[:, : EVEN - 1]], axis=1)
    last = np.stack([np.kron(same, np.eye(SLOTS)), np.kron(turned, np.eye(SLOTS))])
    last = split_table(last).reshape(4, EVEN * SLOTS, 2 * COLS)

    def padded(table):
        extra = -table.shape[1] % 16
        return np.pad(table, ((0, 0), (0, extra), (0, 0))).reshape(-1, 2 * COLS)

    near = np.concatenate([padded(first), second[0], second[1]])
    far_twist = np.pad(twist, ((0, 0), (0, -HALF % SLOTS), (0, 0)))
    far = np.concatenate([near, inverse[0], inverse[1], padded(last)])
    return near, twist, far, far_twist


def table_slice(ref, which):
    rows = -(-HALF * SLOTS // 16) * 16
    if which < 2:
        return ref[which * rows : which * rows + HALF * SLOTS]
    start = 2 * rows + (which - 2) * 2 * COLS
    if which < 5:
        return ref[start : start + 2 * COLS]
    start = 2 * rows + 6 * COLS
    rows = -(-EVEN * SLOTS // 16) * 16
    start += (which - 5) * rows
    return ref[start : start + EVEN * SLOTS]


def dot(left, right):
    return jnp.dot(left, right, preferred_element_type=F32)


def split(value):
    high = value.astype(BF16)
    return high, (value - high.astype(F32)).astype(BF16)


def dot_split(left, right):
    rows = left[0].shape[0]
    both = dot(jnp.concatenate(left, axis=0), right[0])
    return both[:rows] + (both[rows:] + dot(left[0], right[1]))


def transformed(re, im, table):
    rows = re.shape[0]
    value = jnp.concatenate([re, im], axis=0)
    high = value.astype(BF16)
    value = value - high.astype(F32)
    middle = value.astype(BF16)
    low = (value - middle.astype(F32)).astype(BF16)
    main, rest = table[:COLS], table[COLS:, :COLS]
    out = dot(jnp.concatenate([high, middle], axis=1), jnp.concatenate([main, main], axis=0))
    rest = jnp.concatenate([main[:, :COLS], rest], axis=0)
    small = dot(jnp.concatenate([low, high], axis=1), rest)
    out = (out[:, :COLS] + out[:, COLS:]) + small
    re, im = out[:rows], out[rows:]
    lane = lax.broadcasted_iota(jnp.int32, (rows, COLS), 1)
    lower, upper = (lane > 0) & (lane < FOLD), lane > FOLD
    far_re, far_im = pltpu.roll(re, FOLD, axis=1), pltpu.roll(im, FOLD, axis=1)
    out_re = jnp.where(upper, far_re - im, re + jnp.where(lower, far_im, 0.0))
    out_im = jnp.where(upper, far_im + re, im - jnp.where(lower, far_re, 0.0))
    return out_re, out_im


def transformed_back(re, im, table):
    out = dot_split(split(jnp.concatenate([re, im], axis=1)), table)
    return out[:, :COLS], out[:, COLS:]


def first_stage(lower, upper, tables_ref):
    def joined(a, b):
        a = a.astype(F32).reshape(ODD, SLOTS, COLS)
        b = b.astype(F32).reshape(ODD, SLOTS, COLS)
        front = lax.broadcasted_iota(jnp.int32, a.shape, 1) < SLOTS // 2
        even = jnp.where(front, a, pltpu.roll(b, SLOTS // 2, axis=1))
        odd = jnp.where(front, pltpu.roll(a, SLOTS // 2, axis=1), b)
        return [part.reshape(ODD * SLOTS, COLS).astype(BF16) for part in (even, odd)]

    parts = [joined(a, b) for a, b in zip(lower, upper)]
    sums = []
    for parity in range(2):
        held = jnp.concatenate([part[parity] for part in parts], axis=1)
        sums.append(dot(table_slice(tables_ref, parity), jnp.concatenate([held, held], axis=0)))
    plus, minus = sums[0] + sums[1], sums[0] - sums[1]
    half = ODD // 2

    def group(value, i):
        return value[i * SLOTS : (i + 1) * SLOTS]

    none = jnp.zeros_like(group(plus, 0))
    back = list(range(half - 1, -1, -1))
    re = [group(plus, i) for i in range(half + 1)] + [group(minus, i) for i in back]
    re += [group(plus, half + 1 + i) for i in range(half)]
    re += [group(minus, half + 1 + i) for i in back]
    at = 2 * half + 1
    im = [none] + [group(plus, at + i) for i in range(half)]
    im += [-group(minus, at + i) for i in back[1:]] + [none]
    im += [group(plus, at + half + i) for i in range(half)]
    im += [-group(minus, at + half + i) for i in back]
    return jnp.concatenate(re, axis=0), jnp.concatenate(im, axis=0)


def twisted(re, im, twist_ref):
    re = re.reshape(HALF, SLOTS, COLS)
    im = im.reshape(HALF, SLOTS, COLS)
    cos = twist_ref[0, :HALF][:, None, :]
    sin = twist_ref[1, :HALF][:, None, :]
    out_re = (re * cos + im * sin).reshape(HALF * SLOTS, COLS)
    out_im = (im * cos - re * sin).reshape(HALF * SLOTS, COLS)
    return out_re, out_im


def smoothed(power):
    power = power.reshape(HALF, SLOTS, COLS)
    lane = lax.broadcasted_iota(jnp.int32, (SLOTS, COLS), 1)
    below = jnp.where(lane % FOLD == 0, lane, (lane + FOLD) % COLS)
    above = jnp.where(lane < FOLD, lane + FOLD + 1, lane - FOLD - 1)
    above = jnp.where(lane == FOLD - 1, FOLD, jnp.where(lane == FOLD, FOLD - 1, above))

    def mirrored(row, index):
        return jnp.take_along_axis(power[row], index, axis=1)[None]

    even = jnp.concatenate(
        [mirrored(1, below), power[:EVEN], mirrored(EVEN - 2, above)], axis=0
    )
    odd = jnp.concatenate(
        [mirrored(EVEN, below), power[EVEN:], mirrored(HALF - 1, above)], axis=0
    )
    pairs_even = even[:-1] + even[1:]
    pairs_odd = odd[:-1] + odd[1:]
    smooth_even = (pairs_even[:-1] + even[2:]) + pairs_odd
    smooth_odd = (pairs_odd[:-1] + odd[2:]) + pairs_even[1:-1]
    return jnp.concatenate([smooth_even, smooth_odd], axis=0).reshape(HALF * SLOTS, COLS)


def placed(value, index):
    rows = value.shape[0] // SLOTS
    value = value.reshape(rows, SLOTS, COLS)
    index = jnp.broadcast_to(index[None], value.shape)
    return jnp.take_along_axis(value, index, axis=1).reshape(rows * SLOTS, COLS)


def in_order(rows_ref):
    mine = lax.axis_index("tm")
    windows = lax.axis_size("tm")
    return [rows_ref[jnp.bitwise_xor(mine, j)] for j in range(windows)]


def whitened(halves, tables_ref, twist_ref):
    windows = len(halves)
    size, evens = HALF * SLOTS, EVEN * SLOTS
    grid_re, grid_im = first_stage(halves[0::2], halves[1::2], tables_ref)
    front = lax.broadcasted_iota(jnp.int32, (HALF, SLOTS, COLS), 1) < SLOTS // 2

    def rolled(value):
        return pltpu.roll(value.reshape(HALF, SLOTS, COLS), SLOTS // 2, axis=1)

    forth = table_slice(tables_ref, 2)
    packs = []
    power = 0.0
    later = None
    for g in reversed(range(windows // 2)):
        cols = slice(g * COLS, (g + 1) * COLS)
        here = twisted(grid_re[:, cols], grid_im[:, cols], twist_ref)
        turned = [rolled(part) for part in here]
        value = []
        for i in range(2):
            follow = 0.0 if later is None else later[i]
            follow = jnp.where(front, turned[i], follow).reshape(size, COLS)
            value.append(
                jnp.concatenate(
                    [here[i][:evens] + follow[:evens], here[i][evens:] - follow[evens:]], axis=0
                )
            )
        later = turned
        re, im = transformed(*value, forth)
        power = power + (re * re + im * im)
        packs.insert(0, (re, im))
    power = power + rolled(power).reshape(size, COLS)
    root = lax.rsqrt(smoothed(power) * (1.0 / (5 * windows)) + SMALL)
    return [(re * root, im * root) for re, im in packs], power, root


def pair_slots(share):
    pair = lax.axis_index("tm") * share + lax.broadcasted_iota(jnp.int32, (SLOTS, COLS), 0)
    count = SLOTS // 2
    return jnp.minimum(pair // count, count - 1), pair % count


def fetch_kernel(share, number, sizes_hbm, tables_hbm, twist_hbm, tables_ref, twist_ref, live_ref, sizes_ref, sems):
    fetches = [
        pltpu.make_async_copy(tables_hbm, tables_ref, sems.at[0]),
        pltpu.make_async_copy(twist_hbm, twist_ref, sems.at[1]),
        pltpu.make_async_copy(sizes_hbm, sizes_ref, sems.at[2]),
    ]
    for fetch in fetches:
        fetch.start()
    for fetch in fetches:
        fetch.wait()
    slot, far_slot = pair_slots(share)
    block = lax.axis_index("stn")
    other = jnp.bitwise_xor(block, number)
    places = lax.broadcasted_iota(jnp.int32, sizes_ref.shape, 1)
    sizes = sizes_ref[...]
    live_near = jnp.sum(jnp.where(places == block, sizes, 0), axis=1, keepdims=True)
    live_far = jnp.sum(jnp.where(places == other, sizes, 0), axis=1, keepdims=True)
    live_ref[...] = ((slot < live_near) & (far_slot < live_far)).astype(F32)


def near_kernel(share, rows_ref, tables_ref, twist_ref, live_ref, near_ref, keep_ref):
    windows = rows_ref.shape[0]
    slot, _ = pair_slots(share)
    packs, power, root = whitened(in_order(rows_ref), tables_ref, twist_ref)
    live = live_ref[...][None]
    for g, pack in enumerate(packs):
        for h in range(2):
            for i in range(2):
                value = placed(pack[i], slot + h * (SLOTS // 2))
                value = value.reshape(HALF, SLOTS, COLS) * live
                near_ref[2 * g + h, i] = value.reshape(HALF * SLOTS, COLS)
    by_row = (power * (root * root)).reshape(HALF, SLOTS, COLS)
    total = 2.0 * jnp.sum(by_row, axis=0) - by_row[0] - by_row[EVEN - 1]
    mean = jnp.sum(total, axis=1, keepdims=True) * (1.0 / PERIOD)
    scale = 1.0 / (mean + SMALL)
    keep = (1.0 - by_row * scale[None]).reshape(HALF * SLOTS, COLS)
    keep_ref[...] = placed(keep, slot)


def far_kernel(rows_ref, near_ref, keep_ref, tables_ref, twist_ref, plain_ref, refined_ref):
    windows = near_ref.shape[0]
    share = plain_ref.shape[0]
    _, far_slot = pair_slots(share)
    evens = EVEN * SLOTS
    packs, _, _ = whitened(in_order(rows_ref), tables_ref, twist_ref)
    re = im = 0.0
    for g, pack in enumerate(packs):
        for h in range(2):
            index = far_slot + h * (SLOTS // 2)
            far_re, far_im = placed(pack[0], index), placed(pack[1], index)
            near_re, near_im = near_ref[2 * g + h, 0], near_ref[2 * g + h, 1]
            re = re + (near_re * far_re + near_im * far_im)
            im = im + (near_im * far_re - near_re * far_im)
    keep = keep_ref[...]
    back = (table_slice(tables_ref, 3), table_slice(tables_ref, 4))
    halves = []
    for value_re, value_im in ((re, im), (re * keep, im * keep)):
        half = transformed_back(value_re, value_im, back)
        halves.append(twisted(*half, twist_ref))
    half_re = jnp.concatenate([halves[0][0], halves[1][0]], axis=1)
    half_im = jnp.concatenate([halves[0][1], halves[1][1]], axis=1)
    edge = evens - SLOTS
    middle = half_re[edge:evens] * (1.0 / math.sqrt(PERIOD * windows))
    same = jnp.concatenate([half_re[:edge], half_im[evens:]], axis=0)
    turned = jnp.concatenate([half_re[evens:], half_im[:edge]], axis=0)
    same = dot_split((table_slice(tables_ref, 5), table_slice(tables_ref, 7)), split(same))
    turned = dot_split((table_slice(tables_ref, 6), table_slice(tables_ref, 8)), split(turned))

    for j in range(EVEN):
        rows = slice(j * SLOTS, (j + 1) * SLOTS)
        steady = same[rows] + (middle if j % 2 == 0 else -middle)
        mirrored = [(2 * ODD - j, steady - turned[rows])] if 0 < j < ODD else []
        for lag, here in [(j, steady + turned[rows])] + mirrored:
            cols = slice(lag * COLS, (lag + 1) * COLS)
            plain_ref[:, cols] = here[:share, :COLS]
            refined_ref[:, cols] = here[:share, COLS:]


def per_device(samples, array_sizes, partner):
    count = samples.shape[0]
    groups = lax.axis_size("tm")
    blocks = lax.axis_size("stn")
    share = count * count // groups
    vmem = pl.BlockSpec(memory_space=pltpu.VMEM)
    params = pltpu.CompilerParams(vmem_limit_bytes=32 * 1024 * 1024)
    rows = samples.reshape(count, LAGS // COLS, COLS).transpose(1, 0, 2).reshape(-1, COLS)

    def to_fast_memory(value):
        return lax.ppermute(value, "tm", [(i, i) for i in range(groups)])

    own = to_fast_memory(rows)

    def with_others(value):
        return [value] + [
            lax.ppermute(value, "tm", [(i, i ^ step) for i in range(groups)])
            for step in range(1, groups)
        ]

    def fast(shape, kind=F32):
        return jax.ShapeDtypeStruct(shape, kind)

    early = groups == 2

    def own_stations(own, tables, twist, live):
        return pl.pallas_call(
            functools.partial(near_kernel, share),
            out_shape=(
                fast((groups, 2, HALF * SLOTS, COLS)), fast((HALF * SLOTS, COLS))
            ),
            in_specs=[vmem] * 4,
            out_specs=(vmem,) * 2,
            compiler_params=params,
        )(jnp.stack(with_others(own)), tables, twist, live)

    def exchanged(number, own, sizes, tables, twist):
        far = lax.ppermute(own, "stn", [(i, i ^ number) for i in range(blocks)])
        fetched = pl.pallas_call(
            functools.partial(fetch_kernel, share, number),
            out_shape=(fast(tables.shape, BF16), fast(twist.shape), fast((SLOTS, COLS))),
            in_specs=[pl.BlockSpec(memory_space=pltpu.HBM)] * 3,
            out_specs=(vmem,) * 3,
            scratch_shapes=[
                pltpu.VMEM(sizes.shape, sizes.dtype), pltpu.SemaphoreType.DMA((3,))
            ],
            compiler_params=params,
        )(*(pltpu.with_memory_space_constraint(v, pltpu.HBM) for v in (sizes, tables, twist)))
        far, fetched = lax.optimization_barrier((far, fetched))
        mine = own_stations(own, *fetched) if early else fetched
        return jnp.stack(with_others(far)), *mine

    near_tables, near_twist, far_tables, far_twist = tables(count, groups)
    both, *mine = lax.switch(
        partner[0] - 1,
        [functools.partial(exchanged, number) for number in range(1, blocks)],
        own, array_sizes[None], jnp.asarray(near_tables), jnp.asarray(near_twist),
    )
    near, keep = mine if early else own_stations(own, *mine)
    out = fast((share, LAGS))
    return pl.pallas_call(
        far_kernel,
        out_shape=(out, out),
        in_specs=[vmem] * 5,
        out_specs=(vmem, vmem),
        compiler_params=params,
    )(both, near, keep, far_tables, far_twist)


def solution(mesh):
    placed = (P("stn", "tm"), P(), P())
    return jax.shard_map(
        per_device,
        mesh=mesh,
        in_specs=placed,
        out_specs=(P(("stn", "tm"), None), P(("stn", "tm"), None)),
        check_vma=False,
    )
```

```python
import functools
import math

import jax
import jax.numpy as jnp
import numpy as np
from jax import lax
from jax.experimental import pallas as pl
from jax.experimental.pallas import tpu as pltpu
from jax.sharding import PartitionSpec as P

LAGS = 4096
PERIOD = 2 * LAGS
ROWS = 64
COLS = 128
EVEN = ROWS // 4 + 1
ODD = ROWS // 4
HALF = EVEN + ODD
FOLD = COLS // 2
SLOTS = 8
SMALL = 1e-06
F32 = jnp.float32
BF16 = jnp.bfloat16


def split_table(table):
    high = table.astype(np.float32).astype(jnp.bfloat16)
    low = (table - high.astype(np.float64)).astype(np.float32).astype(jnp.bfloat16)
    return np.stack([high, low])


@functools.lru_cache(maxsize=None)
def tables(count, windows):
    f1 = np.concatenate([np.arange(0, ROWS // 2 + 1, 2), np.arange(1, ROWS // 2, 2)])
    lag = np.arange(LAGS // COLS)
    angle = 2 * np.pi * ((f1[:, None] * lag[None, :]) % ROWS) / ROWS
    half = ODD // 2
    base = np.concatenate([np.arange(half + 1), np.arange(EVEN, EVEN + half)])
    first = []
    for parity in range(2):
        kept = angle[base, parity::2]
        part = np.concatenate([np.cos(kept), -np.sin(kept[1:])])
        part = part[:, None, :, None] * np.eye(SLOTS)[None, :, None, :]
        first.append(np.concatenate(list(split_table(part.reshape(-1, COLS))), axis=1))
    first = np.stack(first)
    n2 = np.arange(COLS)
    twist = 2 * np.pi * ((f1[:, None] * n2[None, :]) % PERIOD) / PERIOD
    twist = np.stack([np.cos(twist), np.sin(twist)]).astype(np.float32)
    turn = 2 * np.pi * ((n2[:, None] * n2[None, :]) % COLS) / COLS
    cos, sin = np.cos(turn), np.sin(turn)
    order = np.where(n2 > FOLD, COLS + FOLD - n2, n2)
    pairs = np.concatenate([order, COLS + order])
    inverse = split_table(np.block([[cos, -sin], [sin, cos]])[pairs])
    folded = np.where(n2 > FOLD, n2 - FOLD, n2)
    table = np.where(n2[None, :] > FOLD, sin[:, folded], cos[:, folded])
    high, low = split_table(table)
    rest = (table - high.astype(np.float64) - low.astype(np.float64)).astype(np.float32)
    rest = np.pad(rest.astype(jnp.bfloat16), ((0, 0), (0, COLS)))
    second = np.concatenate([high, low], axis=1), rest
    weight = np.where(f1 % (ROWS // 2) == 0, 1.0, 2.0)[:, None] / math.sqrt(PERIOD * windows)
    cos, sin = (np.cos(angle) * weight)[:, :EVEN].T, (np.sin(angle) * weight)[:, :EVEN].T
    same = np.concatenate([cos[:, : EVEN - 1], sin[:, EVEN:]], axis=1)
    turned = np.concatenate([cos[:, EVEN:], sin[:, : EVEN - 1]], axis=1)
    last = np.stack([np.kron(same, np.eye(SLOTS)), np.kron(turned, np.eye(SLOTS))])
    last = split_table(last).reshape(4, EVEN * SLOTS, 2 * COLS)

    def padded(table):
        extra = -table.shape[1] % 16
        return np.pad(table, ((0, 0), (0, extra), (0, 0))).reshape(-1, 2 * COLS)

    near = np.concatenate([padded(first), second[0], second[1]])
    wide = np.concatenate([twist[0], twist[1]], axis=1).astype(np.float64)
    parts = []
    for _ in range(3):
        parts.append(wide.astype(np.float32).astype(jnp.bfloat16))
        wide = wide - parts[-1].astype(np.float64)
    far_twist = padded(np.stack(parts))
    return near, twist, np.concatenate([near, inverse[0], inverse[1], padded(last), far_twist])


def table_slice(ref, which):
    rows = -(-HALF * SLOTS // 16) * 16
    if which < 2:
        return ref[which * rows : which * rows + HALF * SLOTS]
    start = 2 * rows + (which - 2) * 2 * COLS
    if which < 5:
        return ref[start : start + 2 * COLS]
    start = 2 * rows + 6 * COLS
    rows = -(-EVEN * SLOTS // 16) * 16
    start += (which - 5) * rows
    return ref[start : start + EVEN * SLOTS]


def dot(left, right):
    return jnp.dot(left, right, preferred_element_type=F32)


def split(value):
    high = value.astype(BF16)
    return high, (value - high.astype(F32)).astype(BF16)


def dot_split(left, right):
    rows = left[0].shape[0]
    both = dot(jnp.concatenate(left, axis=0), right[0])
    return both[:rows] + (both[rows:] + dot(left[0], right[1]))


def transformed(re, im, table):
    rows = re.shape[0]
    value = jnp.concatenate([re, im], axis=0)
    high = value.astype(BF16)
    value = value - high.astype(F32)
    middle = value.astype(BF16)
    low = (value - middle.astype(F32)).astype(BF16)
    main, rest = table[:COLS], table[COLS:, :COLS]
    out = dot(jnp.concatenate([high, middle], axis=1), jnp.concatenate([main, main], axis=0))
    rest = jnp.concatenate([main[:, :COLS], rest], axis=0)
    small = dot(jnp.concatenate([low, high], axis=1), rest)
    out = (out[:, :COLS] + out[:, COLS:]) + small
    re, im = out[:rows], out[rows:]
    lane = lax.broadcasted_iota(jnp.int32, (rows, COLS), 1)
    lower, upper = (lane > 0) & (lane < FOLD), lane > FOLD
    far_re, far_im = pltpu.roll(re, FOLD, axis=1), pltpu.roll(im, FOLD, axis=1)
    out_re = jnp.where(upper, far_re - im, re + jnp.where(lower, far_im, 0.0))
    out_im = jnp.where(upper, far_im + re, im - jnp.where(lower, far_re, 0.0))
    return out_re, out_im


def transformed_back(re, im, table):
    out = dot_split(split(jnp.concatenate([re, im], axis=1)), table)
    return out[:, :COLS], out[:, COLS:]


def twist_of(ref):
    rows = -(-HALF // 16) * 16
    start = ref.shape[0] - 3 * rows
    parts = [ref[start + i * rows : start + i * rows + HALF].astype(F32) for i in range(3)]
    whole = (parts[2] + parts[1]) + parts[0]
    return whole[:, :COLS], whole[:, COLS:]


def first_stage(lower, upper, tables_ref):
    def joined(a, b):
        a = a.astype(F32).reshape(ODD, SLOTS, COLS)
        b = b.astype(F32).reshape(ODD, SLOTS, COLS)
        front = lax.broadcasted_iota(jnp.int32, a.shape, 1) < SLOTS // 2
        even = jnp.where(front, a, pltpu.roll(b, SLOTS // 2, axis=1))
        odd = jnp.where(front, pltpu.roll(a, SLOTS // 2, axis=1), b)
        return [part.reshape(ODD * SLOTS, COLS).astype(BF16) for part in (even, odd)]

    parts = [joined(a, b) for a, b in zip(lower, upper)]
    sums = []
    for parity in range(2):
        held = jnp.concatenate([part[parity] for part in parts], axis=1)
        sums.append(dot(table_slice(tables_ref, parity), jnp.concatenate([held, held], axis=0)))
    plus, minus = sums[0] + sums[1], sums[0] - sums[1]
    half = ODD // 2

    def group(value, i):
        return value[i * SLOTS : (i + 1) * SLOTS]

    none = jnp.zeros_like(group(plus, 0))
    back = list(range(half - 1, -1, -1))
    re = [group(plus, i) for i in range(half + 1)] + [group(minus, i) for i in back]
    re += [group(plus, half + 1 + i) for i in range(half)]
    re += [group(minus, half + 1 + i) for i in back]
    at = 2 * half + 1
    im = [none] + [group(plus, at + i) for i in range(half)]
    im += [-group(minus, at + i) for i in back[1:]] + [none]
    im += [group(plus, at + half + i) for i in range(half)]
    im += [-group(minus, at + half + i) for i in back]
    return jnp.concatenate(re, axis=0), jnp.concatenate(im, axis=0)


def twisted(re, im, twist_ref):
    re = re.reshape(HALF, SLOTS, COLS)
    im = im.reshape(HALF, SLOTS, COLS)
    cos = twist_ref[0][:, None, :]
    sin = twist_ref[1][:, None, :]
    out_re = (re * cos + im * sin).reshape(HALF * SLOTS, COLS)
    out_im = (im * cos - re * sin).reshape(HALF * SLOTS, COLS)
    return out_re, out_im


def smoothed(power):
    power = power.reshape(HALF, SLOTS, COLS)
    lane = lax.broadcasted_iota(jnp.int32, (SLOTS, COLS), 1)
    below = jnp.where(lane % FOLD == 0, lane, (lane + FOLD) % COLS)
    above = jnp.where(lane < FOLD, lane + FOLD + 1, lane - FOLD - 1)
    above = jnp.where(lane == FOLD - 1, FOLD, jnp.where(lane == FOLD, FOLD - 1, above))

    def mirrored(row, index):
        return jnp.take_along_axis(power[row], index, axis=1)[None]

    even = jnp.concatenate(
        [mirrored(1, below), power[:EVEN], mirrored(EVEN - 2, above)], axis=0
    )
    odd = jnp.concatenate(
        [mirrored(EVEN, below), power[EVEN:], mirrored(HALF - 1, above)], axis=0
    )
    pairs_even = even[:-1] + even[1:]
    pairs_odd = odd[:-1] + odd[1:]
    smooth_even = (pairs_even[:-1] + even[2:]) + pairs_odd
    smooth_odd = (pairs_odd[:-1] + odd[2:]) + pairs_even[1:-1]
    return jnp.concatenate([smooth_even, smooth_odd], axis=0).reshape(HALF * SLOTS, COLS)


def placed(value, index):
    rows = value.shape[0] // SLOTS
    value = value.reshape(rows, SLOTS, COLS)
    index = jnp.broadcast_to(index[None], value.shape)
    return jnp.take_along_axis(value, index, axis=1).reshape(rows * SLOTS, COLS)


def in_order(rows_ref):
    mine = lax.axis_index("tm")
    windows = lax.axis_size("tm")
    return [rows_ref[jnp.bitwise_xor(mine, j)] for j in range(windows)]


def whitened(halves, tables_ref, twist_ref):
    windows = len(halves)
    size, evens = HALF * SLOTS, EVEN * SLOTS
    grid_re, grid_im = first_stage(halves[0::2], halves[1::2], tables_ref)
    front = lax.broadcasted_iota(jnp.int32, (HALF, SLOTS, COLS), 1) < SLOTS // 2

    def rolled(value):
        return pltpu.roll(value.reshape(HALF, SLOTS, COLS), SLOTS // 2, axis=1)

    forth = table_slice(tables_ref, 2)
    packs = []
    power = 0.0
    later = None
    for g in reversed(range(windows // 2)):
        cols = slice(g * COLS, (g + 1) * COLS)
        here = twisted(grid_re[:, cols], grid_im[:, cols], twist_ref)
        turned = [rolled(part) for part in here]
        value = []
        for i in range(2):
            follow = 0.0 if later is None else later[i]
            follow = jnp.where(front, turned[i], follow).reshape(size, COLS)
            value.append(
                jnp.concatenate(
                    [here[i][:evens] + follow[:evens], here[i][evens:] - follow[evens:]], axis=0
                )
            )
        later = turned
        re, im = transformed(*value, forth)
        power = power + (re * re + im * im)
        packs.insert(0, (re, im))
    power = power + rolled(power).reshape(size, COLS)
    root = lax.rsqrt(smoothed(power) * (1.0 / (5 * windows)) + SMALL)
    return [(re * root, im * root) for re, im in packs], power, root


def pair_slots(share):
    pair = lax.axis_index("tm") * share + lax.broadcasted_iota(jnp.int32, (SLOTS, COLS), 0)
    count = SLOTS // 2
    return jnp.minimum(pair // count, count - 1), pair % count


def fetch_kernel(share, number, sizes_hbm, tables_hbm, twist_hbm, tables_ref, twist_ref, live_ref, sizes_ref, sems):
    fetches = [
        pltpu.make_async_copy(tables_hbm, tables_ref, sems.at[0]),
        pltpu.make_async_copy(twist_hbm, twist_ref, sems.at[1]),
        pltpu.make_async_copy(sizes_hbm, sizes_ref, sems.at[2]),
    ]
    for fetch in fetches:
        fetch.start()
    for fetch in fetches:
        fetch.wait()
    slot, far_slot = pair_slots(share)
    block = lax.axis_index("stn")
    other = jnp.bitwise_xor(block, number)
    places = lax.broadcasted_iota(jnp.int32, sizes_ref.shape, 1)
    sizes = sizes_ref[...]
    live_near = jnp.sum(jnp.where(places == block, sizes, 0), axis=1, keepdims=True)
    live_far = jnp.sum(jnp.where(places == other, sizes, 0), axis=1, keepdims=True)
    live_ref[...] = ((slot < live_near) & (far_slot < live_far)).astype(F32)


def near_kernel(share, rows_ref, tables_ref, twist_ref, live_ref, near_ref, keep_ref):
    windows = rows_ref.shape[0]
    slot, _ = pair_slots(share)
    packs, power, root = whitened(in_order(rows_ref), tables_ref, twist_ref)
    live = live_ref[...][None]
    for g, pack in enumerate(packs):
        for h in range(2):
            for i in range(2):
                value = placed(pack[i], slot + h * (SLOTS // 2))
                value = value.reshape(HALF, SLOTS, COLS) * live
                near_ref[2 * g + h, i] = value.reshape(HALF * SLOTS, COLS)
    by_row = (power * (root * root)).reshape(HALF, SLOTS, COLS)
    total = 2.0 * jnp.sum(by_row, axis=0) - by_row[0] - by_row[EVEN - 1]
    mean = jnp.sum(total, axis=1, keepdims=True) * (1.0 / PERIOD)
    scale = 1.0 / (mean + SMALL)
    keep = (1.0 - by_row * scale[None]).reshape(HALF * SLOTS, COLS)
    keep_ref[...] = placed(keep, slot)


def far_kernel(rows_ref, near_ref, keep_ref, tables_ref, plain_ref, refined_ref):
    twist_ref = twist_of(tables_ref)
    windows = near_ref.shape[0]
    share = plain_ref.shape[0]
    _, far_slot = pair_slots(share)
    evens = EVEN * SLOTS
    packs, _, _ = whitened(in_order(rows_ref), tables_ref, twist_ref)
    re = im = 0.0
    for g, pack in enumerate(packs):
        for h in range(2):
            index = far_slot + h * (SLOTS // 2)
            far_re, far_im = placed(pack[0], index), placed(pack[1], index)
            near_re, near_im = near_ref[2 * g + h, 0], near_ref[2 * g + h, 1]
            re = re + (near_re * far_re + near_im * far_im)
            im = im + (near_im * far_re - near_re * far_im)
    keep = keep_ref[...]
    back = (table_slice(tables_ref, 3), table_slice(tables_ref, 4))
    halves = []
    for value_re, value_im in ((re, im), (re * keep, im * keep)):
        half = transformed_back(value_re, value_im, back)
        halves.append(twisted(*half, twist_ref))
    half_re = jnp.concatenate([halves[0][0], halves[1][0]], axis=1)
    half_im = jnp.concatenate([halves[0][1], halves[1][1]], axis=1)
    edge = evens - SLOTS
    middle = half_re[edge:evens] * (1.0 / math.sqrt(PERIOD * windows))
    same = jnp.concatenate([half_re[:edge], half_im[evens:]], axis=0)
    turned = jnp.concatenate([half_re[evens:], half_im[:edge]], axis=0)
    same = dot_split((table_slice(tables_ref, 5), table_slice(tables_ref, 7)), split(same))
    turned = dot_split((table_slice(tables_ref, 6), table_slice(tables_ref, 8)), split(turned))

    for j in range(EVEN):
        rows = slice(j * SLOTS, (j + 1) * SLOTS)
        steady = same[rows] + (middle if j % 2 == 0 else -middle)
        mirrored = [(2 * ODD - j, steady - turned[rows])] if 0 < j < ODD else []
        for lag, here in [(j, steady + turned[rows])] + mirrored:
            cols = slice(lag * COLS, (lag + 1) * COLS)
            plain_ref[:, cols] = here[:share, :COLS]
            refined_ref[:, cols] = here[:share, COLS:]


def per_device(samples, array_sizes, partner):
    count = samples.shape[0]
    groups = lax.axis_size("tm")
    blocks = lax.axis_size("stn")
    share = count * count // groups
    vmem = pl.BlockSpec(memory_space=pltpu.VMEM)
    params = pltpu.CompilerParams(vmem_limit_bytes=32 * 1024 * 1024)
    rows = samples.reshape(count, LAGS // COLS, COLS).transpose(1, 0, 2).reshape(-1, COLS)

    def to_fast_memory(value):
        return lax.ppermute(value, "tm", [(i, i) for i in range(groups)])

    own = to_fast_memory(rows)

    def with_others(value):
        return [value] + [
            lax.ppermute(value, "tm", [(i, i ^ step) for i in range(groups)])
            for step in range(1, groups)
        ]

    def fast(shape, kind=F32):
        return jax.ShapeDtypeStruct(shape, kind)

    early = groups == 2

    def own_stations(own, tables, twist, live):
        return pl.pallas_call(
            functools.partial(near_kernel, share),
            out_shape=(
                fast((groups, 2, HALF * SLOTS, COLS)), fast((HALF * SLOTS, COLS))
            ),
            in_specs=[vmem] * 4,
            out_specs=(vmem,) * 2,
            compiler_params=params,
        )(jnp.stack(with_others(own)), tables, twist, live)

    def exchanged(number, own, sizes, tables, twist):
        far = lax.ppermute(own, "stn", [(i, i ^ number) for i in range(blocks)])
        fetched = pl.pallas_call(
            functools.partial(fetch_kernel, share, number),
            out_shape=(fast(tables.shape, BF16), fast(twist.shape), fast((SLOTS, COLS))),
            in_specs=[pl.BlockSpec(memory_space=pltpu.HBM)] * 3,
            out_specs=(vmem,) * 3,
            scratch_shapes=[
                pltpu.VMEM(sizes.shape, sizes.dtype), pltpu.SemaphoreType.DMA((3,))
            ],
            compiler_params=params,
        )(*(pltpu.with_memory_space_constraint(v, pltpu.HBM) for v in (sizes, tables, twist)))
        far, fetched = lax.optimization_barrier((far, fetched))
        mine = own_stations(own, *fetched) if early else fetched
        return jnp.stack(with_others(far)), *mine

    near_tables, near_twist, far_tables = tables(count, groups)
    both, *mine = lax.switch(
        partner[0] - 1,
        [functools.partial(exchanged, number) for number in range(1, blocks)],
        own, array_sizes[None], jnp.asarray(near_tables), jnp.asarray(near_twist),
    )
    near, keep = mine if early else own_stations(own, *mine)
    out = fast((share, LAGS))
    return pl.pallas_call(
        far_kernel,
        out_shape=(out, out),
        in_specs=[vmem] * 4,
        out_specs=(vmem, vmem),
        compiler_params=params,
    )(both, near, keep, far_tables)


def solution(mesh):
    placed = (P("stn", "tm"), P(), P())
    return jax.shard_map(
        per_device,
        mesh=mesh,
        in_specs=placed,
        out_specs=(P(("stn", "tm"), None), P(("stn", "tm"), None)),
        check_vma=False,
    )
```
